32 devices in a mesh: loop: 16 (over z, x, core), row: 2 (over y).
Axes of the slice: x: 2, y: 2, z: 4, core: 2. Of those that a mesh axis runs over, the one named last changes fastest.
Arguments:
- features: bfloat16 [4096, 256], P(('loop', 'row')), may hold values from -6 to 6
- weight: bfloat16 [256, 256], replicated, may hold values from -0.375 to 0.375
- bias_vector: float32 [256], replicated, may hold values from -3 to 3
- cotangent: bfloat16 [4096, 256], P(('loop', 'row')), may hold values from -6 to 6
- tile_values: bfloat16 [1024, 128, 128], P(('loop', 'row')), as said below
- tile_rows: int32 [1024], P(('loop', 'row')), may hold values from 0 to 1, as said below
- counts: int32 [512], P(('loop', 'row')), may hold values from 0 to 2, as said below
Outputs:
- output: bfloat16 [4096, 256], P(('loop', 'row'))
- grad_features: bfloat16 [4096, 256], P(('loop', 'row'))
- grad_weight: float32 [256, 256], replicated
- grad_bias: float32 [256], replicated
The draws below stay inside these ranges and needn't reach their ends.
Inputs may be any that keep to these rules, and one draw needn't show every extreme that they name: Within one group the 2 tile_rows are distinct. `counts`: in every device's group j = l (destination and source blocks of the same 2 blocks) all slots are live. `tile_values`: A is symmetric and nonnegative: a live tile for destination block a and source block b exists exactly when one for destination block b and source block a does, and the two are transposes of each other.
All inputs are finite; a program needn't handle non-finite values.
Results may differ from the reference program's by a relative error of at most 0.014.
Values may be sent and summed in bfloat16 or wider, within the bound.
No kernel may reach another device: no remote copies, remote signals or barrier semaphores. Data moves between devices by JAX's collectives and lax.ppermute only.
A program may use at most 128 MiB of HBM per device.

```python
import math
import jax
import jax.numpy as jnp
from jax import lax

HID = 256
TILE = 128
NODES = 4096
N_LOOP = 16
N_ROW = 2
DEVICES = 32


def structure(key):
    block_total = N_LOOP * N_ROW
    group_total = DEVICES * N_LOOP
    popularity = jax.random.randint(jax.random.fold_in(key, 11), (block_total,), 2, 7)
    pair_noise = jax.random.randint(jax.random.fold_in(key, 12), (block_total, block_total), 0, 1024)
    pair_noise = pair_noise + pair_noise.T
    block_ids = jnp.arange(block_total, dtype=jnp.int32)
    same_super = block_ids[:, None] // N_ROW == block_ids[None, :] // N_ROW
    limit_table = jnp.minimum(popularity[:, None] * popularity[None, :], 32)
    present = same_super | (pair_noise % 32 < limit_table)
    group_ids = jnp.arange(group_total, dtype=jnp.int32)
    device_ids = group_ids // N_LOOP
    dest_cands = (device_ids // N_ROW)[:, None] * N_ROW + jnp.arange(N_ROW, dtype=jnp.int32)[None, :]
    source_block = group_ids % N_LOOP * N_ROW + device_ids % N_ROW
    live_cands = present[dest_cands, source_block[:, None]]
    rank_keys = jax.random.randint(jax.random.fold_in(key, 13), (group_total, N_ROW), 0, 4096) * N_ROW + jnp.arange(N_ROW, dtype=jnp.int32)[None, :]
    rank_order = jnp.argsort(jnp.argsort(rank_keys, axis=1), axis=1)
    slot_score = jnp.where(live_cands, 0, N_ROW) + rank_order
    slot_order = jnp.argsort(slot_score, axis=1).astype(jnp.int32)
    live_counts = jnp.sum(live_cands.astype(jnp.int32), axis=1).astype(jnp.int32)
    return (slot_order, live_counts)


def draw_tile_rows(key, part):
    slot_order, live_counts = structure(key)
    return slot_order.reshape(-1)


def draw_counts(key, part):
    slot_order, live_counts = structure(key)
    return live_counts


def draw_tile_values(key, part):
    slot_order, live_counts = structure(key)
    key = jax.random.fold_in(key, 3)
    block_total = N_LOOP * N_ROW
    group_total = DEVICES * N_LOOP
    group_ids = jnp.arange(group_total, dtype=jnp.int32)
    device_ids = group_ids // N_LOOP
    source_block = group_ids % N_LOOP * N_ROW + device_ids % N_ROW
    dest_block = (device_ids // N_ROW)[:, None] * N_ROW + slot_order
    source_grid = jnp.broadcast_to(source_block[:, None], dest_block.shape)
    scale_factor = (DEVICES * TILE / 2.0) ** (-0.5)

    def one_tile(dest_one, source_one):
        lower_block = jnp.minimum(dest_one, source_one)
        upper_block = jnp.maximum(dest_one, source_one)
        pair_key = jax.random.fold_in(key, lower_block * block_total + upper_block)
        base = jax.random.uniform(pair_key, (TILE, TILE), jnp.float32, 0.0, 1.0)
        matrix = base * base * base * 2.6457513
        matrix = jnp.where(dest_one > source_one, matrix.T, matrix)
        matrix = jnp.where(dest_one == source_one, (matrix + matrix.T) * 0.70710678, matrix)
        return (matrix * scale_factor).astype(jnp.bfloat16)

    def one_group(items):
        return jax.vmap(one_tile)(items[0], items[1])
    values = lax.map(one_group, (dest_block, source_grid))
    return values.reshape(group_total * N_ROW, TILE, TILE)


def steps_of(stream_key, dims, cuts, least, largest):
    gain = 1.0
    for axis_at, parts in cuts:
        heights = jax.random.uniform(jax.random.fold_in(jax.random.fold_in(stream_key, 6), axis_at), (parts,), jnp.float32, least / len(cuts), largest / len(cuts))
        gain = gain * jnp.repeat(jnp.exp(heights), dims[axis_at] // parts).reshape((-1,) + (1,) * (len(dims) - 1 - axis_at))
    return gain


def centred(rng, shape, deviation, reach, shards=(), kind=jnp.bfloat16):
    factor_of = steps_of(rng, shape, shards, -0.22, 0.18) if shards else 1.0
    array = jax.random.normal(rng, shape, jnp.float32) * deviation * factor_of
    return jnp.minimum(jnp.maximum(array, -reach), reach).astype(kind)


def setup_inputs(seed: int = 0) -> dict:
    arg_keys = jax.random.split(jax.random.key(seed), 8)
    features = centred(arg_keys[0], (NODES, HID), 1.0, 6.0, ((0, 32),))
    weight = centred(arg_keys[1], (HID, HID), HID ** -0.5, 0.375)
    bias_vector = centred(arg_keys[2], (HID,), 0.5, 3.0, (), jnp.float32)
    cotangent = centred(arg_keys[3], (NODES, HID), 1.0, 6.0, ((0, 32),))
    tile_values = draw_tile_values(jax.random.fold_in(arg_keys[7], 71), 0)
    tile_rows = draw_tile_rows(jax.random.fold_in(arg_keys[7], 71), 0)
    counts = draw_counts(jax.random.fold_in(arg_keys[7], 71), 0)
    return dict(features=features, weight=weight, bias_vector=bias_vector, cotangent=cotangent, tile_values=tile_values, tile_rows=tile_rows, counts=counts)


def expand_groups(tile_block, row_block, count_block):
    groups = count_block.shape[0]
    slots = row_block.shape[0] // groups
    tile_size = tile_block.shape[-1]
    dest_rows = row_block.reshape(groups, slots)
    slot_ids = jnp.arange(slots, dtype=jnp.int32)
    live_slots = slot_ids[None, :] < count_block[:, None]
    onehot = ((dest_rows[:, :, None] == slot_ids[None, None, :]) & live_slots[:, :, None]).astype(jnp.float32)
    matrices = tile_block.reshape(groups, slots, tile_size, tile_size).astype(jnp.float32)
    return jnp.einsum('gsd,gsac->gdac', onehot, matrices, precision=lax.Precision.HIGHEST)

def reference(features, weight, bias_vector, cotangent, tile_values, tile_rows, counts):
    device_tiles = tile_values.reshape(DEVICES, N_LOOP * N_ROW, TILE, TILE)
    device_rows = tile_rows.reshape(DEVICES, N_LOOP * N_ROW)
    device_counts = counts.reshape(DEVICES, N_LOOP)
    device_ids = jnp.arange(DEVICES, dtype=jnp.int32)
    feature_grid = features.astype(jnp.float32).reshape(N_LOOP, N_ROW, TILE, HID)

    def forward_term(items):
        tile_block, row_block, count_block, device = items
        sources = lax.dynamic_index_in_dim(feature_grid, device % N_ROW, 1, keepdims=False)
        expanded = expand_groups(tile_block, row_block, count_block)
        return jnp.einsum('gdac,gch->dah', expanded, sources, precision=lax.Precision.HIGHEST)
    partial_terms = lax.map(forward_term, (device_tiles, device_rows, device_counts, device_ids))
    hidden_sum = partial_terms.reshape(N_LOOP, N_ROW, N_ROW, TILE, HID).sum(axis=1).reshape(NODES, HID)
    hidden = hidden_sum.astype(jnp.bfloat16)
    preact = jnp.dot(hidden, weight, preferred_element_type=jnp.float32) + bias_vector
    sigmoid_z = jax.nn.sigmoid(preact)
    output = (preact * sigmoid_z).astype(jnp.bfloat16)
    grad_z = cotangent.astype(jnp.float32) * sigmoid_z * (1.0 + preact * (1.0 - sigmoid_z))
    grad_z_half = grad_z.astype(jnp.bfloat16)
    norm_factor = 1.0 / math.sqrt(NODES)
    grad_weight = jnp.dot(hidden.T, grad_z_half, preferred_element_type=jnp.float32) * norm_factor
    grad_bias = lax.optimization_barrier(jnp.sum(grad_z, axis=0)) * norm_factor
    grad_hidden = jnp.dot(grad_z_half, weight.T, preferred_element_type=jnp.float32).astype(jnp.bfloat16)
    hidden_grid = grad_hidden.astype(jnp.float32).reshape(N_LOOP, N_ROW, TILE, HID)

    def backward_step(carry, items):
        tile_block, row_block, count_block, device = items
        dest_block = lax.dynamic_index_in_dim(hidden_grid, device // N_ROW, 0, keepdims=False)
        expanded = expand_groups(tile_block, row_block, count_block)
        term = jnp.einsum('gdac,dah->gch', expanded, dest_block, precision=lax.Precision.HIGHEST)
        row_index = device % N_ROW
        current = lax.dynamic_index_in_dim(carry, row_index, 0, keepdims=False)
        return (lax.dynamic_update_index_in_dim(carry, current + term, row_index, 0), None)
    start_sums = jnp.zeros((N_ROW, N_LOOP, TILE, HID), jnp.float32)
    back_sums, unused = lax.scan(backward_step, start_sums, (device_tiles, device_rows, device_counts, device_ids))
    grad_features = jnp.transpose(back_sums, (1, 0, 2, 3)).reshape(NODES, HID).astype(jnp.bfloat16)
    return (output, grad_features, grad_weight, grad_bias)
```

```python
import functools

import jax
import jax.numpy as jnp
from jax import lax
from jax.experimental import pallas as pl
from jax.experimental.pallas import tpu as pltpu
from jax.sharding import PartitionSpec as P

BF16 = jnp.bfloat16
F32 = jnp.float32
VMEM = pl.BlockSpec(memory_space=pltpu.VMEM)
SMEM = pl.BlockSpec(memory_space=pltpu.SMEM)
PARAMS = pltpu.CompilerParams(vmem_limit_bytes=56 * 1024 * 1024)


def gather_stages(n_loop):
    top = [m for m in range(4, n_loop, 4)]
    stages = [top] if top else []
    return stages + [[b] for b in (2, 1) if b < n_loop]


def block_masks(n_loop):
    masks = [0]
    for stage in gather_stages(n_loop):
        masks = masks + [c ^ m for c in stage for m in masks]
    return masks


def xor_permute(x, axis, mask, n):
    return lax.ppermute(x, axis, [(i, i ^ mask) for i in range(n)])


def gather_stage(blocks, stage, n_loop):
    return blocks + [xor_permute(b, "loop", c, n_loop) for c in stage for b in blocks]


def expand_kernel(n_loop, n_row, tile, rows_ref, counts_ref, tiles_ref, out_ref):
    me = lax.axis_index("row")

    def body(j, carry):
        for s in range(n_row):
            slot = j * n_row + s
            place = jnp.bitwise_xor(rows_ref[slot], me)
            live = s < counts_ref[j]
            value = tiles_ref[slot]
            value = jnp.where(live, value, jnp.zeros_like(value))
            out_ref[
                pl.ds(pl.multiple_of(place * tile, tile), tile),
                pl.ds(pl.multiple_of(j * tile, tile), tile),
            ] = value
        return carry

    lax.fori_loop(0, n_loop, body, 0)


def place_blocks(masks, tile, block_refs, out_ref):
    me = lax.axis_index("loop")
    for mask, ref in zip(masks, block_refs):
        j = jnp.bitwise_xor(me, mask)
        out_ref[pl.ds(pl.multiple_of(j * tile, tile), tile), :] = ref[...]


def rows_product(a_ref, x, n_row, tile, own_ref, send_refs):
    step = min(2, n_row)
    for q in range(0, n_row, step):
        product = jnp.dot(
            a_ref[q * tile : (q + step) * tile, :], x, preferred_element_type=F32
        )
        for k in range(step):
            part = product[k * tile : (k + 1) * tile, :]
            if q + k == 0:
                own_ref[...] = part
            else:
                send_refs[q + k - 1][...] = part.astype(BF16)


def forward_kernel(masks, n_row, tile, a_ref, *refs):
    n = len(masks)
    block_refs, own_ref, send_refs, x_ref = refs[:n], refs[n], refs[n + 1 : -1], refs[-1]
    place_blocks(masks, tile, block_refs, x_ref)
    rows_product(a_ref, x_ref[...], n_row, tile, own_ref, send_refs)


def backward_kernel(masks, n_row, tile, a_ref, w_ref, b_ref, *refs):
    n = len(masks)
    h_refs, c_refs = refs[:n], refs[n : 2 * n]
    out_ref, gw_ref, gf_ref = refs[2 * n : 2 * n + 3]
    send_refs = refs[2 * n + 3 : 2 * n + 3 + n_row - 1]
    h_all, c_all, gh_all, out_all = refs[-4:]
    place_blocks(masks, tile, h_refs, h_all)
    place_blocks(masks, tile, c_refs, c_all)
    width = w_ref.shape[0]
    step = min(2, n) * tile

    def body(i, carry):
        grad_w, grad_b = carry
        at = pl.ds(pl.multiple_of(i * step, step), step)
        hidden = h_all[at, :]
        preact = jnp.dot(hidden, w_ref[...], preferred_element_type=F32) + b_ref[...]
        sig = jax.nn.sigmoid(preact)
        out_all[at, :] = (preact * sig).astype(BF16)
        grad_z = c_all[at, :].astype(F32) * sig * (1.0 + preact * (1.0 - sig))
        half = grad_z.astype(BF16)
        grad_b = grad_b + jnp.sum(grad_z, axis=0, keepdims=True)
        grad_w = grad_w + lax.dot_general(
            hidden, half, (((0,), (0,)), ((), ())), preferred_element_type=F32
        )
        gh_all[at, :] = lax.dot_general(
            half, w_ref[...], (((1,), (1,)), ((), ())), preferred_element_type=F32
        ).astype(BF16)
        return grad_w, grad_b

    grad_w, grad_b = lax.fori_loop(
        0,
        n * tile // step,
        body,
        (jnp.zeros((width, width), F32), jnp.zeros((1, width), F32)),
    )
    mine = lax.axis_index("loop")
    out_ref[...] = out_all[pl.ds(pl.multiple_of(mine * tile, tile), tile), :]
    high = grad_b.astype(BF16)
    low = (grad_b - high.astype(F32)).astype(BF16)
    gw_ref[:width, :] = grad_w.astype(BF16)
    row = lax.broadcasted_iota(jnp.int32, (16, width), 0)
    high = jnp.broadcast_to(high.astype(F32), (16, width))
    low = jnp.broadcast_to(low.astype(F32), (16, width))
    gw_ref[width:, :] = jnp.where(row == 0, high, jnp.where(row == 1, low, 0.0)).astype(BF16)
    rows_product(a_ref, gh_all[...], n_row, tile, gf_ref, send_refs)


def call(kernel, outs, scratch=(), specs=None):
    return pl.pallas_call(
        kernel,
        out_shape=outs,
        in_specs=specs,
        out_specs=jax.tree.map(lambda _: VMEM, outs),
        scratch_shapes=scratch,
        compiler_params=PARAMS,
    )


def shards(n_loop, n_row, features, weight, bias_vector, cotangent, tile_values, tile_rows, counts):
    tile, width = features.shape
    masks = block_masks(n_loop)
    stages = gather_stages(n_loop)
    nodes = tile * n_loop * n_row
    shape = jax.ShapeDtypeStruct

    blocks = [features]
    cots = [cotangent]
    for stage in stages:
        blocks = gather_stage(blocks, stage, n_loop)
        blocks, cots = lax.optimization_barrier((blocks, cots))
        cots = gather_stage(cots, stage, n_loop)

    adjacency = call(
        functools.partial(expand_kernel, n_loop, n_row, tile),
        shape((n_row * tile, n_loop * tile), BF16),
        specs=[SMEM, SMEM, VMEM],
    )(tile_rows, counts, tile_values)

    sends = [shape((tile, width), BF16)] * (n_row - 1)
    own, *parts = call(
        functools.partial(forward_kernel, masks, n_row, tile),
        [shape((tile, width), F32)] + sends,
        scratch=[pltpu.VMEM((n_loop * tile, width), BF16)],
        specs=[VMEM] * (1 + n_loop),
    )(adjacency, *blocks)
    for q, part in enumerate(parts):
        own = own + xor_permute(part, "row", q + 1, n_row).astype(F32)
    hidden = own.astype(BF16)

    hiddens = [hidden]
    for stage in stages:
        hiddens = gather_stage(hiddens, stage, n_loop)

    big = pltpu.VMEM((n_loop * tile, width), BF16)
    output, grad_w, own, *parts = call(
        functools.partial(backward_kernel, masks, n_row, tile),
        [shape((tile, width), BF16), shape((width + 16, width), BF16), shape((tile, width), F32)]
        + sends,
        scratch=[big] * 4,
        specs=[VMEM] * (3 + 2 * n_loop),
    )(adjacency, weight, bias_vector.reshape(1, width), *hiddens, *cots)

    for q, part in enumerate(parts):
        own = own + xor_permute(part, "row", q + 1, n_row).astype(F32)
    grad_features = own.astype(BF16)

    norm_factor = 1.0 / nodes**0.5
    bit = 1
    while bit < n_row:
        other = xor_permute(grad_w, "row", bit, n_row)
        total = grad_w.astype(F32) + other.astype(F32)
        bias_total = total[width : width + 1, :] + total[width + 1 : width + 2, :]
        bit *= 2
        if bit < n_row:
            high = bias_total.astype(BF16)
            low = (bias_total - high.astype(F32)).astype(BF16)
            rest = jnp.zeros((14, width), BF16)
            grad_w = jnp.concatenate([total[:width].astype(BF16), high, low, rest], axis=0)
    return (
        output,
        grad_features,
        total[:width] * norm_factor,
        bias_total.reshape(width) * norm_factor,
    )


def solution(mesh):
    in_specs = (
        P(("loop", "row"), None),
        P(),
        P(),
        P(("loop", "row"), None),
        P(("loop", "row"), None, None),
        P(("loop", "row")),
        P(("loop", "row")),
    )
    out_specs = (P(("loop", "row"), None), P(("loop", "row"), None), P(), P())
    return jax.shard_map(
        functools.partial(shards, mesh.shape["loop"], mesh.shape["row"]),
        mesh=mesh,
        in_specs=in_specs,
        out_specs=out_specs,
        check_vma=False,
    )
```

```python
import functools
import math

import jax
import jax.numpy as jnp
from jax import lax
from jax.experimental import pallas as pl
from jax.experimental.pallas import tpu as pltpu
from jax.sharding import Mesh
from jax.sharding import PartitionSpec as P

BF16 = jnp.bfloat16
F32 = jnp.float32
VMEM = pl.BlockSpec(memory_space=pltpu.VMEM)
SMEM = pl.BlockSpec(memory_space=pltpu.SMEM)
MIB = 1024 * 1024


def swap(x, axis):
    return lax.ppermute(x, axis, [(0, 1), (1, 0)])


def gather_far(block, n_far):
    copies = jnp.broadcast_to(block, (n_far,) + block.shape)
    return lax.all_to_all(copies, "far", 0, 0).reshape(n_far * block.shape[0], block.shape[1])


def after(x, *others):
    return lax.optimization_barrier((x,) + others)[0]


def expand_kernel(n_loop, n_row, tile, rows_ref, counts_ref, tiles_ref, out_ref):
    n_far = n_loop // 4
    me = lax.axis_index("row")
    my_near = 2 * lax.axis_index("mid") + lax.axis_index("core")

    def body(j, carry):
        piece = jnp.bitwise_xor(lax.rem(j, 4), my_near)
        column = piece * n_far + lax.div(j, 4)
        for s in range(n_row):
            slot = j * n_row + s
            place = jnp.bitwise_xor(rows_ref[slot], me)
            value = tiles_ref[slot]
            value = jnp.where(s < counts_ref[j], value, jnp.zeros_like(value))
            out_ref[
                pl.ds(pl.multiple_of(place * tile, tile), tile),
                pl.ds(pl.multiple_of(column * tile, tile), tile),
            ] = value
        return carry

    lax.fori_loop(0, n_loop, body, 0)


def columns_product(a_ref, first, pieces, row_slice):
    total = None
    for k, piece in enumerate(pieces):
        depth = piece.shape[0]
        at = (first + k) * depth
        product = jnp.dot(
            a_ref[row_slice, at : at + depth], piece[...], preferred_element_type=F32
        )
        total = product if total is None else total + product
    return total


def forward_half_kernel(tile, n_row, a_ref, p0_ref, p1_ref, out_ref):
    step = min(2, n_row) * tile
    for at in range(0, n_row * tile, step):
        rows = slice(at, at + step)
        out_ref[rows, :] = columns_product(a_ref, 0, (p0_ref, p1_ref), rows)


def split_rows(total_of, tile, n_row, own_ref, send_refs):
    step = min(2, n_row)
    for q in range(0, n_row, step):
        total = total_of(slice(q * tile, (q + step) * tile))
        for k in range(step):
            part = total[k * tile : (k + 1) * tile, :]
            if q + k == 0:
                own_ref[...] = part
            else:
                send_refs[q + k - 1][...] = part.astype(BF16)


def forward_kernel(tile, n_row, a_ref, p2_ref, p3_ref, half_ref, own_ref, *send_refs):
    split_rows(
        lambda rows: half_ref[rows, :] + columns_product(a_ref, 2, (p2_ref, p3_ref), rows),
        tile,
        n_row,
        own_ref,
        send_refs,
    )


def backward_piece(h_ref, c_ref, w_ref, b_ref, gh_ref):
    depth, width = h_ref.shape
    step = min(depth, 256)

    def body(i, carry):
        grad_w, grad_b = carry
        at = pl.ds(pl.multiple_of(i * step, step), step)
        hidden = h_ref[at, :]
        preact = jnp.dot(hidden, w_ref[...], preferred_element_type=F32) + b_ref[...]
        sig = 0.5 * jnp.tanh(0.5 * preact) + 0.5
        grad_z = c_ref[at, :].astype(F32) * sig * (1.0 + preact * (1.0 - sig))
        half = grad_z.astype(BF16)
        grad_b = grad_b + jnp.sum(grad_z.reshape(step // 8, 8, width), axis=0)
        grad_w = grad_w + lax.dot_general(
            hidden, half, (((0,), (0,)), ((), ())), preferred_element_type=F32
        )
        gh_ref[at, :] = lax.dot_general(
            half, w_ref[...], (((1,), (1,)), ((), ())), preferred_element_type=F32
        ).astype(BF16)
        return grad_w, grad_b

    carry = (jnp.zeros((width, width), F32), jnp.zeros((8, width), F32))
    for i in range(depth // step):
        carry = body(i, carry)
    return carry


def backward_half_kernel(
    tile, n_row, a_ref, w_ref, b_ref, h0_ref, h1_ref, c0_ref, c1_ref,
    out_ref, gw_ref, gb_ref, gf_ref, gh0_ref, gh1_ref,
):
    mine = pl.ds(pl.multiple_of(lax.axis_index("far") * tile, tile), tile)
    preact = jnp.dot(h0_ref[mine, :], w_ref[...], preferred_element_type=F32) + b_ref[...]
    out_ref[...] = (preact * (0.5 * jnp.tanh(0.5 * preact) + 0.5)).astype(BF16)
    gw0, gb0 = backward_piece(h0_ref, c0_ref, w_ref, b_ref, gh0_ref)
    gw1, gb1 = backward_piece(h1_ref, c1_ref, w_ref, b_ref, gh1_ref)
    gw_ref[...] = gw0 + gw1
    gb_ref[...] = gb0 + gb1
    step = min(2, n_row) * tile
    for at in range(0, n_row * tile, step):
        rows = slice(at, at + step)
        gf_ref[rows, :] = columns_product(a_ref, 0, (gh0_ref, gh1_ref), rows)


def backward_weight_kernel(
    w_ref, b_ref, h2_ref, h3_ref, c2_ref, c3_ref, gw_ref, gb_ref,
    gh2_ref, gh3_ref, message_ref,
):
    width = w_ref.shape[0]
    gw2, gb2 = backward_piece(h2_ref, c2_ref, w_ref, b_ref, gh2_ref)
    gw3, gb3 = backward_piece(h3_ref, c3_ref, w_ref, b_ref, gh3_ref)
    message_ref[:width, :] = (gw_ref[...] + (gw2 + gw3)).astype(BF16)
    bias = jnp.sum(gb_ref[...] + (gb2 + gb3), axis=0, keepdims=True)
    high = bias.astype(BF16).astype(F32)
    low = bias - high
    row = lax.broadcasted_iota(jnp.int32, (16, width), 0)
    high = jnp.broadcast_to(high, (16, width))
    low = jnp.broadcast_to(low, (16, width))
    message_ref[width:, :] = jnp.where(row == 0, high, jnp.where(row == 1, low, 0.0)).astype(BF16)


def call(kernel, name, outs, operands, scratch=(), specs=None, flops=0):
    size = sum(o.size * o.dtype.itemsize for o in list(operands) + list(outs))
    held = size + sum(math.prod(s.shape) * jnp.dtype(s.dtype).itemsize for s in scratch)
    return pl.pallas_call(
        kernel,
        name=name,
        out_shape=outs,
        in_specs=specs or [VMEM] * len(operands),
        out_specs=[VMEM] * len(outs),
        scratch_shapes=scratch,
        cost_estimate=pl.CostEstimate(flops=flops, bytes_accessed=size, transcendentals=0),
        compiler_params=pltpu.CompilerParams(vmem_limit_bytes=2 * held + 4 * MIB),
    )(*operands)


def shards(n_loop, n_row, features, weight, bias_vector, cotangent, tile_values, tile_rows, counts):
    tile, width = features.shape
    n_far = n_loop // 4
    nodes = tile * n_loop * n_row
    rows, depth = n_row * tile, n_far * tile
    shape = jax.ShapeDtypeStruct
    product = 2 * rows * 2 * depth * width

    f0 = gather_far(features, n_far)
    f2 = swap(f0, "mid")
    f1 = swap(f0, "core")
    c0 = gather_far(after(cotangent, f0), n_far)

    (adjacency,) = call(
        functools.partial(expand_kernel, n_loop, n_row, tile),
        "expand",
        [shape((rows, n_loop * tile), BF16)],
        (tile_rows, counts, tile_values),
        specs=[SMEM, SMEM, VMEM],
    )
    (half,) = call(
        functools.partial(forward_half_kernel, tile, n_row),
        "forward_near",
        [shape((rows, width), F32)],
        (adjacency, f0, f1),
        flops=product,
    )
    f3 = swap(after(f2, c0, half), "core")
    c2 = swap(after(c0, f2), "mid")
    c1 = swap(after(c0, f2), "core")

    sends = [shape((tile, width), BF16)] * (n_row - 1)
    own, *parts = call(
        functools.partial(forward_kernel, tile, n_row),
        "forward_rest",
        [shape((tile, width), F32)] + sends,
        (adjacency, f2, f3, half),
        flops=product,
    )
    for q, part in enumerate(parts):
        own = own + row_swap(part, q + 1, n_row).astype(F32)
    hidden = own.astype(BF16)
    c3 = swap(after(c2, parts[0]), "core")

    h0 = gather_far(hidden, n_far)
    h1 = swap(h0, "core")
    h2 = swap(h0, "mid")

    bias_row = bias_vector.reshape(1, width)
    gh = pltpu.VMEM((depth, width), BF16)
    elements = 2 * 6 * depth * width * width
    output, grad_w, grad_b, half = call(
        functools.partial(backward_half_kernel, tile, n_row),
        "backward_near",
        [
            shape((tile, width), BF16),
            shape((width, width), F32),
            shape((8, width), F32),
            shape((rows, width), F32),
        ],
        (adjacency, weight, bias_row, h0, h1, c0, c1),
        scratch=[gh, gh],
        flops=product + elements,
    )
    h3 = swap(after(h2, half), "core")
    gh2, gh3, message = call(
        backward_weight_kernel,
        "backward_rest",
        [shape((depth, width), BF16)] * 2 + [shape((width + 16, width), BF16)],
        (weight, bias_row, h2, h3, c2, c3, grad_w, grad_b),
        flops=elements,
    )
    own, *parts = call(
        functools.partial(forward_kernel, tile, n_row),
        "features_rest",
        [shape((tile, width), F32)] + sends,
        (adjacency, gh2, gh3, half),
        flops=product,
    )

    norm_factor = 1.0 / nodes**0.5
    bit = 1
    while bit < n_row:
        other = row_swap(message, bit, n_row)
        total = message.astype(F32) + other.astype(F32)
        bias_total = total[width : width + 1, :] + total[width + 1 : width + 2, :]
        bit *= 2
        if bit < n_row:
            high = bias_total.astype(BF16)
            low = (bias_total - high.astype(F32)).astype(BF16)
            rest = jnp.zeros((14, width), BF16)
            message = jnp.concatenate([total[:width].astype(BF16), high, low, rest], axis=0)

    for q, part in enumerate(parts):
        own = own + row_swap(part, q + 1, n_row).astype(F32)
    grad_features = own.astype(BF16)
    return (
        output,
        grad_features,
        total[:width] * norm_factor,
        bias_total.reshape(width) * norm_factor,
    )


def row_swap(x, mask, n_row):
    return lax.ppermute(x, "row", [(i, i ^ mask) for i in range(n_row)])


def solution(mesh):
    n_loop, n_row = mesh.shape["loop"], mesh.shape["row"]
    fine = Mesh(mesh.devices.reshape(n_loop // 4, 2, 2, n_row), ("far", "mid", "core", "row"))
    every = ("far", "mid", "core", "row")
    in_specs = (
        P(every, None),
        P(),
        P(),
        P(every, None),
        P(every, None, None),
        P(every),
        P(every),
    )
    out_specs = (P(every, None), P(every, None), P(), P())
    return jax.shard_map(
        functools.partial(shards, n_loop, n_row),
        mesh=fine,
        in_specs=in_specs,
        out_specs=out_specs,
        check_vma=False,
    )
```

```python
import functools
import math

import jax
import jax.numpy as jnp
from jax import lax
from jax.experimental import pallas as pl
from jax.experimental.pallas import tpu as pltpu
from jax.sharding import Mesh
from jax.sharding import PartitionSpec as P

BF16 = jnp.bfloat16
F32 = jnp.float32
VMEM = pl.BlockSpec(memory_space=pltpu.VMEM)
SMEM = pl.BlockSpec(memory_space=pltpu.SMEM)
MIB = 1024 * 1024
PAD = 16


def partner(x, axis, mask, n):
    return lax.ppermute(x, axis, [(i, i ^ mask) for i in range(n)])


def swap(x, axis):
    return partner(x, axis, 1, 2)


def after(x, *others):
    return lax.optimization_barrier((x,) + others)[0]


def shape(*dims, dtype=BF16):
    return jax.ShapeDtypeStruct(dims, dtype)


def dot(a, b, contract=((1,), (0,))):
    return lax.dot_general(a, b, (contract, ((), ())), preferred_element_type=F32)


def sigmoid(x):
    return 0.5 * jnp.tanh(0.5 * x) + 0.5


def tree_sum(parts):
    while len(parts) > 1:
        parts = [parts[i] + parts[i + 1] for i in range(0, len(parts), 2)]
    return parts[0]


def expand_kernel(n_loop, n_row, tile, rows_ref, counts_ref, tiles_ref, out_ref):
    n_far = n_loop // 4
    my_row, my_far = lax.axis_index("row"), lax.axis_index("far")
    my_near = 2 * lax.axis_index("mid") + lax.axis_index("core")

    def body(j, carry):
        near = jnp.bitwise_xor(lax.rem(j, 4), my_near)
        column = near * n_far + jnp.bitwise_xor(lax.div(j, 4), my_far)
        for s in range(n_row):
            slot = j * n_row + s
            place = jnp.bitwise_xor(rows_ref[slot], my_row)
            value = tiles_ref[slot]
            value = jnp.where(s < counts_ref[j], value, jnp.zeros_like(value))
            out_ref[
                pl.ds(pl.multiple_of(place * tile, tile), tile),
                pl.ds(pl.multiple_of(column * tile, tile), tile),
            ] = value
        return carry

    lax.fori_loop(0, n_loop, body, 0)


def product_rows(a_ref, first, block_refs, rows):
    x = jnp.concatenate([ref[...] for ref in block_refs], axis=0)
    return dot(a_ref[rows, first : first + x.shape[0]], x)


def near_kernel(tile, n_row, a_ref, *refs):
    block_refs, out_ref = refs[:-1], refs[-1]
    step = min(2, n_row) * tile
    for at in range(0, n_row * tile, step):
        rows = slice(at, at + step)
        out_ref[rows, :] = product_rows(a_ref, 0, block_refs, rows)


def rest_kernel(tile, n_row, n_blocks, a_ref, half_ref, *refs):
    block_refs, own_ref, send_refs = refs[:n_blocks], refs[n_blocks], refs[n_blocks + 1 :]
    first = a_ref.shape[1] // 2
    step = min(2, n_row)
    for q in range(0, n_row, step):
        rows = slice(q * tile, (q + step) * tile)
        total = half_ref[rows, :] + product_rows(a_ref, first, block_refs, rows)
        for k in range(step):
            part = total[k * tile : (k + 1) * tile, :]
            if q + k == 0:
                own_ref[...] = part
            else:
                send_refs[q + k - 1][...] = part.astype(BF16)


def sum_kernel(own_ref, *refs):
    part_refs, out_ref = refs[:-1], refs[-1]
    total = own_ref[...]
    for ref in part_refs:
        total = total + ref[...].astype(F32)
    out_ref[...] = total.astype(BF16)


def chunk_grads(w_ref, b_ref, h_refs, c_refs, gh_ref, out_ref=None):
    tile, width = h_refs[0].shape
    weight_sums, bias_sums = [], []
    for k, (h_ref, c_ref) in enumerate(zip(h_refs, c_refs)):
        hidden = h_ref[...]
        preact = dot(hidden, w_ref[...]) + b_ref[...]
        sig = sigmoid(preact)
        if k == 0 and out_ref is not None:
            out_ref[...] = (preact * sig).astype(BF16)
        grad_z = c_ref[...].astype(F32) * sig * (1.0 + preact * (1.0 - sig))
        half = grad_z.astype(BF16)
        gh_ref[k * tile : (k + 1) * tile, :] = dot(half, w_ref[...], ((1,), (1,))).astype(BF16)
        bias_sums.append(jnp.sum(grad_z.reshape(tile // 8, 8, width), axis=0))
        weight_sums.append(dot(hidden, half, ((0,), (0,))))
    return tree_sum(weight_sums), tree_sum(bias_sums)


def first_chunk_kernel(n, w_ref, b_ref, *refs):
    h_refs, c_refs = refs[:n], refs[n : 2 * n]
    gh_ref, out_ref, gw_ref, gb_ref = refs[2 * n :]
    gw_ref[...], gb_ref[...] = chunk_grads(w_ref, b_ref, h_refs, c_refs, gh_ref, out_ref)


def write_message(ref, grad_w, bias):
    rows, width = grad_w.shape
    ref[:rows, :] = grad_w.astype(BF16)
    high = bias.astype(BF16).astype(F32)
    row = lax.broadcasted_iota(jnp.int32, (PAD, width), 0)
    low = jnp.broadcast_to(bias - high, (PAD, width))
    high = jnp.broadcast_to(high, (PAD, width))
    ref[rows:, :] = jnp.where(row == 0, high, jnp.where(row == 1, low, 0.0)).astype(BF16)


def read_message(ref):
    rows = ref.shape[0] - PAD
    tail = ref[rows:, :].astype(F32)
    return ref[:rows, :].astype(F32), tail[0:1, :] + tail[1:2, :]


def last_chunk_kernel(n, w_ref, b_ref, *refs):
    h_refs, c_refs = refs[:n], refs[n : 2 * n]
    gw_ref, gb_ref, gh_ref, keep_ref, send_ref, sum_ref = refs[2 * n :]
    half = keep_ref.shape[0] - PAD
    grad_w, grad_b = chunk_grads(w_ref, b_ref, h_refs, c_refs, gh_ref)
    sum_ref[...] = gw_ref[...] + grad_w
    bias = jnp.sum(gb_ref[...] + grad_b, axis=0, keepdims=True)
    core = lax.axis_index("core")
    kept = sum_ref[pl.ds(pl.multiple_of(core * half, half), half), :]
    sent = sum_ref[pl.ds(pl.multiple_of((1 - core) * half, half), half), :]
    write_message(keep_ref, kept, bias)
    write_message(send_ref, sent, bias)


def message_kernel(own_ref, other_ref, out_ref):
    own_w, own_b = read_message(own_ref)
    other_w, other_b = read_message(other_ref)
    write_message(out_ref, own_w + other_w, own_b + other_b)


def scale_kernel(factor, own_ref, other_ref, half_ref, bias_ref):
    own_w, own_b = read_message(own_ref)
    other_w, other_b = read_message(other_ref)
    half_ref[...] = (own_w + other_w) * factor
    bias_ref[...] = (own_b + other_b) * factor


def halves_kernel(own_ref, other_ref, out_ref):
    half = own_ref.shape[0]
    core = lax.axis_index("core")
    out_ref[pl.ds(pl.multiple_of(core * half, half), half), :] = own_ref[...]
    out_ref[pl.ds(pl.multiple_of((1 - core) * half, half), half), :] = other_ref[...]


def call(kernel, name, outs, operands, scratch=(), specs=None, flops=0):
    size = sum(o.size * o.dtype.itemsize for o in list(operands) + list(outs))
    held = size + sum(math.prod(s.shape) * jnp.dtype(s.dtype).itemsize for s in scratch)
    return pl.pallas_call(
        kernel,
        name=name,
        out_shape=outs,
        in_specs=specs or [VMEM] * len(operands),
        out_specs=[VMEM] * len(outs),
        scratch_shapes=scratch,
        cost_estimate=pl.CostEstimate(flops=flops, bytes_accessed=size, transcendentals=0),
        compiler_params=pltpu.CompilerParams(vmem_limit_bytes=2 * held + 4 * MIB),
    )(*operands)


def shards(n_loop, n_row, features, weight, bias_vector, cotangent, tile_values, tile_rows, counts):
    tile, width = features.shape
    n_far = n_loop // 4
    nodes = tile * n_loop * n_row
    rows = n_row * tile
    flops = rows * n_loop * tile * width

    def far_blocks(block):
        return [block] + [partner(block, "far", m, n_far) for m in range(1, n_far)]

    def product(near, rest, name):
        (half,) = call(
            functools.partial(near_kernel, tile, n_row),
            name + "_near",
            [shape(rows, width, dtype=F32)],
            [adjacency] + near,
            flops=flops,
        )
        own, *parts = call(
            functools.partial(rest_kernel, tile, n_row, len(rest)),
            name + "_rest",
            [shape(tile, width, dtype=F32)] + [shape(tile, width)] * (n_row - 1),
            [adjacency, half] + rest,
            flops=flops,
        )
        others = [partner(part, "row", q + 1, n_row) for q, part in enumerate(parts)]
        (total,) = call(sum_kernel, name + "_sum", [shape(tile, width)], [own] + others)
        return total

    (adjacency,) = call(
        functools.partial(expand_kernel, n_loop, n_row, tile),
        "expand",
        [shape(rows, n_loop * tile)],
        (tile_rows, counts, tile_values),
        specs=[SMEM, SMEM, VMEM],
    )

    f00 = far_blocks(features)
    f10 = [swap(block, "mid") for block in f00]
    f01 = [swap(block, "core") for block in f00]
    f11 = [swap(block, "core") for block in f10]
    cots = far_blocks(after(cotangent, *f00[1:]))
    hidden = product(f00 + f01, f10 + f11, "forward")

    hiddens = far_blocks(hidden)
    bias_row = bias_vector.reshape(1, width)
    n = n_far // 2
    chunk_flops = n * tile * 6 * width * width
    gh_a, output, grad_w, grad_b = call(
        functools.partial(first_chunk_kernel, n),
        "first_chunk",
        [
            shape(n * tile, width),
            shape(tile, width),
            shape(width, width, dtype=F32),
            shape(8, width, dtype=F32),
        ],
        [weight, bias_row] + hiddens[:n] + cots[:n],
        flops=chunk_flops,
    )
    half_rows = width // 2 + PAD
    gh_b, keep, send = call(
        functools.partial(last_chunk_kernel, n),
        "last_chunk",
        [shape(n * tile, width), shape(half_rows, width), shape(half_rows, width)],
        [weight, bias_row] + hiddens[n:] + cots[n:] + [grad_w, grad_b],
        scratch=[pltpu.VMEM((width, width), F32)],
        flops=chunk_flops,
    )
    g00 = [gh_a, gh_b]
    g10 = [swap(chunk, "mid") for chunk in g00]
    g01 = [swap(chunk, "core") for chunk in g00]
    g11 = [swap(chunk, "core") for chunk in g10]
    grad_features = product(g00 + g01, g10 + g11, "backward")

    (message,) = call(
        message_kernel, "sum_core", [shape(half_rows, width)], [keep, swap(send, "core")]
    )
    bit = 1
    while bit < n_row:
        (message,) = call(
            message_kernel,
            "sum_row",
            [shape(half_rows, width)],
            [message, partner(message, "row", bit, n_row)],
        )
        bit *= 2
    half, bias_grad = call(
        functools.partial(scale_kernel, 1.0 / nodes**0.5),
        "sum_mid",
        [shape(width // 2, width, dtype=F32), shape(1, width, dtype=F32)],
        [message, swap(message, "mid")],
    )
    (weight_grad,) = call(
        halves_kernel, "halves", [shape(width, width, dtype=F32)], [half, swap(half, "core")]
    )
    return output, grad_features, weight_grad, bias_grad.reshape(width)


def solution(mesh):
    n_loop, n_row = mesh.shape["loop"], mesh.shape["row"]
    every = ("far", "mid", "core", "row")
    fine = Mesh(mesh.devices.reshape(n_loop // 4, 2, 2, n_row), every)
    in_specs = (
        P(every, None),
        P(),
        P(),
        P(every, None),
        P(every, None, None),
        P(every),
        P(every),
    )
    out_specs = (P(every, None), P(every, None), P(), P())
    return jax.shard_map(
        functools.partial(shards, n_loop, n_row),
        mesh=fine,
        in_specs=in_specs,
        out_specs=out_specs,
        check_vma=False,
    )
```

```python
import functools
import math

import jax
import jax.numpy as jnp
from jax import lax
from jax.experimental import pallas as pl
from jax.experimental.pallas import tpu as pltpu
from jax.sharding import Mesh
from jax.sharding import PartitionSpec as P

BF16 = jnp.bfloat16
F32 = jnp.float32
VMEM = pl.BlockSpec(memory_space=pltpu.VMEM)
SMEM = pl.BlockSpec(memory_space=pltpu.SMEM)
MIB = 1024 * 1024
PAD = 16


def partner(x, axis, mask, n):
    return lax.ppermute(x, axis, [(i, i ^ mask) for i in range(n)])


def swap(x, axis):
    return partner(x, axis, 1, 2)


def after(x, *others):
    return lax.optimization_barrier((x,) + others)[0]


def shape(*dims, dtype=BF16):
    return jax.ShapeDtypeStruct(dims, dtype)


def dot(a, b, contract=((1,), (0,))):
    return lax.dot_general(a, b, (contract, ((), ())), preferred_element_type=F32)


def sigmoid(x):
    return 0.5 * jnp.tanh(0.5 * x) + 0.5


def tree_sum(parts):
    while len(parts) > 1:
        parts = [parts[i] + parts[i + 1] for i in range(0, len(parts), 2)]
    return parts[0]


def far_masks(n_far):
    return [1 << k for k in reversed(range(n_far.bit_length() - 1))]


def far_place(mask, n_far):
    place = 0
    for k, step in enumerate(far_masks(n_far)):
        place = place + jnp.where(jnp.bitwise_and(mask, step) > 0, 1 << k, 0)
    return place


def expand_kernel(n_loop, n_row, tile, rows_ref, counts_ref, tiles_ref, out_ref):
    n_far = n_loop // 4
    my_row, my_far = lax.axis_index("row"), lax.axis_index("far")
    my_near = 2 * lax.axis_index("mid") + lax.axis_index("core")

    def body(j, carry):
        near = jnp.bitwise_xor(lax.rem(j, 4), my_near)
        column = near * n_far + far_place(jnp.bitwise_xor(lax.div(j, 4), my_far), n_far)
        for s in range(n_row):
            slot = j * n_row + s
            place = jnp.bitwise_xor(rows_ref[slot], my_row)
            value = tiles_ref[slot]
            value = jnp.where(s < counts_ref[j], value, jnp.zeros_like(value))
            out_ref[
                pl.ds(pl.multiple_of(place * tile, tile), tile),
                pl.ds(pl.multiple_of(column * tile, tile), tile),
            ] = value
        return carry

    lax.fori_loop(0, n_loop, body, 0)


def product_rows(a_ref, first, block_refs, rows):
    x = jnp.concatenate([ref[...] for ref in block_refs], axis=0)
    return dot(a_ref[rows, first : first + x.shape[0]], x)


def pack_kernel(*refs):
    at = 0
    for ref in refs[:-1]:
        refs[-1][at : at + ref.shape[0], :] = ref[...]
        at += ref.shape[0]


def near_kernel(tile, n_row, a_ref, *refs):
    block_refs, out_ref = refs[:-1], refs[-1]
    step = min(2, n_row) * tile
    for at in range(0, n_row * tile, step):
        rows = slice(at, at + step)
        out_ref[rows, :] = product_rows(a_ref, 0, block_refs, rows)


def rest_kernel(tile, n_row, n_blocks, a_ref, half_ref, *refs):
    block_refs, own_ref, send_refs = refs[:n_blocks], refs[n_blocks], refs[n_blocks + 1 :]
    first = a_ref.shape[1] // 2
    step = min(2, n_row)
    for q in range(0, n_row, step):
        rows = slice(q * tile, (q + step) * tile)
        total = half_ref[rows, :] + product_rows(a_ref, first, block_refs, rows)
        for k in range(step):
            part = total[k * tile : (k + 1) * tile, :]
            if q + k == 0:
                own_ref[...] = part
            else:
                send_refs[q + k - 1][...] = part.astype(BF16)


def sum_kernel(own_ref, *refs):
    part_refs, out_ref = refs[:-1], refs[-1]
    total = own_ref[...]
    for ref in part_refs:
        total = total + ref[...].astype(F32)
    out_ref[...] = total.astype(BF16)


def chunk_grads(w_ref, b_ref, h_ref, c_ref, gh_ref, out_ref=None):
    tile, width = h_ref.shape[0] // 2, h_ref.shape[1]
    weight_sums, bias_sums = [], []
    for k in range(2):
        rows = slice(k * tile, (k + 1) * tile)
        hidden = h_ref[rows, :]
        preact = dot(hidden, w_ref[...]) + b_ref[...]
        sig = sigmoid(preact)
        if k == 0 and out_ref is not None:
            out_ref[...] = (preact * sig).astype(BF16)
        grad_z = c_ref[rows, :].astype(F32) * sig * (1.0 + preact * (1.0 - sig))
        half = grad_z.astype(BF16)
        gh_ref[rows, :] = dot(half, w_ref[...], ((1,), (1,))).astype(BF16)
        bias_sums.append(jnp.sum(grad_z.reshape(tile // 8, 8, width), axis=0))
        weight_sums.append(dot(hidden, half, ((0,), (0,))))
    return tree_sum(weight_sums), tree_sum(bias_sums)


def chunk_kernel(w_ref, b_ref, h_ref, c_ref, gh_ref, gw_ref, gb_ref, *out_refs):
    gw_ref[...], gb_ref[...] = chunk_grads(w_ref, b_ref, h_ref, c_ref, gh_ref, *out_refs)


def write_message(ref, grad_w, bias):
    rows, width = grad_w.shape
    ref[:rows, :] = grad_w.astype(BF16)
    high = bias.astype(BF16).astype(F32)
    row = lax.broadcasted_iota(jnp.int32, (PAD, width), 0)
    low = jnp.broadcast_to(bias - high, (PAD, width))
    high = jnp.broadcast_to(high, (PAD, width))
    ref[rows:, :] = jnp.where(row == 0, high, jnp.where(row == 1, low, 0.0)).astype(BF16)


def read_message(ref):
    rows = ref.shape[0] - PAD
    tail = ref[rows:, :].astype(F32)
    return ref[:rows, :].astype(F32), tail[0:1, :] + tail[1:2, :]


def last_chunk_kernel(n, w_ref, b_ref, h_ref, c_ref, *refs):
    gw_refs, gb_refs = refs[:n], refs[n : 2 * n]
    gh_ref, keep_ref, send_ref, sum_ref = refs[2 * n :]
    half = keep_ref.shape[0] - PAD
    grad_w, grad_b = chunk_grads(w_ref, b_ref, h_ref, c_ref, gh_ref)
    sum_ref[...] = tree_sum([ref[...] for ref in gw_refs] + [grad_w])
    grad_b = tree_sum([ref[...] for ref in gb_refs] + [grad_b])
    bias = jnp.sum(grad_b, axis=0, keepdims=True)
    core = lax.axis_index("core")
    kept = sum_ref[pl.ds(pl.multiple_of(core * half, half), half), :]
    sent = sum_ref[pl.ds(pl.multiple_of((1 - core) * half, half), half), :]
    write_message(keep_ref, kept, bias)
    write_message(send_ref, sent, bias)


def message_kernel(own_ref, other_ref, out_ref):
    own_w, own_b = read_message(own_ref)
    other_w, other_b = read_message(other_ref)
    write_message(out_ref, own_w + other_w, own_b + other_b)


def last_kernel(n_parts, factor, own_ref, *refs):
    part_refs = refs[:n_parts]
    m00_ref, m10_ref, m01_ref, m11_ref, features_ref, weight_ref, bias_ref = refs[n_parts:]
    sum_kernel(own_ref, *part_refs, features_ref)
    half = weight_ref.shape[0] // 2
    core = lax.axis_index("core")
    for k, (near_ref, far_ref) in enumerate(((m00_ref, m10_ref), (m01_ref, m11_ref))):
        near_w, near_b = read_message(near_ref)
        far_w, far_b = read_message(far_ref)
        at = jnp.bitwise_xor(core, k) * half
        weight_ref[pl.ds(pl.multiple_of(at, half), half), :] = (near_w + far_w) * factor
        if k == 0:
            bias_ref[...] = (near_b + far_b) * factor


def call(kernel, name, outs, operands, scratch=(), specs=None, flops=0):
    size = sum(o.size * o.dtype.itemsize for o in list(operands) + list(outs))
    held = size + sum(math.prod(s.shape) * jnp.dtype(s.dtype).itemsize for s in scratch)
    return pl.pallas_call(
        kernel,
        name=name,
        out_shape=outs,
        in_specs=specs or [VMEM] * len(operands),
        out_specs=[VMEM] * len(outs),
        scratch_shapes=scratch,
        cost_estimate=pl.CostEstimate(flops=flops, bytes_accessed=size, transcendentals=0),
        compiler_params=pltpu.CompilerParams(vmem_limit_bytes=2 * held + 4 * MIB),
    )(*operands)


def shards(n_loop, n_row, features, weight, bias_vector, cotangent, tile_values, tile_rows, counts):
    tile, width = features.shape
    n_far = n_loop // 4
    nodes = tile * n_loop * n_row
    rows = n_row * tile
    flops = rows * n_loop * tile * width

    steps = far_masks(n_far)

    def far_pair(block):
        blocks = [block, partner(block, "far", steps[0], n_far)]
        return call(pack_kernel, "pack", [shape(2 * tile, width)], blocks)[0]

    def far_chunks(pair):
        chunks = [pair]
        for step in steps[1:]:
            chunks = chunks + [partner(chunk, "far", step, n_far) for chunk in chunks]
        return chunks

    def near_product(near, name):
        return call(
            functools.partial(near_kernel, tile, n_row),
            name + "_near",
            [shape(rows, width, dtype=F32)],
            [adjacency] + near,
            flops=flops,
        )[0]

    def rest_product(half, rest, name):
        return call(
            functools.partial(rest_kernel, tile, n_row, len(rest)),
            name + "_rest",
            [shape(tile, width, dtype=F32)] + [shape(tile, width)] * (n_row - 1),
            [adjacency, half] + rest,
            flops=flops,
        )

    def from_row(parts):
        return [partner(part, "row", q + 1, n_row) for q, part in enumerate(parts)]

    pair = far_pair(features)
    (adjacency,) = call(
        functools.partial(expand_kernel, n_loop, n_row, tile),
        "expand",
        [shape(rows, n_loop * tile)],
        (after(tile_rows, pair), counts, tile_values),
        specs=[SMEM, SMEM, VMEM],
    )
    f00 = far_chunks(pair)
    cot_pair = far_pair(after(cotangent, adjacency))
    f00 = f00[:1] + [after(chunk, adjacency) for chunk in f00[1:]]
    f10 = [swap(chunk, "mid") for chunk in f00]
    f01 = [swap(chunk, "core") for chunk in f00]
    f11 = [swap(chunk, "core") for chunk in f10]
    half = near_product(f00 + f01, "forward")
    cots = far_chunks(after(cot_pair, half))
    own, *parts = rest_product(half, f10 + f11, "forward")
    (hidden,) = call(
        sum_kernel, "hidden", [shape(tile, width)], [after(own, *cots)] + from_row(parts)
    )

    hiddens = far_chunks(far_pair(hidden))
    bias_row = bias_vector.reshape(1, width)
    chunk_flops = 2 * tile * 6 * width * width
    g00, weight_sums, bias_sums = [], [], []
    sums = [shape(width, width, dtype=F32), shape(8, width, dtype=F32)]
    for k, (chunk, cot) in enumerate(zip(hiddens[:-1], cots[:-1])):
        outs = [shape(2 * tile, width)] + sums + [shape(tile, width)] * (k == 0)
        gh, weight_sum, bias_sum, *rest = call(
            chunk_kernel, "chunk", outs, [weight, bias_row, chunk, cot], flops=chunk_flops
        )
        g00.append(gh)
        weight_sums.append(weight_sum)
        bias_sums.append(bias_sum)
        output = output if k else rest[0]
    half_rows = width // 2 + PAD
    gh, keep, send = call(
        functools.partial(last_chunk_kernel, len(g00)),
        "last_chunk",
        [shape(2 * tile, width), shape(half_rows, width), shape(half_rows, width)],
        [weight, bias_row, hiddens[-1], cots[-1]] + weight_sums + bias_sums,
        scratch=[pltpu.VMEM((width, width), F32)],
        flops=chunk_flops,
    )
    g00.append(gh)
    g10 = [swap(chunk, "mid") for chunk in g00]
    g01 = [swap(chunk, "core") for chunk in g00]
    g11 = [swap(chunk, "core") for chunk in g10]
    half = near_product(g00 + g01, "backward")
    own, *parts = rest_product(half, g10 + g11, "backward")

    (message,) = call(
        message_kernel, "sum_core", [shape(half_rows, width)], [keep, swap(send, "core")]
    )
    bit = 1
    while bit < n_row:
        (message,) = call(
            message_kernel,
            "sum_row",
            [shape(half_rows, width)],
            [after(message, own), partner(message, "row", bit, n_row)],
        )
        bit *= 2
    messages = [
        message,
        swap(message, "mid"),
        swap(message, "core"),
        lax.ppermute(message, ("mid", "core"), [(i, 3 - i) for i in range(4)]),
    ]
    others = from_row(parts)
    grad_features, weight_grad, bias_grad = call(
        functools.partial(last_kernel, len(others), 1.0 / nodes**0.5),
        "last",
        [shape(tile, width), shape(width, width, dtype=F32), shape(1, width, dtype=F32)],
        [own] + others + messages,
    )
    return output, grad_features, weight_grad, bias_grad.reshape(width)


def solution(mesh):
    n_loop, n_row = mesh.shape["loop"], mesh.shape["row"]
    every = ("far", "mid", "core", "row")
    fine = Mesh(mesh.devices.reshape(n_loop // 4, 2, 2, n_row), every)
    in_specs = (
        P(every, None),
        P(),
        P(),
        P(every, None),
        P(every, None, None),
        P(every),
        P(every),
    )
    out_specs = (P(every, None), P(every, None), P(), P())
    return jax.shard_map(
        functools.partial(shards, n_loop, n_row),
        mesh=fine,
        in_specs=in_specs,
        out_specs=out_specs,
        check_vma=False,
    )
```

```python
import functools
import math

import jax
import jax.numpy as jnp
from jax import lax
from jax.experimental import pallas as pl
from jax.experimental.pallas import tpu as pltpu
from jax.sharding import Mesh
from jax.sharding import PartitionSpec as P

BF16 = jnp.bfloat16
F32 = jnp.float32
VMEM = pl.BlockSpec(memory_space=pltpu.VMEM)
SMEM = pl.BlockSpec(memory_space=pltpu.SMEM)
MIB = 1024 * 1024
PAD = 16


def partner(x, axis, mask, n):
    return lax.ppermute(x, axis, [(i, i ^ mask) for i in range(n)])


def swap(x, axis):
    return partner(x, axis, 1, 2)


def after(x, *others):
    return lax.optimization_barrier((x,) + others)[0]


def shape(*dims, dtype=BF16):
    return jax.ShapeDtypeStruct(dims, dtype)


def dot(a, b, contract=((1,), (0,))):
    return lax.dot_general(a, b, (contract, ((), ())), preferred_element_type=F32)


def sigmoid(x):
    return 0.5 * jnp.tanh(0.5 * x) + 0.5


def tree_sum(parts):
    while len(parts) > 1:
        parts = [parts[i] + parts[i + 1] for i in range(0, len(parts), 2)]
    return parts[0]


def far_masks(n_far):
    return [1 << k for k in reversed(range(n_far.bit_length() - 1))]


def far_place(mask, n_far):
    place = 0
    for k, step in enumerate(far_masks(n_far)):
        place = place + jnp.where(jnp.bitwise_and(mask, step) > 0, 1 << k, 0)
    return place


def expand_kernel(
    n_loop, n_row, tile, rows_ref, counts_ref, tiles_ref, f_ref, c_ref, out_ref, f_out, c_out
):
    n_far = n_loop // 4
    my_row, my_far = lax.axis_index("row"), lax.axis_index("far")
    my_near = 2 * lax.axis_index("mid") + lax.axis_index("core")

    def body(j, carry):
        near = jnp.bitwise_xor(lax.rem(j, 4), my_near)
        column = near * n_far + far_place(jnp.bitwise_xor(lax.div(j, 4), my_far), n_far)
        for s in range(n_row):
            slot = j * n_row + s
            place = jnp.bitwise_xor(rows_ref[slot], my_row)
            value = tiles_ref[slot]
            value = jnp.where(s < counts_ref[j], value, jnp.zeros_like(value))
            out_ref[
                pl.ds(pl.multiple_of(place * tile, tile), tile),
                pl.ds(pl.multiple_of(column * tile, tile), tile),
            ] = value
        return carry

    lax.fori_loop(0, n_loop, body, 0)
    f_out[...] = f_ref[...]
    c_out[...] = c_ref[...]


def product_rows(a_ref, first, block_refs, rows):
    step = a_ref.shape[1] // (2 * len(block_refs))
    x = jnp.concatenate([ref[:step, :] for ref in block_refs], axis=0)
    return dot(a_ref[rows, first : first + x.shape[0]], x)


def pack_kernel(*refs):
    at = 0
    for ref in refs[:-1]:
        refs[-1][at : at + ref.shape[0], :] = ref[...]
        at += ref.shape[0]


def near_kernel(tile, n_row, a_ref, *refs):
    block_refs, out_ref = refs[:-1], refs[-1]
    step = min(2, n_row) * tile
    for at in range(0, n_row * tile, step):
        rows = slice(at, at + step)
        out_ref[rows, :] = product_rows(a_ref, 0, block_refs, rows)


def output_near_kernel(tile, n_row, w_ref, b_ref, h_ref, a_ref, *refs):
    preact = dot(h_ref[...], w_ref[...]) + b_ref[...]
    refs[-2][...] = (preact * sigmoid(preact)).astype(BF16)
    near_kernel(tile, n_row, a_ref, *refs[:-2], refs[-1])


def rest_kernel(tile, n_row, n_blocks, a_ref, half_ref, *refs):
    block_refs, own_ref, send_refs = refs[:n_blocks], refs[n_blocks], refs[n_blocks + 1 :]
    first = a_ref.shape[1] // 2
    step = min(2, n_row)
    for q in range(0, n_row, step):
        rows = slice(q * tile, (q + step) * tile)
        total = half_ref[rows, :] + product_rows(a_ref, first, block_refs, rows)
        for k in range(step):
            part = total[k * tile : (k + 1) * tile, :]
            if q + k == 0:
                own_ref[...] = part
            else:
                send_refs[q + k - 1][...] = part.astype(BF16)


def sum_kernel(own_ref, *refs):
    part_refs, out_ref = refs[:-1], refs[-1]
    total = own_ref[...]
    for ref in part_refs:
        total = total + ref[...].astype(F32)
    out_ref[...] = total.astype(BF16)


def chunk_grads(w_ref, b_ref, h_ref, c_ref, gh_ref):
    tile, width = h_ref.shape[0] // 2, h_ref.shape[1]
    weight_sums, bias_sums = [], []
    for k in range(2):
        rows = slice(k * tile, (k + 1) * tile)
        hidden = h_ref[rows, :]
        preact = dot(hidden, w_ref[...]) + b_ref[...]
        sig = sigmoid(preact)
        grad_z = c_ref[rows, :].astype(F32) * sig * (1.0 + preact * (1.0 - sig))
        half = grad_z.astype(BF16)
        gh_ref[rows, :] = dot(half, w_ref[...], ((1,), (1,))).astype(BF16)
        bias_sums.append(jnp.sum(grad_z.reshape(tile // 8, 8, width), axis=0))
        weight_sums.append(dot(hidden, half, ((0,), (0,))))
    return tree_sum(weight_sums), tree_sum(bias_sums)


def chunk_kernel(w_ref, b_ref, h_ref, c_ref, gh_ref, gw_ref, gb_ref):
    gw_ref[...], gb_ref[...] = chunk_grads(w_ref, b_ref, h_ref, c_ref, gh_ref)


def write_message(ref, grad_w, bias):
    rows, width = grad_w.shape
    ref[:rows, :] = grad_w.astype(BF16)
    high = bias.astype(BF16).astype(F32)
    row = lax.broadcasted_iota(jnp.int32, (PAD, width), 0)
    low = jnp.broadcast_to(bias - high, (PAD, width))
    high = jnp.broadcast_to(high, (PAD, width))
    ref[rows:, :] = jnp.where(row == 0, high, jnp.where(row == 1, low, 0.0)).astype(BF16)


def read_message(ref):
    rows = ref.shape[0] - PAD
    tail = ref[rows:, :].astype(F32)
    return ref[:rows, :].astype(F32), tail[0:1, :] + tail[1:2, :]


def last_chunk_kernel(n, w_ref, b_ref, h_ref, c_ref, *refs):
    gw_refs, gb_refs = refs[:n], refs[n : 2 * n]
    gh_ref, both_ref, keep_ref, sum_ref = refs[2 * n :]
    half = keep_ref.shape[0] - PAD
    grad_w, grad_b = chunk_grads(w_ref, b_ref, h_ref, c_ref, gh_ref)
    sum_ref[...] = tree_sum([ref[...] for ref in gw_refs] + [grad_w])
    grad_b = tree_sum([ref[...] for ref in gb_refs] + [grad_b])
    bias = jnp.sum(grad_b, axis=0, keepdims=True)
    core = lax.axis_index("core")
    kept = sum_ref[pl.ds(pl.multiple_of(core * half, half), half), :]
    sent = sum_ref[pl.ds(pl.multiple_of((1 - core) * half, half), half), :]
    write_message(keep_ref, kept, bias)
    at = gh_ref.shape[0]
    both_ref[:at, :] = gh_ref[...]
    write_message(both_ref.at[at:, :], sent, bias)


def message_kernel(own_ref, other_ref, out_ref):
    own_w, own_b = read_message(own_ref)
    other_w, other_b = read_message(other_ref.at[other_ref.shape[0] - own_ref.shape[0] :, :])
    write_message(out_ref, own_w + other_w, own_b + other_b)


def last_kernel(factor, m00_ref, m10_ref, m01_ref, m11_ref, weight_ref, bias_ref):
    half = weight_ref.shape[0] // 2
    core = lax.axis_index("core")
    for k, (near_ref, far_ref) in enumerate(((m00_ref, m10_ref), (m01_ref, m11_ref))):
        near_w, near_b = read_message(near_ref)
        far_w, far_b = read_message(far_ref)
        at = jnp.bitwise_xor(core, k) * half
        weight_ref[pl.ds(pl.multiple_of(at, half), half), :] = (near_w + far_w) * factor
        if k == 0:
            bias_ref[...] = (near_b + far_b) * factor


def call(kernel, name, outs, operands, scratch=(), specs=None, flops=0):
    size = sum(o.size * o.dtype.itemsize for o in list(operands) + list(outs))
    held = size + sum(math.prod(s.shape) * jnp.dtype(s.dtype).itemsize for s in scratch)
    return pl.pallas_call(
        kernel,
        name=name,
        out_shape=outs,
        in_specs=specs or [VMEM] * len(operands),
        out_specs=[VMEM] * len(outs),
        scratch_shapes=scratch,
        cost_estimate=pl.CostEstimate(flops=flops, bytes_accessed=size, transcendentals=0),
        compiler_params=pltpu.CompilerParams(vmem_limit_bytes=2 * held + 4 * MIB),
    )(*operands)


def shards(n_loop, n_row, features, weight, bias_vector, cotangent, tile_values, tile_rows, counts):
    tile, width = features.shape
    n_far = n_loop // 4
    nodes = tile * n_loop * n_row
    rows = n_row * tile
    flops = rows * n_loop * tile * width

    steps = far_masks(n_far)

    def pack(*blocks):
        return call(pack_kernel, "pack", [shape(2 * tile, width)], blocks)[0]

    def far_partner(block):
        return partner(block, "far", steps[0], n_far)

    def far_chunks(pair):
        chunks = [pair]
        for step in steps[1:]:
            chunks = chunks + [partner(chunk, "far", step, n_far) for chunk in chunks]
        return chunks

    def near_product(near, name):
        return call(
            functools.partial(near_kernel, tile, n_row),
            name + "_near",
            [shape(rows, width, dtype=F32)],
            [adjacency] + near,
            flops=flops,
        )[0]

    def rest_product(half, rest, name):
        return call(
            functools.partial(rest_kernel, tile, n_row, len(rest)),
            name + "_rest",
            [shape(tile, width, dtype=F32)] + [shape(tile, width)] * (n_row - 1),
            [adjacency, half] + rest,
            flops=flops,
        )

    def from_row(parts):
        return [partner(part, "row", q + 1, n_row) for q, part in enumerate(parts)]

    other = far_partner(features)
    adjacency, features, cotangent = call(
        functools.partial(expand_kernel, n_loop, n_row, tile),
        "expand",
        [shape(rows, n_loop * tile), shape(tile, width), shape(tile, width)],
        (tile_rows, counts, tile_values, features, cotangent),
        specs=[SMEM, SMEM] + [VMEM] * 3,
    )
    f00 = far_chunks(pack(features, other))
    f10 = [swap(chunk, "mid") for chunk in f00]
    other_cot = far_partner(after(cotangent, f00[-1]))
    f01 = [swap(chunk, "core") for chunk in f00]
    f11 = [swap(chunk, "core") for chunk in f10]
    half = near_product(f00 + f01, "forward")
    own, *parts = rest_product(half, f10 + f11, "forward")
    others = from_row(parts)
    cots = far_chunks(pack(after(cotangent, own), other_cot))
    (hidden,) = call(sum_kernel, "hidden", [shape(tile, width)], [after(own, other_cot)] + others)

    hiddens = far_chunks(pack(hidden, far_partner(hidden)))
    bias_row = bias_vector.reshape(1, width)
    chunk_flops = 2 * tile * 6 * width * width
    g00, weight_sums, bias_sums = [], [], []
    sums = [shape(width, width, dtype=F32), shape(8, width, dtype=F32)]
    for chunk, cot in zip(hiddens[:-1], cots[:-1]):
        gh, weight_sum, bias_sum = call(
            chunk_kernel,
            "chunk",
            [shape(2 * tile, width)] + sums,
            [weight, bias_row, chunk, after(cot, cots[-1])],
            flops=chunk_flops,
        )
        g00.append(gh)
        weight_sums.append(weight_sum)
        bias_sums.append(bias_sum)
    half_rows = width // 2 + PAD
    g01 = [swap(chunk, "core") for chunk in g00]
    g10 = [swap(chunk, "mid") for chunk in g00]
    gh, both, keep = call(
        functools.partial(last_chunk_kernel, len(g00)),
        "last_chunk",
        [shape(2 * tile, width), shape(2 * tile + half_rows, width), shape(half_rows, width)],
        [weight, bias_row, after(hiddens[-1], *g10), cots[-1]] + weight_sums + bias_sums,
        scratch=[pltpu.VMEM((width, width), F32)],
        flops=chunk_flops,
    )
    g00.append(gh)
    g01.append(swap(both, "core"))
    g10.append(swap(gh, "mid"))

    (message,) = call(message_kernel, "sum_core", [shape(half_rows, width)], [keep, g01[-1]])
    bit = 1
    while bit < n_row:
        (message,) = call(
            message_kernel,
            "sum_row",
            [shape(half_rows, width)],
            [message, partner(message, "row", bit, n_row)],
        )
        bit *= 2
    g11 = [swap(chunk, "core") for chunk in g10[:-1] + [after(g10[-1], message)]]
    output, half = call(
        functools.partial(output_near_kernel, tile, n_row),
        "backward_near",
        [shape(tile, width), shape(rows, width, dtype=F32)],
        [weight, bias_row, hidden, adjacency] + g00 + g01,
        flops=flops,
    )
    own, *parts = rest_product(half, g10 + g11, "backward")
    others = from_row(parts)
    (grad_features,) = call(sum_kernel, "features_sum", [shape(tile, width)], [own] + others)
    message = after(message, own)
    messages = [
        message,
        swap(message, "mid"),
        swap(message, "core"),
        lax.ppermute(message, ("mid", "core"), [(i, 3 - i) for i in range(4)]),
    ]
    weight_grad, bias_grad = call(
        functools.partial(last_kernel, 1.0 / nodes**0.5),
        "last",
        [shape(width, width, dtype=F32), shape(1, width, dtype=F32)],
        messages,
    )
    return output, grad_features, weight_grad, bias_grad.reshape(width)


def solution(mesh):
    n_loop, n_row = mesh.shape["loop"], mesh.shape["row"]
    every = ("far", "mid", "core", "row")
    fine = Mesh(mesh.devices.reshape(n_loop // 4, 2, 2, n_row), every)
    in_specs = (
        P(every, None),
        P(),
        P(),
        P(every, None),
        P(every, None, None),
        P(every),
        P(every),
    )
    out_specs = (P(every, None), P(every, None), P(), P())
    return jax.shard_map(
        functools.partial(shards, n_loop, n_row),
        mesh=fine,
        in_specs=in_specs,
        out_specs=out_specs,
        check_vma=False,
    )
```

```python
import functools
import math

import jax
import jax.numpy as jnp
from jax import lax
from jax.experimental import pallas as pl
from jax.experimental.pallas import tpu as pltpu
from jax.sharding import Mesh
from jax.sharding import PartitionSpec as P

BF16 = jnp.bfloat16
F32 = jnp.float32
VMEM = pl.BlockSpec(memory_space=pltpu.VMEM)
SMEM = pl.BlockSpec(memory_space=pltpu.SMEM)
MIB = 1024 * 1024
PAD = 16


def partner(x, axis, mask, n):
    return lax.ppermute(x, axis, [(i, i ^ mask) for i in range(n)])


def swap(x, axis):
    return partner(x, axis, 1, 2)


def after(x, *others):
    return lax.optimization_barrier((x,) + others)[0]


def shape(*dims, dtype=BF16):
    return jax.ShapeDtypeStruct(dims, dtype)


def dot(a, b, contract=((1,), (0,))):
    return lax.dot_general(a, b, (contract, ((), ())), preferred_element_type=F32)


def sigmoid(x):
    return 0.5 * jnp.tanh(0.5 * x) + 0.5


def tree_sum(parts):
    while len(parts) > 1:
        parts = [parts[i] + parts[i + 1] for i in range(0, len(parts), 2)]
    return parts[0]


def far_masks(n_far):
    return [1 << k for k in reversed(range(n_far.bit_length() - 1))]


def far_place(mask, n_far):
    place = 0
    for k, step in enumerate(far_masks(n_far)):
        place = place + jnp.where(jnp.bitwise_and(mask, step) > 0, 1 << k, 0)
    return place


def expand_kernel(
    n_loop, n_row, tile, rows_hbm, counts_hbm, tiles_hbm, f_hbm, c_hbm, out_ref, f_out, c_out,
    rows_ref, counts_ref, tiles_ref, sems,
):
    copies = [
        pltpu.make_async_copy(source, target, sems.at[k])
        for k, (source, target) in enumerate(
            (
                (rows_hbm, rows_ref),
                (counts_hbm, counts_ref),
                (tiles_hbm, tiles_ref),
                (f_hbm, f_out),
                (c_hbm, c_out),
            )
        )
    ]
    for copy in copies:
        copy.start()
    n_far = n_loop // 4
    my_row, my_far = lax.axis_index("row"), lax.axis_index("far")
    my_near = 2 * lax.axis_index("mid") + lax.axis_index("core")
    for copy in copies:
        copy.wait()

    def body(j, carry):
        near = jnp.bitwise_xor(lax.rem(j, 4), my_near)
        column = near * n_far + far_place(jnp.bitwise_xor(lax.div(j, 4), my_far), n_far)
        for s in range(n_row):
            slot = j * n_row + s
            place = jnp.bitwise_xor(rows_ref[slot], my_row)
            value = tiles_ref[slot]
            value = jnp.where(s < counts_ref[j], value, jnp.zeros_like(value))
            out_ref[
                pl.ds(pl.multiple_of(place * tile, tile), tile),
                pl.ds(pl.multiple_of(column * tile, tile), tile),
            ] = value
        return carry

    lax.fori_loop(0, n_loop, body, 0)


def product_rows(a_ref, first, block_refs, rows):
    step = a_ref.shape[1] // (2 * len(block_refs))
    x = jnp.concatenate([ref[:step, :] for ref in block_refs], axis=0)
    return dot(a_ref[rows, first : first + x.shape[0]], x)


def pack_kernel(*refs):
    at = 0
    for ref in refs[:-1]:
        refs[-1][at : at + ref.shape[0], :] = ref[...]
        at += ref.shape[0]


def near_kernel(tile, n_row, a_ref, *refs):
    block_refs, out_ref = refs[:-1], refs[-1]
    step = min(2, n_row) * tile
    for at in range(0, n_row * tile, step):
        rows = slice(at, at + step)
        out_ref[rows, :] = product_rows(a_ref, 0, block_refs, rows)


def output_kernel(w_ref, b_ref, h_ref, out_ref):
    preact = dot(h_ref[...], w_ref[...]) + b_ref[...]
    out_ref[...] = (preact * sigmoid(preact)).astype(BF16)


def rest_kernel(tile, n_row, n_blocks, a_ref, half_ref, *refs):
    block_refs, own_ref, send_refs = refs[:n_blocks], refs[n_blocks], refs[n_blocks + 1 :]
    first = a_ref.shape[1] // 2
    step = min(2, n_row)
    for q in range(0, n_row, step):
        rows = slice(q * tile, (q + step) * tile)
        total = half_ref[rows, :] + product_rows(a_ref, first, block_refs, rows)
        for k in range(step):
            part = total[k * tile : (k + 1) * tile, :]
            if q + k == 0:
                own_ref[...] = part
            else:
                send_refs[q + k - 1][...] = part.astype(BF16)


def sum_kernel(own_ref, *refs):
    part_refs, out_ref = refs[:-1], refs[-1]
    total = own_ref[...]
    for ref in part_refs:
        total = total + ref[...].astype(F32)
    out_ref[...] = total.astype(BF16)


def chunk_grads(w_ref, b_ref, h_ref, c_ref, gh_ref):
    tile, width = h_ref.shape[0] // 2, h_ref.shape[1]
    weight_sums, bias_sums = [], []
    for k in range(2):
        rows = slice(k * tile, (k + 1) * tile)
        hidden = h_ref[rows, :]
        preact = dot(hidden, w_ref[...]) + b_ref[...]
        sig = sigmoid(preact)
        grad_z = c_ref[rows, :].astype(F32) * sig * (1.0 + preact * (1.0 - sig))
        half = grad_z.astype(BF16)
        gh_ref[rows, :] = dot(half, w_ref[...], ((1,), (1,))).astype(BF16)
        bias_sums.append(jnp.sum(grad_z.reshape(tile // 8, 8, width), axis=0))
        weight_sums.append(dot(hidden, half, ((0,), (0,))))
    return tree_sum(weight_sums), tree_sum(bias_sums)


def chunk_kernel(w_ref, b_ref, h_ref, c_ref, gh_ref, gw_ref, gb_ref):
    gw_ref[...], gb_ref[...] = chunk_grads(w_ref, b_ref, h_ref, c_ref, gh_ref)


def write_message(ref, grad_w, bias):
    rows, width = grad_w.shape
    ref[:rows, :] = grad_w.astype(BF16)
    high = bias.astype(BF16).astype(F32)
    row = lax.broadcasted_iota(jnp.int32, (PAD, width), 0)
    low = jnp.broadcast_to(bias - high, (PAD, width))
    high = jnp.broadcast_to(high, (PAD, width))
    ref[rows:, :] = jnp.where(row == 0, high, jnp.where(row == 1, low, 0.0)).astype(BF16)


def read_message(ref):
    rows = ref.shape[0] - PAD
    tail = ref[rows:, :].astype(F32)
    return ref[:rows, :].astype(F32), tail[0:1, :] + tail[1:2, :]


def last_chunk_kernel(n, w_ref, b_ref, h_ref, c_ref, *refs):
    gw_refs, gb_refs = refs[:n], refs[n : 2 * n]
    gh_ref, both_ref, keep_ref, sum_ref = refs[2 * n :]
    half = keep_ref.shape[0] - PAD
    grad_w, grad_b = chunk_grads(w_ref, b_ref, h_ref, c_ref, gh_ref)
    sum_ref[...] = tree_sum([ref[...] for ref in gw_refs] + [grad_w])
    grad_b = tree_sum([ref[...] for ref in gb_refs] + [grad_b])
    bias = jnp.sum(grad_b, axis=0, keepdims=True)
    core = lax.axis_index("core")
    kept = sum_ref[pl.ds(pl.multiple_of(core * half, half), half), :]
    sent = sum_ref[pl.ds(pl.multiple_of((1 - core) * half, half), half), :]
    write_message(keep_ref, kept, bias)
    at = gh_ref.shape[0]
    both_ref[:at, :] = gh_ref[...]
    write_message(both_ref.at[at:, :], sent, bias)


def message_kernel(own_ref, other_ref, out_ref):
    own_w, own_b = read_message(own_ref)
    other_w, other_b = read_message(other_ref.at[other_ref.shape[0] - own_ref.shape[0] :, :])
    write_message(out_ref, own_w + other_w, own_b + other_b)


def last_kernel(factor, m00_ref, m10_ref, m01_ref, m11_ref, *refs):
    weight_ref, bias_ref, features_ref = refs[-3:]
    sum_kernel(*refs[:-3], features_ref)
    half = weight_ref.shape[0] // 2
    core = lax.axis_index("core")
    for k, (near_ref, far_ref) in enumerate(((m00_ref, m10_ref), (m01_ref, m11_ref))):
        near_w, near_b = read_message(near_ref)
        far_w, far_b = read_message(far_ref)
        at = jnp.bitwise_xor(core, k) * half
        weight_ref[pl.ds(pl.multiple_of(at, half), half), :] = (near_w + far_w) * factor
        if k == 0:
            bias_ref[...] = (near_b + far_b) * factor


def call(kernel, name, outs, operands, scratch=(), specs=None, flops=0):
    size = sum(o.size * o.dtype.itemsize for o in list(operands) + list(outs))
    held = size + sum(
        math.prod(s.shape) * s.dtype.itemsize for s in scratch if hasattr(s.dtype, "itemsize")
    )
    return pl.pallas_call(
        kernel,
        name=name,
        out_shape=outs,
        in_specs=specs or [VMEM] * len(operands),
        out_specs=[VMEM] * len(outs),
        scratch_shapes=scratch,
        cost_estimate=pl.CostEstimate(flops=flops, bytes_accessed=size, transcendentals=0),
        compiler_params=pltpu.CompilerParams(vmem_limit_bytes=2 * held + 4 * MIB),
    )(*operands)


def shards(n_loop, n_row, features, weight, bias_vector, cotangent, tile_values, tile_rows, counts):
    tile, width = features.shape
    n_far = n_loop // 4
    nodes = tile * n_loop * n_row
    rows = n_row * tile
    flops = rows * n_loop * tile * width

    steps = far_masks(n_far)

    def pack(*blocks):
        return call(pack_kernel, "pack", [shape(2 * tile, width)], blocks)[0]

    def far_partner(block):
        return partner(block, "far", steps[0], n_far)

    def far_chunks(pair):
        chunks = [pair]
        for step in steps[1:]:
            chunks = chunks + [partner(chunk, "far", step, n_far) for chunk in chunks]
        return chunks

    def near_product(near, name):
        return call(
            functools.partial(near_kernel, tile, n_row),
            name + "_near",
            [shape(rows, width, dtype=F32)],
            [adjacency] + near,
            flops=flops,
        )[0]

    def rest_product(half, rest, name):
        return call(
            functools.partial(rest_kernel, tile, n_row, len(rest)),
            name + "_rest",
            [shape(tile, width, dtype=F32)] + [shape(tile, width)] * (n_row - 1),
            [adjacency, half] + rest,
            flops=flops,
        )

    def from_row(parts):
        return [partner(part, "row", q + 1, n_row) for q, part in enumerate(parts)]

    other = far_partner(features)
    adjacency, features, cotangent = call(
        functools.partial(expand_kernel, n_loop, n_row, tile),
        "expand",
        [shape(rows, n_loop * tile), shape(tile, width), shape(tile, width)],
        [
            pltpu.with_memory_space_constraint(x, pltpu.HBM)
            for x in (tile_rows, counts, tile_values, features, cotangent)
        ],
        scratch=[
            pltpu.SMEM(tile_rows.shape, jnp.int32),
            pltpu.SMEM(counts.shape, jnp.int32),
            pltpu.VMEM(tile_values.shape, BF16),
            pltpu.SemaphoreType.DMA((5,)),
        ],
        specs=[pl.BlockSpec(memory_space=pltpu.HBM)] * 5,
    )
    f00 = far_chunks(pack(features, other))
    f10 = [swap(chunk, "mid") for chunk in f00]
    other_cot = far_partner(after(cotangent, f00[-1]))
    f01 = [swap(chunk, "core") for chunk in f00]
    f11 = [swap(chunk, "core") for chunk in f10]
    half = near_product(f00 + f01, "forward")
    own, *parts = rest_product(half, f10 + f11, "forward")
    others = from_row(parts)
    cots = far_chunks(pack(after(cotangent, own), other_cot))
    (hidden,) = call(sum_kernel, "hidden", [shape(tile, width)], [after(own, other_cot)] + others)

    bias_row = bias_vector.reshape(1, width)
    (output,) = call(
        output_kernel, "output", [shape(tile, width)], [weight, bias_row, hidden]
    )
    other, hidden = far_partner(hidden), after(hidden, output)
    hiddens = far_chunks(pack(hidden, other))
    chunk_flops = 2 * tile * 6 * width * width
    g00, weight_sums, bias_sums = [], [], []
    sums = [shape(width, width, dtype=F32), shape(8, width, dtype=F32)]
    for chunk, cot in zip(hiddens[:-1], cots[:-1]):
        gh, weight_sum, bias_sum = call(
            chunk_kernel,
            "chunk",
            [shape(2 * tile, width)] + sums,
            [weight, bias_row, chunk, after(cot, cots[-1])],
            flops=chunk_flops,
        )
        g00.append(gh)
        weight_sums.append(weight_sum)
        bias_sums.append(bias_sum)
    half_rows = width // 2 + PAD
    g01 = [swap(chunk, "core") for chunk in g00]
    g10 = [swap(chunk, "mid") for chunk in g00]
    gh, both, keep = call(
        functools.partial(last_chunk_kernel, len(g00)),
        "last_chunk",
        [shape(2 * tile, width), shape(2 * tile + half_rows, width), shape(half_rows, width)],
        [weight, bias_row, hiddens[-1], cots[-1]] + weight_sums + bias_sums,
        scratch=[pltpu.VMEM((width, width), F32)],
        flops=chunk_flops,
    )
    g00.append(gh)
    g01.append(swap(after(both, *g10), "core"))
    g10.append(swap(gh, "mid"))

    (message,) = call(message_kernel, "sum_core", [shape(half_rows, width)], [keep, g01[-1]])
    bit = 1
    while bit < n_row:
        (message,) = call(
            message_kernel,
            "sum_row",
            [shape(half_rows, width)],
            [message, partner(message, "row", bit, n_row)],
        )
        bit *= 2
    g11 = [swap(chunk, "core") for chunk in g10[:-1] + [after(g10[-1], message)]]
    half = near_product(g00 + g01, "backward")
    own, *parts = rest_product(half, g10 + g11, "backward")
    others = from_row(parts)
    message = after(message, own)
    messages = [
        message,
        swap(message, "mid"),
        swap(message, "core"),
        lax.ppermute(message, ("mid", "core"), [(i, 3 - i) for i in range(4)]),
    ]
    weight_grad, bias_grad, grad_features = call(
        functools.partial(last_kernel, 1.0 / nodes**0.5),
        "last",
        [shape(width, width, dtype=F32), shape(1, width, dtype=F32), shape(tile, width)],
        messages + [own] + others,
    )
    return output, grad_features, weight_grad, bias_grad.reshape(width)


def solution(mesh):
    n_loop, n_row = mesh.shape["loop"], mesh.shape["row"]
    every = ("far", "mid", "core", "row")
    fine = Mesh(mesh.devices.reshape(n_loop // 4, 2, 2, n_row), every)
    in_specs = (
        P(every, None),
        P(),
        P(),
        P(every, None),
        P(every, None, None),
        P(every),
        P(every),
    )
    out_specs = (P(every, None), P(every, None), P(), P())
    return jax.shard_map(
        functools.partial(shards, n_loop, n_row),
        mesh=fine,
        in_specs=in_specs,
        out_specs=out_specs,
        check_vma=False,
    )
```

```python
import functools
import math

import jax
import jax.numpy as jnp
from jax import lax
from jax.experimental import pallas as pl
from jax.experimental.pallas import tpu as pltpu
from jax.sharding import Mesh
from jax.sharding import PartitionSpec as P

BF16 = jnp.bfloat16
F32 = jnp.float32
VMEM = pl.BlockSpec(memory_space=pltpu.VMEM)
SMEM = pl.BlockSpec(memory_space=pltpu.SMEM)
MIB = 1024 * 1024
PAD = 16


def partner(x, axis, mask, n):
    return lax.ppermute(x, axis, [(i, i ^ mask) for i in range(n)])


def swap(x, axis):
    return partner(x, axis, 1, 2)


def after(x, *others):
    return lax.optimization_barrier((x,) + others)[0]


def shape(*dims, dtype=BF16):
    return jax.ShapeDtypeStruct(dims, dtype)


def dot(a, b, contract=((1,), (0,))):
    return lax.dot_general(a, b, (contract, ((), ())), preferred_element_type=F32)


def sigmoid(x):
    return 0.5 * jnp.tanh(0.5 * x) + 0.5


def tree_sum(parts):
    while len(parts) > 1:
        parts = [parts[i] + parts[i + 1] for i in range(0, len(parts), 2)]
    return parts[0]


def far_masks(n_far):
    return [1 << k for k in reversed(range(n_far.bit_length() - 1))]


def far_place(mask, n_far):
    place = 0
    for k, step in enumerate(far_masks(n_far)):
        place = place + jnp.where(jnp.bitwise_and(mask, step) > 0, 1 << k, 0)
    return place


def expand_kernel(
    n_loop, n_row, tile, rows_hbm, counts_hbm, tiles_hbm, f_hbm, c_hbm, out_ref, f_out, c_out,
    rows_ref, counts_ref, tiles_ref, sems,
):
    copies = [
        pltpu.make_async_copy(source, target, sems.at[k])
        for k, (source, target) in enumerate(
            (
                (rows_hbm, rows_ref),
                (counts_hbm, counts_ref),
                (tiles_hbm, tiles_ref),
                (f_hbm, f_out),
                (c_hbm, c_out),
            )
        )
    ]
    for copy in copies:
        copy.start()
    n_far = n_loop // 4
    my_row, my_far = lax.axis_index("row"), lax.axis_index("far")
    my_near = 2 * lax.axis_index("mid") + lax.axis_index("core")
    for copy in copies:
        copy.wait()

    def body(j, carry):
        near = jnp.bitwise_xor(lax.rem(j, 4), my_near)
        column = near * n_far + far_place(jnp.bitwise_xor(lax.div(j, 4), my_far), n_far)
        for s in range(n_row):
            slot = j * n_row + s
            place = jnp.bitwise_xor(rows_ref[slot], my_row)
            value = tiles_ref[slot]
            value = jnp.where(s < counts_ref[j], value, jnp.zeros_like(value))
            out_ref[
                pl.ds(pl.multiple_of(place * tile, tile), tile),
                pl.ds(pl.multiple_of(column * tile, tile), tile),
            ] = value
        return carry

    lax.fori_loop(0, n_loop, body, 0)


def product_rows(a_ref, first, block_refs, rows):
    step = a_ref.shape[1] // (2 * len(block_refs))
    x = jnp.concatenate([ref[:step, :] for ref in block_refs], axis=0)
    return dot(a_ref[rows, first : first + x.shape[0]], x)


def pack_kernel(*refs):
    at = 0
    for ref in refs[:-1]:
        refs[-1][at : at + ref.shape[0], :] = ref[...]
        at += ref.shape[0]


def near_kernel(tile, n_row, a_ref, *refs):
    block_refs, out_ref = refs[:-1], refs[-1]
    step = min(2, n_row) * tile
    for at in range(0, n_row * tile, step):
        rows = slice(at, at + step)
        out_ref[rows, :] = product_rows(a_ref, 0, block_refs, rows)


def output_kernel(w_ref, b_ref, h_ref, out_ref):
    preact = dot(h_ref[...], w_ref[...]) + b_ref[...]
    out_ref[...] = (preact * sigmoid(preact)).astype(BF16)


def rest_kernel(tile, n_row, n_blocks, a_ref, half_ref, *refs):
    block_refs, own_ref, send_refs = refs[:n_blocks], refs[n_blocks], refs[n_blocks + 1 :]
    first = a_ref.shape[1] // 2
    step = min(2, n_row)
    for q in range(0, n_row, step):
        rows = slice(q * tile, (q + step) * tile)
        total = half_ref[rows, :] + product_rows(a_ref, first, block_refs, rows)
        for k in range(step):
            part = total[k * tile : (k + 1) * tile, :]
            if q + k == 0:
                own_ref[...] = part
            else:
                send_refs[q + k - 1][...] = part.astype(BF16)


def sum_kernel(own_ref, *refs):
    part_refs, out_ref = refs[:-1], refs[-1]
    total = own_ref[...]
    for ref in part_refs:
        total = total + ref[...].astype(F32)
    out_ref[...] = total.astype(BF16)


def chunk_grads(w_ref, b_ref, h_ref, c_ref, gh_ref):
    tile, width = h_ref.shape[0] // 2, h_ref.shape[1]
    weight_sums, bias_sums = [], []
    for k in range(2):
        rows = slice(k * tile, (k + 1) * tile)
        hidden = h_ref[rows, :]
        preact = dot(hidden, w_ref[...]) + b_ref[...]
        sig = sigmoid(preact)
        grad_z = c_ref[rows, :].astype(F32) * sig * (1.0 + preact * (1.0 - sig))
        half = grad_z.astype(BF16)
        gh_ref[rows, :] = dot(half, w_ref[...], ((1,), (1,))).astype(BF16)
        bias_sums.append(jnp.sum(grad_z.reshape(tile // 8, 8, width), axis=0))
        weight_sums.append(dot(hidden, half, ((0,), (0,))))
    return tree_sum(weight_sums), tree_sum(bias_sums)


def chunk_kernel(w_ref, b_ref, h_ref, c_ref, gh_ref, gw_ref, gb_ref):
    gw_ref[...], gb_ref[...] = chunk_grads(w_ref, b_ref, h_ref, c_ref, gh_ref)


def write_message(ref, grad_w, bias):
    rows, width = grad_w.shape
    ref[:rows, :] = grad_w.astype(BF16)
    high = bias.astype(BF16).astype(F32)
    row = lax.broadcasted_iota(jnp.int32, (PAD, width), 0)
    low = jnp.broadcast_to(bias - high, (PAD, width))
    high = jnp.broadcast_to(high, (PAD, width))
    ref[rows:, :] = jnp.where(row == 0, high, jnp.where(row == 1, low, 0.0)).astype(BF16)


def read_message(ref):
    rows = ref.shape[0] - PAD
    tail = ref[rows:, :].astype(F32)
    return ref[:rows, :].astype(F32), tail[0:1, :] + tail[1:2, :]


def last_chunk_kernel(n, w_ref, b_ref, h_ref, c_ref, *refs):
    gw_refs, gb_refs = refs[:n], refs[n : 2 * n]
    gh_ref, both_ref, keep_ref, sum_ref = refs[2 * n :]
    half = keep_ref.shape[0] - PAD
    grad_w, grad_b = chunk_grads(w_ref, b_ref, h_ref, c_ref, gh_ref)
    sum_ref[...] = tree_sum([ref[...] for ref in gw_refs] + [grad_w])
    grad_b = tree_sum([ref[...] for ref in gb_refs] + [grad_b])
    bias = jnp.sum(grad_b, axis=0, keepdims=True)
    core = lax.axis_index("core")
    kept = sum_ref[pl.ds(pl.multiple_of(core * half, half), half), :]
    sent = sum_ref[pl.ds(pl.multiple_of((1 - core) * half, half), half), :]
    write_message(keep_ref, kept, bias)
    at = gh_ref.shape[0]
    both_ref[:at, :] = gh_ref[...]
    write_message(both_ref.at[at:, :], sent, bias)


def message_kernel(own_ref, other_ref, out_ref):
    own_w, own_b = read_message(own_ref)
    other_w, other_b = read_message(other_ref.at[other_ref.shape[0] - own_ref.shape[0] :, :])
    write_message(out_ref, own_w + other_w, own_b + other_b)


def halves_kernel(own_ref, other_ref, out_ref):
    half = own_ref.shape[0] - PAD
    core = lax.axis_index("core")
    out_ref[pl.ds(pl.multiple_of(core * half, half), half), :] = own_ref[:half, :]
    out_ref[pl.ds(pl.multiple_of((1 - core) * half, half), half), :] = other_ref[:half, :]
    out_ref[2 * half :, :] = own_ref[half:, :]


def last_kernel(factor, near_ref, far_ref, *refs):
    weight_ref, bias_ref, features_ref = refs[-3:]
    sum_kernel(*refs[:-3], features_ref)
    near_w, near_b = read_message(near_ref)
    far_w, far_b = read_message(far_ref)
    weight_ref[...] = (near_w + far_w) * factor
    bias_ref[...] = (near_b + far_b) * factor


def call(kernel, name, outs, operands, scratch=(), specs=None, flops=0):
    size = sum(o.size * o.dtype.itemsize for o in list(operands) + list(outs))
    held = size + sum(
        math.prod(s.shape) * s.dtype.itemsize for s in scratch if hasattr(s.dtype, "itemsize")
    )
    return pl.pallas_call(
        kernel,
        name=name,
        out_shape=outs,
        in_specs=specs or [VMEM] * len(operands),
        out_specs=[VMEM] * len(outs),
        scratch_shapes=scratch,
        cost_estimate=pl.CostEstimate(flops=flops, bytes_accessed=size, transcendentals=0),
        compiler_params=pltpu.CompilerParams(vmem_limit_bytes=2 * held + 4 * MIB),
    )(*operands)


def shards(n_loop, n_row, features, weight, bias_vector, cotangent, tile_values, tile_rows, counts):
    tile, width = features.shape
    n_far = n_loop // 4
    nodes = tile * n_loop * n_row
    rows = n_row * tile
    flops = rows * n_loop * tile * width

    steps = far_masks(n_far)

    def pack(*blocks):
        return call(pack_kernel, "pack", [shape(2 * tile, width)], blocks)[0]

    def far_partner(block):
        return partner(block, "far", steps[0], n_far)

    def far_chunks(pair):
        chunks = [pair]
        for step in steps[1:]:
            chunks = chunks + [partner(chunk, "far", step, n_far) for chunk in chunks]
        return chunks

    def near_product(near, name):
        return call(
            functools.partial(near_kernel, tile, n_row),
            name + "_near",
            [shape(rows, width, dtype=F32)],
            [adjacency] + near,
            flops=flops,
        )[0]

    def rest_product(half, rest, name):
        return call(
            functools.partial(rest_kernel, tile, n_row, len(rest)),
            name + "_rest",
            [shape(tile, width, dtype=F32)] + [shape(tile, width)] * (n_row - 1),
            [adjacency, half] + rest,
            flops=flops,
        )

    def from_row(parts):
        return [partner(part, "row", q + 1, n_row) for q, part in enumerate(parts)]

    other, other_cot = far_partner(features), far_partner(cotangent)
    adjacency, features, cotangent = call(
        functools.partial(expand_kernel, n_loop, n_row, tile),
        "expand",
        [shape(rows, n_loop * tile), shape(tile, width), shape(tile, width)],
        [
            pltpu.with_memory_space_constraint(x, pltpu.HBM)
            for x in (tile_rows, counts, tile_values, features, cotangent)
        ],
        scratch=[
            pltpu.SMEM(tile_rows.shape, jnp.int32),
            pltpu.SMEM(counts.shape, jnp.int32),
            pltpu.VMEM(tile_values.shape, BF16),
            pltpu.SemaphoreType.DMA((5,)),
        ],
        specs=[pl.BlockSpec(memory_space=pltpu.HBM)] * 5,
    )
    f00 = far_chunks(pack(features, after(other, other_cot)))
    f10 = [swap(chunk, "mid") for chunk in f00]
    cots = far_chunks(pack(cotangent, other_cot))
    f01 = [swap(chunk, "core") for chunk in f00]
    f11 = [swap(chunk, "core") for chunk in f10[:-1] + [after(f10[-1], *cots)]]
    half = near_product(f00 + f01, "forward")
    own, *parts = rest_product(half, f10 + f11, "forward")
    others = from_row(parts)
    (hidden,) = call(sum_kernel, "hidden", [shape(tile, width)], [own] + others)

    bias_row = bias_vector.reshape(1, width)
    (output,) = call(
        output_kernel, "output", [shape(tile, width)], [weight, bias_row, hidden]
    )
    other, hidden = far_partner(hidden), after(hidden, output)
    hiddens = far_chunks(pack(hidden, other))
    chunk_flops = 2 * tile * 6 * width * width
    g00, weight_sums, bias_sums = [], [], []
    sums = [shape(width, width, dtype=F32), shape(8, width, dtype=F32)]
    for chunk, cot in zip(hiddens[:-1], cots[:-1]):
        gh, weight_sum, bias_sum = call(
            chunk_kernel,
            "chunk",
            [shape(2 * tile, width)] + sums,
            [weight, bias_row, chunk, cot],
            flops=chunk_flops,
        )
        g00.append(gh)
        weight_sums.append(weight_sum)
        bias_sums.append(bias_sum)
    half_rows = width // 2 + PAD
    g01 = [swap(chunk, "core") for chunk in g00]
    g10 = [swap(chunk, "mid") for chunk in g00]
    gh, both, keep = call(
        functools.partial(last_chunk_kernel, len(g00)),
        "last_chunk",
        [shape(2 * tile, width), shape(2 * tile + half_rows, width), shape(half_rows, width)],
        [weight, bias_row, hiddens[-1], cots[-1]] + weight_sums + bias_sums,
        scratch=[pltpu.VMEM((width, width), F32)],
        flops=chunk_flops,
    )
    g00.append(gh)
    g01.append(swap(after(both, *g10), "core"))
    g10.append(swap(gh, "mid"))

    (message,) = call(message_kernel, "sum_core", [shape(half_rows, width)], [keep, g01[-1]])
    bit = 1
    while bit < n_row:
        (message,) = call(
            message_kernel,
            "sum_row",
            [shape(half_rows, width)],
            [message, partner(message, "row", bit, n_row)],
        )
        bit *= 2
    g11 = [swap(chunk, "core") for chunk in g10[:-1] + [after(g10[-1], message)]]
    half = near_product(g00 + g01, "backward")
    own, *parts = rest_product(half, g10 + g11, "backward")
    others = from_row(parts)
    (message,) = call(
        halves_kernel,
        "halves",
        [shape(width + PAD, width)],
        [message, swap(message, "core")],
    )
    message = after(message, own)
    messages = [message, swap(message, "mid")]
    weight_grad, bias_grad, grad_features = call(
        functools.partial(last_kernel, 1.0 / nodes**0.5),
        "last",
        [shape(width, width, dtype=F32), shape(1, width, dtype=F32), shape(tile, width)],
        messages + [own] + others,
    )
    return output, grad_features, weight_grad, bias_grad.reshape(width)


def solution(mesh):
    n_loop, n_row = mesh.shape["loop"], mesh.shape["row"]
    every = ("far", "mid", "core", "row")
    fine = Mesh(mesh.devices.reshape(n_loop // 4, 2, 2, n_row), every)
    in_specs = (
        P(every, None),
        P(),
        P(),
        P(every, None),
        P(every, None, None),
        P(every),
        P(every),
    )
    out_specs = (P(every, None), P(every, None), P(), P())
    return jax.shard_map(
        functools.partial(shards, n_loop, n_row),
        mesh=fine,
        in_specs=in_specs,
        out_specs=out_specs,
        check_vma=False,
    )
```

```python
import functools
import math

import jax
import jax.numpy as jnp
from jax import lax
from jax.experimental import pallas as pl
from jax.experimental.pallas import tpu as pltpu
from jax.sharding import Mesh
from jax.sharding import PartitionSpec as P

BF16 = jnp.bfloat16
F32 = jnp.float32
VMEM = pl.BlockSpec(memory_space=pltpu.VMEM)
SMEM = pl.BlockSpec(memory_space=pltpu.SMEM)
MIB = 1024 * 1024
PAD = 16


def partner(x, axis, mask, n):
    return lax.ppermute(x, axis, [(i, i ^ mask) for i in range(n)])


def swap(x, axis):
    return partner(x, axis, 1, 2)


def after(x, *others):
    return lax.optimization_barrier((x,) + others)[0]


def shape(*dims, dtype=BF16):
    return jax.ShapeDtypeStruct(dims, dtype)


def dot(a, b, contract=((1,), (0,))):
    return lax.dot_general(a, b, (contract, ((), ())), preferred_element_type=F32)


def sigmoid(x):
    return 0.5 * jnp.tanh(0.5 * x) + 0.5


def tree_sum(parts):
    while len(parts) > 1:
        parts = [parts[i] + parts[i + 1] for i in range(0, len(parts), 2)]
    return parts[0]


def far_masks(n_far):
    return [1 << k for k in reversed(range(n_far.bit_length() - 1))]


def far_place(mask, n_far):
    place = 0
    for k, step in enumerate(far_masks(n_far)):
        place = place + jnp.where(jnp.bitwise_and(mask, step) > 0, 1 << k, 0)
    return place


def expand_kernel(
    n_loop, n_row, tile, rows_hbm, counts_hbm, tiles_hbm, f_hbm, c_hbm, out_ref, f_out, c_out,
    rows_ref, counts_ref, tiles_ref, sems,
):
    copies = [
        pltpu.make_async_copy(source, target, sems.at[k])
        for k, (source, target) in enumerate(
            (
                (rows_hbm, rows_ref),
                (counts_hbm, counts_ref),
                (tiles_hbm, tiles_ref),
                (f_hbm, f_out),
                (c_hbm, c_out),
            )
        )
    ]
    for copy in copies:
        copy.start()
    n_far = n_loop // 4
    my_row, my_far = lax.axis_index("row"), lax.axis_index("far")
    my_near = 2 * lax.axis_index("mid") + lax.axis_index("core")
    for copy in copies:
        copy.wait()

    def body(j, carry):
        near = jnp.bitwise_xor(lax.rem(j, 4), my_near)
        column = near * n_far + far_place(jnp.bitwise_xor(lax.div(j, 4), my_far), n_far)
        for s in range(n_row):
            slot = j * n_row + s
            place = jnp.bitwise_xor(rows_ref[slot], my_row)
            value = tiles_ref[slot]
            value = jnp.where(s < counts_ref[j], value, jnp.zeros_like(value))
            out_ref[
                pl.ds(pl.multiple_of(place * tile, tile), tile),
                pl.ds(pl.multiple_of(column * tile, tile), tile),
            ] = value
        return carry

    lax.fori_loop(0, n_loop, body, 0)


def product_rows(a_ref, first, block_refs, rows):
    step = a_ref.shape[1] // (2 * len(block_refs))
    x = jnp.concatenate([ref[:step, :] for ref in block_refs], axis=0)
    return dot(a_ref[rows, first : first + x.shape[0]], x)


def pack_kernel(*refs):
    at = 0
    for ref in refs[:-1]:
        refs[-1][at : at + ref.shape[0], :] = ref[...]
        at += ref.shape[0]


def near_kernel(tile, n_row, a_ref, *refs):
    block_refs, out_ref = refs[:-1], refs[-1]
    step = min(2, n_row) * tile
    for at in range(0, n_row * tile, step):
        rows = slice(at, at + step)
        out_ref[rows, :] = product_rows(a_ref, 0, block_refs, rows)


def output_kernel(w_ref, b_ref, h_ref, out_ref):
    preact = dot(h_ref[...], w_ref[...]) + b_ref[...]
    out_ref[...] = (preact * sigmoid(preact)).astype(BF16)


def rest_kernel(tile, n_row, n_blocks, a_ref, half_ref, *refs):
    block_refs, own_ref, send_refs = refs[:n_blocks], refs[n_blocks], refs[n_blocks + 1 :]
    first = a_ref.shape[1] // 2
    step = min(2, n_row)
    for q in range(0, n_row, step):
        rows = slice(q * tile, (q + step) * tile)
        total = half_ref[rows, :] + product_rows(a_ref, first, block_refs, rows)
        for k in range(step):
            part = total[k * tile : (k + 1) * tile, :]
            if q + k == 0:
                own_ref[...] = part
            else:
                send_refs[q + k - 1][...] = part.astype(BF16)


def sum_kernel(own_ref, *refs):
    part_refs, out_ref = refs[:-1], refs[-1]
    total = own_ref[...]
    for ref in part_refs:
        total = total + ref[...].astype(F32)
    out_ref[...] = total.astype(BF16)


def chunk_grads(w_ref, b_ref, h_ref, c_refs, gh_ref):
    tile, width = h_ref.shape[0] // 2, h_ref.shape[1]
    weight_sums, bias_sums = [], []
    for k, (c_ref, half) in enumerate(c_refs):
        rows = slice(k * tile, (k + 1) * tile)
        hidden = h_ref[rows, :]
        preact = dot(hidden, w_ref[...]) + b_ref[...]
        sig = sigmoid(preact)
        cot = c_ref[half * tile : (half + 1) * tile, :].astype(F32)
        grad_z = cot * sig * (1.0 + preact * (1.0 - sig))
        half = grad_z.astype(BF16)
        gh_ref[rows, :] = dot(half, w_ref[...], ((1,), (1,))).astype(BF16)
        bias_sums.append(jnp.sum(grad_z.reshape(tile // 8, 8, width), axis=0))
        weight_sums.append(dot(hidden, half, ((0,), (0,))))
    return tree_sum(weight_sums), tree_sum(bias_sums)


def chunk_kernel(halves, w_ref, b_ref, h_ref, c0_ref, c1_ref, gh_ref, gw_ref, gb_ref):
    c_refs = list(zip((c0_ref, c1_ref), halves))
    gw_ref[...], gb_ref[...] = chunk_grads(w_ref, b_ref, h_ref, c_refs, gh_ref)


def write_message(ref, grad_w, bias):
    rows, width = grad_w.shape
    ref[:rows, :] = grad_w.astype(BF16)
    high = bias.astype(BF16).astype(F32)
    row = lax.broadcasted_iota(jnp.int32, (PAD, width), 0)
    low = jnp.broadcast_to(bias - high, (PAD, width))
    high = jnp.broadcast_to(high, (PAD, width))
    ref[rows:, :] = jnp.where(row == 0, high, jnp.where(row == 1, low, 0.0)).astype(BF16)


def read_message(ref):
    rows = ref.shape[0] - PAD
    tail = ref[rows:, :].astype(F32)
    return ref[:rows, :].astype(F32), tail[0:1, :] + tail[1:2, :]


def last_chunk_kernel(halves, n, w_ref, b_ref, h_ref, c0_ref, c1_ref, *refs):
    gw_refs, gb_refs = refs[:n], refs[n : 2 * n]
    gh_ref, both_ref, keep_ref, sum_ref = refs[2 * n :]
    half = keep_ref.shape[0] - PAD
    c_refs = list(zip((c0_ref, c1_ref), halves))
    grad_w, grad_b = chunk_grads(w_ref, b_ref, h_ref, c_refs, gh_ref)
    sum_ref[...] = tree_sum([ref[...] for ref in gw_refs] + [grad_w])
    grad_b = tree_sum([ref[...] for ref in gb_refs] + [grad_b])
    bias = jnp.sum(grad_b, axis=0, keepdims=True)
    core = lax.axis_index("core")
    kept = sum_ref[pl.ds(pl.multiple_of(core * half, half), half), :]
    sent = sum_ref[pl.ds(pl.multiple_of((1 - core) * half, half), half), :]
    write_message(keep_ref, kept, bias)
    at = gh_ref.shape[0]
    both_ref[:at, :] = gh_ref[...]
    write_message(both_ref.at[at:, :], sent, bias)


def message_kernel(own_ref, other_ref, out_ref):
    own_w, own_b = read_message(own_ref)
    other_w, other_b = read_message(other_ref.at[other_ref.shape[0] - own_ref.shape[0] :, :])
    write_message(out_ref, own_w + other_w, own_b + other_b)


def halves_kernel(own_ref, other_ref, out_ref):
    half = own_ref.shape[0] - PAD
    core = lax.axis_index("core")
    out_ref[pl.ds(pl.multiple_of(core * half, half), half), :] = own_ref[:half, :]
    out_ref[pl.ds(pl.multiple_of((1 - core) * half, half), half), :] = other_ref[:half, :]
    out_ref[2 * half :, :] = own_ref[half:, :]


def last_kernel(factor, near_ref, far_ref, *refs):
    weight_ref, bias_ref, features_ref = refs[-3:]
    sum_kernel(*refs[:-3], features_ref)
    near_w, near_b = read_message(near_ref)
    far_w, far_b = read_message(far_ref)
    weight_ref[...] = (near_w + far_w) * factor
    bias_ref[...] = (near_b + far_b) * factor


def call(kernel, name, outs, operands, scratch=(), specs=None, flops=0):
    size = sum(o.size * o.dtype.itemsize for o in list(operands) + list(outs))
    held = size + sum(
        math.prod(s.shape) * s.dtype.itemsize for s in scratch if hasattr(s.dtype, "itemsize")
    )
    return pl.pallas_call(
        kernel,
        name=name,
        out_shape=outs,
        in_specs=specs or [VMEM] * len(operands),
        out_specs=[VMEM] * len(outs),
        scratch_shapes=scratch,
        cost_estimate=pl.CostEstimate(flops=flops, bytes_accessed=size, transcendentals=0),
        compiler_params=pltpu.CompilerParams(vmem_limit_bytes=2 * held + 4 * MIB),
    )(*operands)


def shards(n_loop, n_row, features, weight, bias_vector, cotangent, tile_values, tile_rows, counts):
    tile, width = features.shape
    n_far = n_loop // 4
    nodes = tile * n_loop * n_row
    rows = n_row * tile
    flops = rows * n_loop * tile * width

    steps = far_masks(n_far)

    def pack(*blocks):
        return call(pack_kernel, "pack", [shape(2 * tile, width)], blocks)[0]

    def far_partner(block, step):
        return partner(block, "far", step, n_far)

    def far_chunks(pair, steps):
        chunks = [pair]
        for step in steps[1:]:
            chunks = chunks + [partner(chunk, "far", step, n_far) for chunk in chunks]
        return chunks

    def near_product(near, name):
        return call(
            functools.partial(near_kernel, tile, n_row),
            name + "_near",
            [shape(rows, width, dtype=F32)],
            [adjacency] + near,
            flops=flops,
        )[0]

    def rest_product(half, rest, name):
        return call(
            functools.partial(rest_kernel, tile, n_row, len(rest)),
            name + "_rest",
            [shape(tile, width, dtype=F32)] + [shape(tile, width)] * (n_row - 1),
            [adjacency, half] + rest,
            flops=flops,
        )

    def from_row(parts):
        return [partner(part, "row", q + 1, n_row) for q, part in enumerate(parts)]

    cot_steps = steps[::-1]
    other, other_cot = far_partner(features, steps[0]), far_partner(cotangent, cot_steps[0])
    adjacency, features, cotangent = call(
        functools.partial(expand_kernel, n_loop, n_row, tile),
        "expand",
        [shape(rows, n_loop * tile), shape(tile, width), shape(tile, width)],
        [
            pltpu.with_memory_space_constraint(x, pltpu.HBM)
            for x in (tile_rows, counts, tile_values, features, cotangent)
        ],
        scratch=[
            pltpu.SMEM(tile_rows.shape, jnp.int32),
            pltpu.SMEM(counts.shape, jnp.int32),
            pltpu.VMEM(tile_values.shape, BF16),
            pltpu.SemaphoreType.DMA((5,)),
        ],
        specs=[pl.BlockSpec(memory_space=pltpu.HBM)] * 5,
    )
    f00 = far_chunks(pack(features, after(other, other_cot)), steps)
    f10 = [swap(chunk, "mid") for chunk in f00]
    cots = far_chunks(pack(cotangent, other_cot), cot_steps)
    f01 = [swap(chunk, "core") for chunk in f00]
    f11 = [swap(chunk, "core") for chunk in f10[:-1] + [after(f10[-1], *cots)]]
    half = near_product(f00 + f01, "forward")
    own, *parts = rest_product(half, f10 + f11, "forward")
    others = from_row(parts)
    (hidden,) = call(sum_kernel, "hidden", [shape(tile, width)], [own] + others)

    bias_row = bias_vector.reshape(1, width)
    (output,) = call(
        output_kernel, "output", [shape(tile, width)], [weight, bias_row, hidden]
    )
    other, hidden = far_partner(hidden, steps[0]), after(hidden, output)
    hiddens = far_chunks(pack(hidden, other), steps)

    def chunk_cots(k):
        bits = len(steps)
        places = [int(f"{2 * k + b:0{bits}b}"[::-1], 2) for b in range(2)]
        return [cots[p // 2] for p in places], [p % 2 for p in places]

    chunk_flops = 2 * tile * 6 * width * width
    g00, weight_sums, bias_sums = [], [], []
    sums = [shape(width, width, dtype=F32), shape(8, width, dtype=F32)]
    for k, chunk in enumerate(hiddens[:-1]):
        chunk_cot, halves = chunk_cots(k)
        gh, weight_sum, bias_sum = call(
            functools.partial(chunk_kernel, halves),
            "chunk",
            [shape(2 * tile, width)] + sums,
            [weight, bias_row, chunk] + chunk_cot,
            flops=chunk_flops,
        )
        g00.append(gh)
        weight_sums.append(weight_sum)
        bias_sums.append(bias_sum)
    half_rows = width // 2 + PAD
    g01 = [swap(chunk, "core") for chunk in g00]
    g10 = [swap(chunk, "mid") for chunk in g00]
    chunk_cot, halves = chunk_cots(len(g00))
    gh, both, keep = call(
        functools.partial(last_chunk_kernel, halves, len(g00)),
        "last_chunk",
        [shape(2 * tile, width), shape(2 * tile + half_rows, width), shape(half_rows, width)],
        [weight, bias_row, hiddens[-1]] + chunk_cot + weight_sums + bias_sums,
        scratch=[pltpu.VMEM((width, width), F32)],
        flops=chunk_flops,
    )
    g00.append(gh)
    g01.append(swap(after(both, *g10), "core"))
    g10.append(swap(gh, "mid"))

    (message,) = call(message_kernel, "sum_core", [shape(half_rows, width)], [keep, g01[-1]])
    bit = 1
    while bit < n_row:
        (message,) = call(
            message_kernel,
            "sum_row",
            [shape(half_rows, width)],
            [message, partner(message, "row", bit, n_row)],
        )
        bit *= 2
    g11 = [swap(chunk, "core") for chunk in g10]
    half = near_product([after(g00[0], message)] + g00[1:] + g01, "backward")
    own, *parts = rest_product(half, g10 + g11, "backward")
    others = from_row(parts)
    (message,) = call(
        halves_kernel,
        "halves",
        [shape(width + PAD, width)],
        [message, swap(message, "core")],
    )
    message = after(message, own)
    messages = [message, swap(message, "mid")]
    weight_grad, bias_grad, grad_features = call(
        functools.partial(last_kernel, 1.0 / nodes**0.5),
        "last",
        [shape(width, width, dtype=F32), shape(1, width, dtype=F32), shape(tile, width)],
        messages + [own] + others,
    )
    return output, grad_features, weight_grad, bias_grad.reshape(width)


def solution(mesh):
    n_loop, n_row = mesh.shape["loop"], mesh.shape["row"]
    every = ("far", "mid", "core", "row")
    fine = Mesh(mesh.devices.reshape(n_loop // 4, 2, 2, n_row), every)
    in_specs = (
        P(every, None),
        P(),
        P(),
        P(every, None),
        P(every, None, None),
        P(every),
        P(every),
    )
    out_specs = (P(every, None), P(every, None), P(), P())
    return jax.shard_map(
        functools.partial(shards, n_loop, n_row),
        mesh=fine,
        in_specs=in_specs,
        out_specs=out_specs,
        check_vma=False,
    )
```

```python
import functools
import math

import jax
import jax.numpy as jnp
from jax import lax
from jax.experimental import pallas as pl
from jax.experimental.pallas import tpu as pltpu
from jax.sharding import Mesh
from jax.sharding import PartitionSpec as P

BF16 = jnp.bfloat16
F32 = jnp.float32
VMEM = pl.BlockSpec(memory_space=pltpu.VMEM)
SMEM = pl.BlockSpec(memory_space=pltpu.SMEM)
MIB = 1024 * 1024
PAD = 16


def partner(x, axis, mask, n):
    return lax.ppermute(x, axis, [(i, i ^ mask) for i in range(n)])


def swap(x, axis):
    return partner(x, axis, 1, 2)


def after(x, *others):
    return lax.optimization_barrier((x,) + others)[0]


def shape(*dims, dtype=BF16):
    return jax.ShapeDtypeStruct(dims, dtype)


def dot(a, b, contract=((1,), (0,))):
    return lax.dot_general(a, b, (contract, ((), ())), preferred_element_type=F32)


def sigmoid(x):
    return 0.5 * jnp.tanh(0.5 * x) + 0.5


def far_masks(n_far):
    return [1 << k for k in reversed(range(n_far.bit_length() - 1))]


def far_place(mask, n_far):
    place = 0
    for k, step in enumerate(far_masks(n_far)):
        place = place + jnp.where(jnp.bitwise_and(mask, step) > 0, 1 << k, 0)
    return place


def expand_kernel(
    n_loop, n_row, tile, rows_hbm, counts_hbm, tiles_hbm, f_hbm, c_hbm, out_ref, f_out, c_out,
    rows_ref, counts_ref, tiles_ref, sems,
):
    copies = [
        pltpu.make_async_copy(source, target, sems.at[k])
        for k, (source, target) in enumerate(
            (
                (rows_hbm, rows_ref),
                (counts_hbm, counts_ref),
                (tiles_hbm, tiles_ref),
                (f_hbm, f_out),
                (c_hbm, c_out),
            )
        )
    ]
    for copy in copies:
        copy.start()
    n_far = n_loop // 4
    my_row, my_far = lax.axis_index("row"), lax.axis_index("far")
    my_near = 2 * lax.axis_index("mid") + lax.axis_index("core")
    for copy in copies:
        copy.wait()

    def body(j, carry):
        near = jnp.bitwise_xor(lax.rem(j, 4), my_near)
        column = near * n_far + far_place(jnp.bitwise_xor(lax.div(j, 4), my_far), n_far)
        for s in range(n_row):
            slot = j * n_row + s
            place = jnp.bitwise_xor(rows_ref[slot], my_row)
            value = tiles_ref[slot]
            value = jnp.where(s < counts_ref[j], value, jnp.zeros_like(value))
            out_ref[
                pl.ds(pl.multiple_of(place * tile, tile), tile),
                pl.ds(pl.multiple_of(column * tile, tile), tile),
            ] = value
        return carry

    lax.fori_loop(0, n_loop, body, 0)


def product_rows(a_ref, first, block_refs, rows):
    step = a_ref.shape[1] // (2 * len(block_refs))
    x = jnp.concatenate([ref[:step, :] for ref in block_refs], axis=0)
    return dot(a_ref[rows, first : first + x.shape[0]], x)


def pack_kernel(*refs):
    tile = refs[-1].shape[0] // (len(refs) - 1)
    for k, ref in enumerate(refs[:-1]):
        refs[-1][k * tile : (k + 1) * tile, :] = ref[:tile, :]


def near_kernel(tile, n_row, a_ref, *refs):
    block_refs, out_ref = refs[:-1], refs[-1]
    step = min(2, n_row) * tile
    for at in range(0, n_row * tile, step):
        rows = slice(at, at + step)
        out_ref[rows, :] = product_rows(a_ref, 0, block_refs, rows)


def output_kernel(w_ref, b_ref, h_ref, out_ref):
    preact = dot(h_ref[...], w_ref[...]) + b_ref[...]
    out_ref[...] = (preact * sigmoid(preact)).astype(BF16)


def rest_kernel(tile, n_row, n_blocks, a_ref, half_ref, *refs):
    block_refs, own_ref, send_refs = refs[:n_blocks], refs[n_blocks], refs[n_blocks + 1 :]
    first = a_ref.shape[1] // 2
    step = min(2, n_row)
    for q in range(0, n_row, step):
        rows = slice(q * tile, (q + step) * tile)
        total = half_ref[rows, :] + product_rows(a_ref, first, block_refs, rows)
        for k in range(step):
            part = total[k * tile : (k + 1) * tile, :]
            if q + k == 0:
                own_ref[...] = part
            else:
                send_refs[q + k - 1][...] = part.astype(BF16)


def sum_kernel(own_ref, *refs):
    part_refs, out_ref = refs[:-1], refs[-1]
    total = own_ref[...]
    for ref in part_refs:
        total = total + ref[...].astype(F32)
    out_ref[...] = total.astype(BF16)


def write_message(ref, grad_w, bias):
    rows, width = grad_w.shape
    ref[:rows, :] = grad_w.astype(BF16)
    high = bias.astype(BF16).astype(F32)
    row = lax.broadcasted_iota(jnp.int32, (PAD, width), 0)
    low = jnp.broadcast_to(bias - high, (PAD, width))
    high = jnp.broadcast_to(high, (PAD, width))
    ref[rows:, :] = jnp.where(row == 0, high, jnp.where(row == 1, low, 0.0)).astype(BF16)


def read_message(ref):
    rows = ref.shape[0] - PAD
    tail = ref[rows:, :].astype(F32)
    return ref[:rows, :].astype(F32), tail[0:1, :] + tail[1:2, :]


def grads_kernel(w_ref, b_ref, h_ref, c_ref, gh_ref, keep_ref, send_ref, sum_ref):
    half_rows = keep_ref.shape[0] - PAD
    hidden = h_ref[...]
    preact = dot(hidden, w_ref[...]) + b_ref[...]
    sig = sigmoid(preact)
    grad_z = c_ref[...].astype(F32) * sig * (1.0 + preact * (1.0 - sig))
    half = grad_z.astype(BF16)
    tile, width = h_ref.shape
    gh_ref[:tile, :] = dot(half, w_ref[...], ((1,), (1,))).astype(BF16)
    gh_ref[tile:, :] = jnp.zeros((gh_ref.shape[0] - tile, width), BF16)
    sum_ref[...] = dot(hidden, half, ((0,), (0,)))
    bias = jnp.sum(grad_z, axis=0, keepdims=True)
    core = lax.axis_index("core")
    for at, ref in ((core, keep_ref), (1 - core, send_ref)):
        rows = pl.ds(pl.multiple_of(at * half_rows, half_rows), half_rows)
        write_message(ref, sum_ref[rows, :], bias)


def message_kernel(own_ref, other_ref, out_ref):
    own_w, own_b = read_message(own_ref)
    other_w, other_b = read_message(other_ref)
    write_message(out_ref, own_w + other_w, own_b + other_b)


def last_kernel(factor, half_ref, other_ref, *refs):
    weight_ref, bias_ref, features_ref = refs[-3:]
    sum_kernel(*refs[:-3], features_ref)
    half = weight_ref.shape[0] // 2
    core = lax.axis_index("core")
    for at, ref in ((core, half_ref), (1 - core, other_ref)):
        weight, bias = read_message(ref)
        weight_ref[pl.ds(pl.multiple_of(at * half, half), half), :] = weight * factor
    bias_ref[...] = bias * factor


def call(kernel, name, outs, operands, scratch=(), specs=None, flops=0):
    size = sum(o.size * o.dtype.itemsize for o in list(operands) + list(outs))
    held = size + sum(
        math.prod(s.shape) * s.dtype.itemsize for s in scratch if hasattr(s.dtype, "itemsize")
    )
    return pl.pallas_call(
        kernel,
        name=name,
        out_shape=outs,
        in_specs=specs or [VMEM] * len(operands),
        out_specs=[VMEM] * len(outs),
        scratch_shapes=scratch,
        cost_estimate=pl.CostEstimate(flops=flops, bytes_accessed=size, transcendentals=0),
        compiler_params=pltpu.CompilerParams(vmem_limit_bytes=2 * held + 4 * MIB),
    )(*operands)


def shards(n_loop, n_row, features, weight, bias_vector, cotangent, tile_values, tile_rows, counts):
    tile, width = features.shape
    n_far = n_loop // 4
    nodes = tile * n_loop * n_row
    rows = n_row * tile
    flops = rows * n_loop * tile * width

    steps = far_masks(n_far)

    def pack(*blocks):
        return call(pack_kernel, "pack", [shape(2 * tile, width)], blocks)[0]

    def far_chunks(pair):
        chunks = [pair]
        for step in steps[1:]:
            chunks = chunks + [partner(chunk, "far", step, n_far) for chunk in chunks]
        return chunks

    def near_product(near, name):
        return call(
            functools.partial(near_kernel, tile, n_row),
            name + "_near",
            [shape(rows, width, dtype=F32)],
            [adjacency] + near,
            flops=flops,
        )[0]

    def rest_product(half, rest, name):
        return call(
            functools.partial(rest_kernel, tile, n_row, len(rest)),
            name + "_rest",
            [shape(tile, width, dtype=F32)] + [shape(tile, width)] * (n_row - 1),
            [adjacency, half] + rest,
            flops=flops,
        )

    def from_row(parts):
        return [partner(part, "row", q + 1, n_row) for q, part in enumerate(parts)]

    other = partner(features, "far", steps[0], n_far)
    adjacency, features, cotangent = call(
        functools.partial(expand_kernel, n_loop, n_row, tile),
        "expand",
        [shape(rows, n_loop * tile), shape(tile, width), shape(tile, width)],
        [
            pltpu.with_memory_space_constraint(x, pltpu.HBM)
            for x in (tile_rows, counts, tile_values, features, cotangent)
        ],
        scratch=[
            pltpu.SMEM(tile_rows.shape, jnp.int32),
            pltpu.SMEM(counts.shape, jnp.int32),
            pltpu.VMEM(tile_values.shape, BF16),
            pltpu.SemaphoreType.DMA((5,)),
        ],
        specs=[pl.BlockSpec(memory_space=pltpu.HBM)] * 5,
    )
    f00 = far_chunks(pack(features, other))
    f10 = [swap(chunk, "mid") for chunk in f00]
    f01 = [swap(chunk, "core") for chunk in f00]
    f11 = [swap(chunk, "core") for chunk in f10]
    half = near_product(f00 + f01, "forward")
    own, *parts = rest_product(half, f10 + f11, "forward")
    (hidden,) = call(sum_kernel, "hidden", [shape(tile, width)], [own] + from_row(parts))

    bias_row = bias_vector.reshape(1, width)
    message_shape = shape(width // 2 + PAD, width)
    grad_hidden, message, send = call(
        grads_kernel,
        "grads",
        [shape(tile + 2 * PAD, width), message_shape, message_shape],
        [weight, bias_row, hidden, cotangent],
        scratch=[pltpu.VMEM((width, width), F32)],
        flops=6 * tile * width * width,
    )
    (output,) = call(
        output_kernel, "output", [shape(tile, width)], [weight, bias_row, hidden]
    )

    def add(message, other, name):
        return call(message_kernel, name, [message_shape], [message, other])[0]

    message = add(message, swap(send, "core"), "sum_core")
    bit = 1
    while bit < n_row:
        message = add(message, partner(message, "row", bit, n_row), "sum_row")
        bit *= 2
    other = after(partner(grad_hidden, "far", steps[0], n_far), message, output)
    g00 = far_chunks(pack(grad_hidden, other))
    g10 = [swap(chunk, "mid") for chunk in g00]
    g01 = [swap(chunk, "core") for chunk in g00]
    g11 = [swap(chunk, "core") for chunk in g10]
    message = add(message, partner(message, "far", steps[0], n_far), "sum_far")
    half = near_product([after(g00[0], message)] + g00[1:] + g01, "backward")
    own, *parts = rest_product(half, g10 + g11, "backward")
    others = from_row(parts)
    for step in steps[1:]:
        message = add(after(message, own), partner(message, "far", step, n_far), "sum_far")
    message = add(after(message, *others), swap(message, "mid"), "sum_mid")
    weight_grad, bias_grad, grad_features = call(
        functools.partial(last_kernel, 1.0 / nodes**0.5),
        "last",
        [shape(width, width, dtype=F32), shape(1, width, dtype=F32), shape(tile, width)],
        [message, swap(message, "core"), own] + others,
    )
    return output, grad_features, weight_grad, bias_grad.reshape(width)


def solution(mesh):
    n_loop, n_row = mesh.shape["loop"], mesh.shape["row"]
    every = ("far", "mid", "core", "row")
    fine = Mesh(mesh.devices.reshape(n_loop // 4, 2, 2, n_row), every)
    in_specs = (
        P(every, None),
        P(),
        P(),
        P(every, None),
        P(every, None, None),
        P(every),
        P(every),
    )
    out_specs = (P(every, None), P(every, None), P(), P())
    return jax.shard_map(
        functools.partial(shards, n_loop, n_row),
        mesh=fine,
        in_specs=in_specs,
        out_specs=out_specs,
        check_vma=False,
    )
```

```python
import functools
import math

import jax
import jax.numpy as jnp
from jax import lax
from jax.experimental import pallas as pl
from jax.experimental.pallas import tpu as pltpu
from jax.sharding import Mesh
from jax.sharding import PartitionSpec as P

BF16 = jnp.bfloat16
F32 = jnp.float32
VMEM = pl.BlockSpec(memory_space=pltpu.VMEM)
SMEM = pl.BlockSpec(memory_space=pltpu.SMEM)
MIB = 1024 * 1024
PAD = 16


def partner(x, axis, mask, n):
    return lax.ppermute(x, axis, [(i, i ^ mask) for i in range(n)])


def swap(x, axis):
    return partner(x, axis, 1, 2)


def after(x, *others):
    return lax.optimization_barrier((x,) + others)[0]


def shape(*dims, dtype=BF16):
    return jax.ShapeDtypeStruct(dims, dtype)


def dot(a, b, contract=((1,), (0,))):
    return lax.dot_general(a, b, (contract, ((), ())), preferred_element_type=F32)


def sigmoid(x):
    return 0.5 * jnp.tanh(0.5 * x) + 0.5


def far_masks(n_far):
    return [1 << k for k in reversed(range(n_far.bit_length() - 1))]


def far_place(mask, n_far):
    place = 0
    for k, step in enumerate(far_masks(n_far)):
        place = place + jnp.where(jnp.bitwise_and(mask, step) > 0, 1 << k, 0)
    return place


def expand_kernel(
    n_loop, n_row, tile, rows_hbm, counts_hbm, tiles_hbm, f_hbm, c_hbm, w_hbm, b_hbm,
    out_ref, f_out, c_out, w_out, b_out, rows_ref, counts_ref, tiles_ref, sems,
):
    copies = [
        pltpu.make_async_copy(source, target, sems.at[k])
        for k, (source, target) in enumerate(
            (
                (rows_hbm, rows_ref),
                (counts_hbm, counts_ref),
                (tiles_hbm, tiles_ref),
                (f_hbm, f_out),
                (c_hbm, c_out),
                (w_hbm, w_out),
                (b_hbm, b_out),
            )
        )
    ]
    for copy in copies:
        copy.start()
    n_far = n_loop // 4
    my_row, my_far = lax.axis_index("row"), lax.axis_index("far")
    my_near = 2 * lax.axis_index("mid") + lax.axis_index("core")
    for copy in copies:
        copy.wait()

    def body(j, carry):
        near = jnp.bitwise_xor(lax.rem(j, 4), my_near)
        column = near * n_far + far_place(jnp.bitwise_xor(lax.div(j, 4), my_far), n_far)
        for s in range(n_row):
            slot = j * n_row + s
            place = jnp.bitwise_xor(rows_ref[slot], my_row)
            value = tiles_ref[slot]
            value = jnp.where(s < counts_ref[j], value, jnp.zeros_like(value))
            out_ref[
                pl.ds(pl.multiple_of(place * tile, tile), tile),
                pl.ds(pl.multiple_of(column * tile, tile), tile),
            ] = value
        return carry

    lax.fori_loop(0, n_loop, body, 0)


def product_rows(a_ref, first, block_refs, rows):
    step = a_ref.shape[1] // (2 * len(block_refs))
    x = jnp.concatenate([ref[:step, :] for ref in block_refs], axis=0)
    return dot(a_ref[rows, first : first + x.shape[0]], x)


def pack_kernel(*refs):
    tile = refs[-1].shape[0] // (len(refs) - 1)
    for k, ref in enumerate(refs[:-1]):
        refs[-1][k * tile : (k + 1) * tile, :] = ref[:tile, :]


def near_kernel(tile, n_row, a_ref, *refs):
    block_refs, out_ref = refs[:-1], refs[-1]
    step = min(2, n_row) * tile
    for at in range(0, n_row * tile, step):
        rows = slice(at, at + step)
        out_ref[rows, :] = product_rows(a_ref, 0, block_refs, rows)


def output_kernel(w_ref, b_ref, h_ref, out_ref):
    preact = dot(h_ref[...], w_ref[...]) + b_ref[...]
    out_ref[...] = (preact * sigmoid(preact)).astype(BF16)


def rest_kernel(tile, n_row, n_blocks, a_ref, half_ref, *refs):
    block_refs, own_ref, send_refs = refs[:n_blocks], refs[n_blocks], refs[n_blocks + 1 :]
    first = a_ref.shape[1] // 2
    step = min(2, n_row)
    for q in range(0, n_row, step):
        rows = slice(q * tile, (q + step) * tile)
        total = half_ref[rows, :] + product_rows(a_ref, first, block_refs, rows)
        for k in range(step):
            part = total[k * tile : (k + 1) * tile, :]
            if q + k == 0:
                own_ref[...] = part
            else:
                send_refs[q + k - 1][...] = part.astype(BF16)


def sum_kernel(own_ref, *refs):
    part_refs, out_ref = refs[:-1], refs[-1]
    total = own_ref[...]
    for ref in part_refs:
        total = total + ref[...].astype(F32)
    out_ref[...] = total.astype(BF16)


def write_message(ref, grad_w, bias):
    rows, width = grad_w.shape
    ref[:rows, :] = grad_w.astype(BF16)
    high = bias.astype(BF16).astype(F32)
    row = lax.broadcasted_iota(jnp.int32, (PAD, width), 0)
    low = jnp.broadcast_to(bias - high, (PAD, width))
    high = jnp.broadcast_to(high, (PAD, width))
    ref[rows:, :] = jnp.where(row == 0, high, jnp.where(row == 1, low, 0.0)).astype(BF16)


def read_message(ref):
    rows = ref.shape[0] - PAD
    tail = ref[rows:, :].astype(F32)
    return ref[:rows, :].astype(F32), tail[0:1, :] + tail[1:2, :]


def grads_kernel(w_ref, b_ref, h_ref, c_ref, gh_ref, keep_ref, send_ref, sum_ref):
    half_rows = keep_ref.shape[0] - PAD
    hidden = h_ref[...]
    preact = dot(hidden, w_ref[...]) + b_ref[...]
    sig = sigmoid(preact)
    grad_z = c_ref[...].astype(F32) * sig * (1.0 + preact * (1.0 - sig))
    half = grad_z.astype(BF16)
    tile, width = h_ref.shape
    gh_ref[:tile, :] = dot(half, w_ref[...], ((1,), (1,))).astype(BF16)
    gh_ref[tile:, :] = jnp.zeros((gh_ref.shape[0] - tile, width), BF16)
    sum_ref[...] = dot(hidden, half, ((0,), (0,)))
    bias = jnp.sum(grad_z, axis=0, keepdims=True)
    core = lax.axis_index("core")
    for at, ref in ((core, keep_ref), (1 - core, send_ref)):
        rows = pl.ds(pl.multiple_of(at * half_rows, half_rows), half_rows)
        write_message(ref, sum_ref[rows, :], bias)


def message_kernel(own_ref, other_ref, out_ref):
    own_w, own_b = read_message(own_ref)
    other_w, other_b = read_message(other_ref)
    write_message(out_ref, own_w + other_w, own_b + other_b)


def halves_kernel(own_ref, other_ref, out_ref):
    half = own_ref.shape[0] - PAD
    core = lax.axis_index("core")
    out_ref[pl.ds(pl.multiple_of(core * half, half), half), :] = own_ref[:half, :]
    out_ref[pl.ds(pl.multiple_of((1 - core) * half, half), half), :] = other_ref[:half, :]
    out_ref[2 * half :, :] = own_ref[half:, :]


def last_kernel(factor, near_ref, far_ref, *refs):
    weight_ref, bias_ref, features_ref = refs[-3:]
    sum_kernel(*refs[:-3], features_ref)
    near_w, near_b = read_message(near_ref)
    far_w, far_b = read_message(far_ref)
    weight_ref[...] = (near_w + far_w) * factor
    bias_ref[...] = (near_b + far_b) * factor


def call(kernel, name, outs, operands, scratch=(), specs=None, flops=0):
    size = sum(o.size * o.dtype.itemsize for o in list(operands) + list(outs))
    held = size + sum(
        math.prod(s.shape) * s.dtype.itemsize for s in scratch if hasattr(s.dtype, "itemsize")
    )
    return pl.pallas_call(
        kernel,
        name=name,
        out_shape=outs,
        in_specs=specs or [VMEM] * len(operands),
        out_specs=[VMEM] * len(outs),
        scratch_shapes=scratch,
        cost_estimate=pl.CostEstimate(flops=flops, bytes_accessed=size, transcendentals=0),
        compiler_params=pltpu.CompilerParams(vmem_limit_bytes=2 * held + 4 * MIB),
    )(*operands)


def shards(n_loop, n_row, features, weight, bias_vector, cotangent, tile_values, tile_rows, counts):
    tile, width = features.shape
    n_far = n_loop // 4
    nodes = tile * n_loop * n_row
    rows = n_row * tile
    flops = rows * n_loop * tile * width

    steps = far_masks(n_far)

    def pack(*blocks):
        return call(pack_kernel, "pack", [shape(2 * tile, width)], blocks)[0]

    def far_chunks(pair):
        chunks = [pair]
        for step in steps[1:]:
            chunks = chunks + [partner(chunk, "far", step, n_far) for chunk in chunks]
        return chunks

    def near_product(near, name):
        return call(
            functools.partial(near_kernel, tile, n_row),
            name + "_near",
            [shape(rows, width, dtype=F32)],
            [adjacency] + near,
            flops=flops,
        )[0]

    def rest_product(half, rest, name):
        return call(
            functools.partial(rest_kernel, tile, n_row, len(rest)),
            name + "_rest",
            [shape(tile, width, dtype=F32)] + [shape(tile, width)] * (n_row - 1),
            [adjacency, half] + rest,
            flops=flops,
        )

    def from_row(parts):
        return [partner(part, "row", q + 1, n_row) for q, part in enumerate(parts)]

    other = partner(features, "far", steps[0], n_far)
    adjacency, features, cotangent, weight, bias_row = call(
        functools.partial(expand_kernel, n_loop, n_row, tile),
        "expand",
        [
            shape(rows, n_loop * tile),
            shape(tile, width),
            shape(tile, width),
            shape(width, width),
            shape(1, width, dtype=F32),
        ],
        [
            pltpu.with_memory_space_constraint(x, pltpu.HBM)
            for x in (
                tile_rows, counts, tile_values, features, cotangent, weight,
                bias_vector.reshape(1, width),
            )
        ],
        scratch=[
            pltpu.SMEM(tile_rows.shape, jnp.int32),
            pltpu.SMEM(counts.shape, jnp.int32),
            pltpu.VMEM(tile_values.shape, BF16),
            pltpu.SemaphoreType.DMA((7,)),
        ],
        specs=[pl.BlockSpec(memory_space=pltpu.HBM)] * 7,
    )
    f00 = far_chunks(pack(features, other))
    f10 = [swap(chunk, "mid") for chunk in f00]
    f01 = [swap(chunk, "core") for chunk in f00]
    f11 = [swap(chunk, "core") for chunk in f10]
    half = near_product(f00 + f01, "forward")
    own, *parts = rest_product(half, f10 + f11, "forward")
    (hidden,) = call(sum_kernel, "hidden", [shape(tile, width)], [own] + from_row(parts))

    message_shape = shape(width // 2 + PAD, width)
    grad_hidden, message, send = call(
        grads_kernel,
        "grads",
        [shape(tile + 2 * PAD, width), message_shape, message_shape],
        [weight, bias_row, hidden, cotangent],
        scratch=[pltpu.VMEM((width, width), F32)],
        flops=6 * tile * width * width,
    )
    (output,) = call(
        output_kernel, "output", [shape(tile, width)], [weight, bias_row, hidden]
    )

    def add(message, other, name):
        return call(message_kernel, name, [message_shape], [message, other])[0]

    message = add(message, swap(send, "core"), "sum_core")
    bit = 1
    while bit < n_row:
        message = add(message, partner(message, "row", bit, n_row), "sum_row")
        bit *= 2
    other = after(partner(grad_hidden, "far", steps[0], n_far), message, output)
    g00 = far_chunks(pack(grad_hidden, other))
    message = add(message, partner(message, "far", steps[0], n_far), "sum_far")
    g10 = [swap(chunk, "mid") for chunk in g00[:1] + [after(c, message) for c in g00[1:]]]
    g01 = [swap(chunk, "core") for chunk in g00]
    for step in steps[1:]:
        message = add(message, partner(message, "far", step, n_far), "sum_far")
    g11 = [swap(chunk, "core") for chunk in g10[:-1] + [after(g10[-1], message)]]
    half = near_product(g00 + g01, "backward")
    own, *parts = rest_product(half, g10 + g11, "backward")
    others = from_row(parts)
    (message,) = call(
        halves_kernel,
        "halves",
        [shape(width + PAD, width)],
        [message, swap(message, "core")],
    )
    message = after(message, own)
    weight_grad, bias_grad, grad_features = call(
        functools.partial(last_kernel, 1.0 / nodes**0.5),
        "last",
        [shape(width, width, dtype=F32), shape(1, width, dtype=F32), shape(tile, width)],
        [message, swap(message, "mid"), own] + others,
    )
    return output, grad_features, weight_grad, bias_grad.reshape(width)


def solution(mesh):
    n_loop, n_row = mesh.shape["loop"], mesh.shape["row"]
    every = ("far", "mid", "core", "row")
    fine = Mesh(mesh.devices.reshape(n_loop // 4, 2, 2, n_row), every)
    in_specs = (
        P(every, None),
        P(),
        P(),
        P(every, None),
        P(every, None, None),
        P(every),
        P(every),
    )
    out_specs = (P(every, None), P(every, None), P(), P())
    return jax.shard_map(
        functools.partial(shards, n_loop, n_row),
        mesh=fine,
        in_specs=in_specs,
        out_specs=out_specs,
        check_vma=False,
    )
```

```python
import functools
import math

import jax
import jax.numpy as jnp
from jax import lax
from jax.experimental import pallas as pl
from jax.experimental.pallas import tpu as pltpu
from jax.sharding import Mesh
from jax.sharding import PartitionSpec as P

BF16 = jnp.bfloat16
F32 = jnp.float32
VMEM = pl.BlockSpec(memory_space=pltpu.VMEM)
SMEM = pl.BlockSpec(memory_space=pltpu.SMEM)
MIB = 1024 * 1024
PAD = 16


def partner(x, axis, mask, n):
    return lax.ppermute(x, axis, [(i, i ^ mask) for i in range(n)])


def swap(x, axis):
    return partner(x, axis, 1, 2)


def after(x, *others):
    return lax.optimization_barrier((x,) + others)[0]


def shape(*dims, dtype=BF16):
    return jax.ShapeDtypeStruct(dims, dtype)


def dot(a, b, contract=((1,), (0,))):
    return lax.dot_general(a, b, (contract, ((), ())), preferred_element_type=F32)


def sigmoid(x):
    return 0.5 * jnp.tanh(0.5 * x) + 0.5


def far_masks(n_far):
    return [1 << k for k in reversed(range(n_far.bit_length() - 1))]


def far_place(mask, n_far):
    place = 0
    for k, step in enumerate(far_masks(n_far)):
        place = place + jnp.where(jnp.bitwise_and(mask, step) > 0, 1 << k, 0)
    return place


def expand_kernel(
    n_loop, n_row, tile, rows_hbm, counts_hbm, tiles_hbm, f_hbm, c_hbm, w_hbm, b_hbm,
    out_ref, f_out, c_out, w_out, b_out, rows_ref, counts_ref, tiles_ref, sems,
):
    copies = [
        pltpu.make_async_copy(source, target, sems.at[k])
        for k, (source, target) in enumerate(
            (
                (rows_hbm, rows_ref),
                (counts_hbm, counts_ref),
                (tiles_hbm, tiles_ref),
                (f_hbm, f_out),
                (c_hbm, c_out),
                (w_hbm, w_out),
                (b_hbm, b_out),
            )
        )
    ]
    for copy in copies:
        copy.start()
    n_far = n_loop // 4
    my_row, my_far = lax.axis_index("row"), lax.axis_index("far")
    my_near = 2 * lax.axis_index("mid") + lax.axis_index("core")
    for copy in copies:
        copy.wait()

    def body(j, carry):
        near = jnp.bitwise_xor(lax.rem(j, 4), my_near)
        column = near * n_far + far_place(jnp.bitwise_xor(lax.div(j, 4), my_far), n_far)
        for s in range(n_row):
            slot = j * n_row + s
            place = jnp.bitwise_xor(rows_ref[slot], my_row)
            value = tiles_ref[slot]
            value = jnp.where(s < counts_ref[j], value, jnp.zeros_like(value))
            out_ref[
                pl.ds(pl.multiple_of(place * tile, tile), tile),
                pl.ds(pl.multiple_of(column * tile, tile), tile),
            ] = value
        return carry

    lax.fori_loop(0, n_loop, body, 0)


def pack_message_kernel(a_ref, b_ref, message_ref, pair_ref, packed_ref):
    rows = pair_ref.shape[0]
    pack_kernel(a_ref, b_ref, pair_ref)
    packed_ref[:rows, :] = pair_ref[...]
    packed_ref[rows:, :] = message_ref[...]


def unpack_message_kernel(message_ref, packed_ref, pair_ref, sum_ref):
    rows = pair_ref.shape[0]
    pair_ref[...] = packed_ref[:rows, :]
    message_kernel(message_ref, packed_ref.at[rows:, :], sum_ref)


def product_rows(a_ref, first, block_refs, rows):
    step = a_ref.shape[1] // (2 * len(block_refs))
    x = jnp.concatenate([ref[:step, :] for ref in block_refs], axis=0)
    return dot(a_ref[rows, first : first + x.shape[0]], x)


def pack_kernel(*refs):
    tile = refs[-1].shape[0] // (len(refs) - 1)
    for k, ref in enumerate(refs[:-1]):
        refs[-1][k * tile : (k + 1) * tile, :] = ref[:tile, :]


def near_kernel(tile, n_row, a_ref, *refs):
    block_refs, out_ref = refs[:-1], refs[-1]
    step = min(2, n_row) * tile
    for at in range(0, n_row * tile, step):
        rows = slice(at, at + step)
        out_ref[rows, :] = product_rows(a_ref, 0, block_refs, rows)


def output_kernel(w_ref, b_ref, h_ref, out_ref):
    preact = dot(h_ref[...], w_ref[...]) + b_ref[...]
    out_ref[...] = (preact * sigmoid(preact)).astype(BF16)


def rest_kernel(tile, n_row, n_blocks, a_ref, half_ref, *refs):
    block_refs, own_ref, send_refs = refs[:n_blocks], refs[n_blocks], refs[n_blocks + 1 :]
    first = a_ref.shape[1] // 2
    step = min(2, n_row)
    for q in range(0, n_row, step):
        rows = slice(q * tile, (q + step) * tile)
        total = half_ref[rows, :] + product_rows(a_ref, first, block_refs, rows)
        for k in range(step):
            part = total[k * tile : (k + 1) * tile, :]
            if q + k == 0:
                own_ref[...] = part
            else:
                send_refs[q + k - 1][...] = part.astype(BF16)


def sum_kernel(own_ref, *refs):
    part_refs, out_ref = refs[:-1], refs[-1]
    total = own_ref[...]
    for ref in part_refs:
        total = total + ref[...].astype(F32)
    out_ref[...] = total.astype(BF16)


def write_message(ref, grad_w, bias):
    rows, width = grad_w.shape
    ref[:rows, :] = grad_w.astype(BF16)
    high = bias.astype(BF16).astype(F32)
    row = lax.broadcasted_iota(jnp.int32, (PAD, width), 0)
    low = jnp.broadcast_to(bias - high, (PAD, width))
    high = jnp.broadcast_to(high, (PAD, width))
    ref[rows:, :] = jnp.where(row == 0, high, jnp.where(row == 1, low, 0.0)).astype(BF16)


def read_message(ref):
    rows = ref.shape[0] - PAD
    tail = ref[rows:, :].astype(F32)
    return ref[:rows, :].astype(F32), tail[0:1, :] + tail[1:2, :]


def grads_kernel(w_ref, b_ref, h_ref, c_ref, gh_ref, keep_ref, send_ref, sum_ref):
    half_rows = keep_ref.shape[0] - PAD
    hidden = h_ref[...]
    preact = dot(hidden, w_ref[...]) + b_ref[...]
    sig = sigmoid(preact)
    grad_z = c_ref[...].astype(F32) * sig * (1.0 + preact * (1.0 - sig))
    half = grad_z.astype(BF16)
    tile, width = h_ref.shape
    gh_ref[:tile, :] = dot(half, w_ref[...], ((1,), (1,))).astype(BF16)
    gh_ref[tile:, :] = jnp.zeros((gh_ref.shape[0] - tile, width), BF16)
    sum_ref[...] = dot(hidden, half, ((0,), (0,)))
    bias = jnp.sum(grad_z, axis=0, keepdims=True)
    core = lax.axis_index("core")
    for at, ref in ((core, keep_ref), (1 - core, send_ref)):
        rows = pl.ds(pl.multiple_of(at * half_rows, half_rows), half_rows)
        write_message(ref, sum_ref[rows, :], bias)


def message_kernel(own_ref, other_ref, out_ref):
    own_w, own_b = read_message(own_ref)
    other_w, other_b = read_message(other_ref)
    write_message(out_ref, own_w + other_w, own_b + other_b)


def halves_kernel(own_ref, other_ref, out_ref):
    half = own_ref.shape[0] - PAD
    core = lax.axis_index("core")
    out_ref[pl.ds(pl.multiple_of(core * half, half), half), :] = own_ref[:half, :]
    out_ref[pl.ds(pl.multiple_of((1 - core) * half, half), half), :] = other_ref[:half, :]
    out_ref[2 * half :, :] = own_ref[half:, :]


def last_kernel(factor, near_ref, far_ref, *refs):
    weight_ref, bias_ref, features_ref = refs[-3:]
    sum_kernel(*refs[:-3], features_ref)
    near_w, near_b = read_message(near_ref)
    far_w, far_b = read_message(far_ref)
    weight_ref[...] = (near_w + far_w) * factor
    bias_ref[...] = (near_b + far_b) * factor


def call(kernel, name, outs, operands, scratch=(), specs=None, flops=0):
    size = sum(o.size * o.dtype.itemsize for o in list(operands) + list(outs))
    held = size + sum(
        math.prod(s.shape) * s.dtype.itemsize for s in scratch if hasattr(s.dtype, "itemsize")
    )
    return pl.pallas_call(
        kernel,
        name=name,
        out_shape=outs,
        in_specs=specs or [VMEM] * len(operands),
        out_specs=[VMEM] * len(outs),
        scratch_shapes=scratch,
        cost_estimate=pl.CostEstimate(flops=flops, bytes_accessed=size, transcendentals=0),
        compiler_params=pltpu.CompilerParams(vmem_limit_bytes=2 * held + 4 * MIB),
    )(*operands)


def shards(n_loop, n_row, features, weight, bias_vector, cotangent, tile_values, tile_rows, counts):
    tile, width = features.shape
    n_far = n_loop // 4
    nodes = tile * n_loop * n_row
    rows = n_row * tile
    flops = rows * n_loop * tile * width

    steps = far_masks(n_far)

    def pack(*blocks):
        return call(pack_kernel, "pack", [shape(2 * tile, width)], blocks)[0]

    def far_chunks(pair):
        chunks = [pair]
        for step in steps[1:]:
            chunks = chunks + [partner(chunk, "far", step, n_far) for chunk in chunks]
        return chunks

    def near_product(near, name):
        return call(
            functools.partial(near_kernel, tile, n_row),
            name + "_near",
            [shape(rows, width, dtype=F32)],
            [adjacency] + near,
            flops=flops,
        )[0]

    def rest_product(half, rest, name):
        return call(
            functools.partial(rest_kernel, tile, n_row, len(rest)),
            name + "_rest",
            [shape(tile, width, dtype=F32)] + [shape(tile, width)] * (n_row - 1),
            [adjacency, half] + rest,
            flops=flops,
        )

    def from_row(parts):
        return [partner(part, "row", q + 1, n_row) for q, part in enumerate(parts)]

    other = partner(features, "far", steps[0], n_far)
    adjacency, features, cotangent, weight, bias_row = call(
        functools.partial(expand_kernel, n_loop, n_row, tile),
        "expand",
        [
            shape(rows, n_loop * tile),
            shape(tile, width),
            shape(tile, width),
            shape(width, width),
            shape(1, width, dtype=F32),
        ],
        [
            pltpu.with_memory_space_constraint(x, pltpu.HBM)
            for x in (
                tile_rows, counts, tile_values, features, cotangent, weight,
                bias_vector.reshape(1, width),
            )
        ],
        scratch=[
            pltpu.SMEM(tile_rows.shape, jnp.int32),
            pltpu.SMEM(counts.shape, jnp.int32),
            pltpu.VMEM(tile_values.shape, BF16),
            pltpu.SemaphoreType.DMA((7,)),
        ],
        specs=[pl.BlockSpec(memory_space=pltpu.HBM)] * 7,
    )
    f00 = far_chunks(pack(features, other))
    f10 = [swap(chunk, "mid") for chunk in f00]
    f01 = [swap(chunk, "core") for chunk in f00]
    f11 = [swap(chunk, "core") for chunk in f10]
    half = near_product(f00 + f01, "forward")
    own, *parts = rest_product(half, f10 + f11, "forward")
    (hidden,) = call(sum_kernel, "hidden", [shape(tile, width)], [own] + from_row(parts))

    message_shape = shape(width // 2 + PAD, width)
    grad_hidden, message, send = call(
        grads_kernel,
        "grads",
        [shape(tile + 2 * PAD, width), message_shape, message_shape],
        [weight, bias_row, hidden, cotangent],
        scratch=[pltpu.VMEM((width, width), F32)],
        flops=6 * tile * width * width,
    )
    (output,) = call(
        output_kernel, "output", [shape(tile, width)], [weight, bias_row, hidden]
    )

    def add(message, other, name):
        return call(message_kernel, name, [message_shape], [message, other])[0]

    message = add(message, swap(send, "core"), "sum_core")
    bit = 1
    while bit < n_row:
        message = add(message, partner(message, "row", bit, n_row), "sum_row")
        bit *= 2
    other = after(partner(grad_hidden, "far", steps[0], n_far), message, output)
    pair_shape = shape(2 * tile, width)
    pair, packed = call(
        pack_message_kernel,
        "pack_message",
        [pair_shape, shape(2 * tile + message_shape.shape[0], width)],
        [grad_hidden, other, message],
    )
    chunk, message = call(
        unpack_message_kernel,
        "unpack_message",
        [pair_shape, message_shape],
        [message, partner(packed, "far", steps[1], n_far)],
    )
    g00 = [pair, chunk]
    for step in steps[2:]:
        g00 = g00 + [partner(chunk, "far", step, n_far) for chunk in g00]
    g10 = [swap(chunk, "mid") for chunk in g00]
    g01 = [swap(chunk, "core") for chunk in g00]
    g11 = [swap(chunk, "core") for chunk in g10]
    for step in steps[:1] + steps[2:]:
        message = add(message, partner(message, "far", step, n_far), "sum_far")
    half = near_product([after(g00[0], message)] + g00[1:] + g01, "backward")
    own, *parts = rest_product(half, g10 + g11, "backward")
    others = from_row(parts)
    (message,) = call(
        halves_kernel,
        "halves",
        [shape(width + PAD, width)],
        [message, swap(message, "core")],
    )
    message = after(message, own)
    weight_grad, bias_grad, grad_features = call(
        functools.partial(last_kernel, 1.0 / nodes**0.5),
        "last",
        [shape(width, width, dtype=F32), shape(1, width, dtype=F32), shape(tile, width)],
        [message, swap(message, "mid"), own] + others,
    )
    return output, grad_features, weight_grad, bias_grad.reshape(width)


def solution(mesh):
    n_loop, n_row = mesh.shape["loop"], mesh.shape["row"]
    every = ("far", "mid", "core", "row")
    fine = Mesh(mesh.devices.reshape(n_loop // 4, 2, 2, n_row), every)
    in_specs = (
        P(every, None),
        P(),
        P(),
        P(every, None),
        P(every, None, None),
        P(every),
        P(every),
    )
    out_specs = (P(every, None), P(every, None), P(), P())
    return jax.shard_map(
        functools.partial(shards, n_loop, n_row),
        mesh=fine,
        in_specs=in_specs,
        out_specs=out_specs,
        check_vma=False,
    )
```

```python
import functools
import math

import jax
import jax.numpy as jnp
from jax import lax
from jax.experimental import pallas as pl
from jax.experimental.pallas import tpu as pltpu
from jax.sharding import Mesh
from jax.sharding import PartitionSpec as P

BF16 = jnp.bfloat16
F32 = jnp.float32
VMEM = pl.BlockSpec(memory_space=pltpu.VMEM)
SMEM = pl.BlockSpec(memory_space=pltpu.SMEM)
MIB = 1024 * 1024
PAD = 16


def partner(x, axis, mask, n):
    return lax.ppermute(x, axis, [(i, i ^ mask) for i in range(n)])


def swap(x, axis):
    return partner(x, axis, 1, 2)


def after(x, *others):
    return lax.optimization_barrier((x,) + others)[0]


def shape(*dims, dtype=BF16):
    return jax.ShapeDtypeStruct(dims, dtype)


def dot(a, b, contract=((1,), (0,))):
    return lax.dot_general(a, b, (contract, ((), ())), preferred_element_type=F32)


def sigmoid(x):
    return 0.5 * jnp.tanh(0.5 * x) + 0.5


def tree_sum(parts):
    while len(parts) > 1:
        parts = [parts[i] + parts[i + 1] for i in range(0, len(parts), 2)]
    return parts[0]


def far_masks(n_far):
    return [1 << k for k in reversed(range(n_far.bit_length() - 1))]


def far_place(mask, n_far):
    place = 0
    for k, step in enumerate(far_masks(n_far)):
        place = place + jnp.where(jnp.bitwise_and(mask, step) > 0, 1 << k, 0)
    return place


def expand_kernel(
    n_loop, n_row, tile, rows_hbm, counts_hbm, tiles_hbm, f_hbm, c_hbm, out_ref, f_out, c_out,
    rows_ref, counts_ref, tiles_ref, sems,
):
    copies = [
        pltpu.make_async_copy(source, target, sems.at[k])
        for k, (source, target) in enumerate(
            (
                (rows_hbm, rows_ref),
                (counts_hbm, counts_ref),
                (tiles_hbm, tiles_ref),
                (f_hbm, f_out),
                (c_hbm, c_out),
            )
        )
    ]
    for copy in copies:
        copy.start()
    n_far = n_loop // 4
    my_row, my_far = lax.axis_index("row"), lax.axis_index("far")
    my_near = 2 * lax.axis_index("mid") + lax.axis_index("core")
    for copy in copies:
        copy.wait()

    def body(j, carry):
        near = jnp.bitwise_xor(lax.rem(j, 4), my_near)
        column = near * n_far + far_place(jnp.bitwise_xor(lax.div(j, 4), my_far), n_far)
        for s in range(n_row):
            slot = j * n_row + s
            place = jnp.bitwise_xor(rows_ref[slot], my_row)
            value = tiles_ref[slot]
            value = jnp.where(s < counts_ref[j], value, jnp.zeros_like(value))
            out_ref[
                pl.ds(pl.multiple_of(place * tile, tile), tile),
                pl.ds(pl.multiple_of(column * tile, tile), tile),
            ] = value
        return carry

    lax.fori_loop(0, n_loop, body, 0)


def product_rows(a_ref, first, block_refs, rows):
    step = a_ref.shape[1] // (2 * len(block_refs))
    x = jnp.concatenate([ref[:step, :] for ref in block_refs], axis=0)
    return dot(a_ref[rows, first : first + x.shape[0]], x)


def pack_kernel(*refs):
    at = 0
    for ref in refs[:-1]:
        refs[-1][at : at + ref.shape[0], :] = ref[...]
        at += ref.shape[0]


def near_kernel(tile, n_row, a_ref, *refs):
    block_refs, out_ref = refs[:-1], refs[-1]
    step = min(2, n_row) * tile
    for at in range(0, n_row * tile, step):
        rows = slice(at, at + step)
        out_ref[rows, :] = product_rows(a_ref, 0, block_refs, rows)


def output_kernel(w_ref, b_ref, h_ref, out_ref):
    preact = dot(h_ref[...], w_ref[...]) + b_ref[...]
    out_ref[...] = (preact * sigmoid(preact)).astype(BF16)


def rest_kernel(tile, n_row, n_blocks, a_ref, half_ref, *refs):
    block_refs, own_ref, send_refs = refs[:n_blocks], refs[n_blocks], refs[n_blocks + 1 :]
    first = a_ref.shape[1] // 2
    step = min(2, n_row)
    for q in range(0, n_row, step):
        rows = slice(q * tile, (q + step) * tile)
        total = half_ref[rows, :] + product_rows(a_ref, first, block_refs, rows)
        for k in range(step):
            part = total[k * tile : (k + 1) * tile, :]
            if q + k == 0:
                own_ref[...] = part
            else:
                send_refs[q + k - 1][...] = part.astype(BF16)


def sum_kernel(own_ref, *refs):
    part_refs, out_ref = refs[:-1], refs[-1]
    total = own_ref[...]
    for ref in part_refs:
        total = total + ref[...].astype(F32)
    out_ref[...] = total.astype(BF16)


def chunk_grads(w_ref, b_ref, h_ref, c_refs, gh_ref):
    tile, width = h_ref.shape[0] // 2, h_ref.shape[1]
    weight_sums, bias_sums = [], []
    for k, (c_ref, half) in enumerate(c_refs):
        rows = slice(k * tile, (k + 1) * tile)
        hidden = h_ref[rows, :]
        preact = dot(hidden, w_ref[...]) + b_ref[...]
        sig = sigmoid(preact)
        cot = c_ref[half * tile : (half + 1) * tile, :].astype(F32)
        grad_z = cot * sig * (1.0 + preact * (1.0 - sig))
        half = grad_z.astype(BF16)
        gh_ref[rows, :] = dot(half, w_ref[...], ((1,), (1,))).astype(BF16)
        bias_sums.append(jnp.sum(grad_z.reshape(tile // 8, 8, width), axis=0))
        weight_sums.append(dot(hidden, half, ((0,), (0,))))
    return tree_sum(weight_sums), tree_sum(bias_sums)


def chunk_kernel(halves, w_ref, b_ref, h_ref, c0_ref, c1_ref, gh_ref, gw_ref, gb_ref):
    c_refs = list(zip((c0_ref, c1_ref), halves))
    gw_ref[...], gb_ref[...] = chunk_grads(w_ref, b_ref, h_ref, c_refs, gh_ref)


def write_message(ref, grad_w, bias):
    rows, width = grad_w.shape
    ref[:rows, :] = grad_w.astype(BF16)
    high = bias.astype(BF16).astype(F32)
    row = lax.broadcasted_iota(jnp.int32, (PAD, width), 0)
    low = jnp.broadcast_to(bias - high, (PAD, width))
    high = jnp.broadcast_to(high, (PAD, width))
    ref[rows:, :] = jnp.where(row == 0, high, jnp.where(row == 1, low, 0.0)).astype(BF16)


def read_message(ref):
    rows = ref.shape[0] - PAD
    tail = ref[rows:, :].astype(F32)
    return ref[:rows, :].astype(F32), tail[0:1, :] + tail[1:2, :]


def last_chunk_kernel(halves, n, w_ref, b_ref, h_ref, c0_ref, c1_ref, *refs):
    gw_refs, gb_refs = refs[:n], refs[n : 2 * n]
    gh_ref, both_ref, keep_ref, sum_ref = refs[2 * n :]
    half = keep_ref.shape[0] - PAD
    c_refs = list(zip((c0_ref, c1_ref), halves))
    grad_w, grad_b = chunk_grads(w_ref, b_ref, h_ref, c_refs, gh_ref)
    sum_ref[...] = tree_sum([ref[...] for ref in gw_refs] + [grad_w])
    grad_b = tree_sum([ref[...] for ref in gb_refs] + [grad_b])
    bias = jnp.sum(grad_b, axis=0, keepdims=True)
    core = lax.axis_index("core")
    kept = sum_ref[pl.ds(pl.multiple_of(core * half, half), half), :]
    sent = sum_ref[pl.ds(pl.multiple_of((1 - core) * half, half), half), :]
    write_message(keep_ref, kept, bias)
    at = gh_ref.shape[0]
    both_ref[:at, :] = gh_ref[...]
    write_message(both_ref.at[at:, :], sent, bias)


def message_kernel(own_ref, other_ref, out_ref):
    own_w, own_b = read_message(own_ref)
    other_w, other_b = read_message(other_ref.at[other_ref.shape[0] - own_ref.shape[0] :, :])
    write_message(out_ref, own_w + other_w, own_b + other_b)


def halves_kernel(own_ref, other_ref, out_ref):
    half = own_ref.shape[0] - PAD
    core = lax.axis_index("core")
    out_ref[pl.ds(pl.multiple_of(core * half, half), half), :] = own_ref[:half, :]
    out_ref[pl.ds(pl.multiple_of((1 - core) * half, half), half), :] = other_ref[:half, :]
    out_ref[2 * half :, :] = own_ref[half:, :]


def last_kernel(factor, near_ref, far_ref, *refs):
    weight_ref, bias_ref, features_ref = refs[-3:]
    sum_kernel(*refs[:-3], features_ref)
    near_w, near_b = read_message(near_ref)
    far_w, far_b = read_message(far_ref)
    weight_ref[...] = (near_w + far_w) * factor
    bias_ref[...] = (near_b + far_b) * factor


def call(kernel, name, outs, operands, scratch=(), specs=None, flops=0):
    size = sum(o.size * o.dtype.itemsize for o in list(operands) + list(outs))
    held = size + sum(
        math.prod(s.shape) * s.dtype.itemsize for s in scratch if hasattr(s.dtype, "itemsize")
    )
    return pl.pallas_call(
        kernel,
        name=name,
        out_shape=outs,
        in_specs=specs or [VMEM] * len(operands),
        out_specs=[VMEM] * len(outs),
        scratch_shapes=scratch,
        cost_estimate=pl.CostEstimate(flops=flops, bytes_accessed=size, transcendentals=0),
        compiler_params=pltpu.CompilerParams(vmem_limit_bytes=2 * held + 4 * MIB),
    )(*operands)


def shards(n_loop, n_row, features, weight, bias_vector, cotangent, tile_values, tile_rows, counts):
    tile, width = features.shape
    n_far = n_loop // 4
    nodes = tile * n_loop * n_row
    rows = n_row * tile
    flops = rows * n_loop * tile * width

    steps = far_masks(n_far)

    def pack(*blocks):
        return call(pack_kernel, "pack", [shape(2 * tile, width)], blocks)[0]

    def far_partner(block, step):
        return partner(block, "far", step, n_far)

    def far_chunks(pair, steps):
        chunks = [pair]
        for step in steps[1:]:
            chunks = chunks + [partner(chunk, "far", step, n_far) for chunk in chunks]
        return chunks

    def near_product(near, name):
        return call(
            functools.partial(near_kernel, tile, n_row),
            name + "_near",
            [shape(rows, width, dtype=F32)],
            [adjacency] + near,
            flops=flops,
        )[0]

    def rest_product(half, rest, name):
        return call(
            functools.partial(rest_kernel, tile, n_row, len(rest)),
            name + "_rest",
            [shape(tile, width, dtype=F32)] + [shape(tile, width)] * (n_row - 1),
            [adjacency, half] + rest,
            flops=flops,
        )

    def from_row(parts):
        return [partner(part, "row", q + 1, n_row) for q, part in enumerate(parts)]

    cot_steps = steps[::-1]
    other, other_cot = far_partner(features, steps[0]), far_partner(cotangent, cot_steps[0])
    adjacency, features, cotangent = call(
        functools.partial(expand_kernel, n_loop, n_row, tile),
        "expand",
        [shape(rows, n_loop * tile), shape(tile, width), shape(tile, width)],
        [
            pltpu.with_memory_space_constraint(x, pltpu.HBM)
            for x in (tile_rows, counts, tile_values, features, cotangent)
        ],
        scratch=[
            pltpu.SMEM(tile_rows.shape, jnp.int32),
            pltpu.SMEM(counts.shape, jnp.int32),
            pltpu.VMEM(tile_values.shape, BF16),
            pltpu.SemaphoreType.DMA((5,)),
        ],
        specs=[pl.BlockSpec(memory_space=pltpu.HBM)] * 5,
    )
    f00 = far_chunks(after(pack(features, other), other_cot), steps)
    f10 = [swap(chunk, "mid") for chunk in f00]
    cots = far_chunks(pack(cotangent, other_cot), cot_steps)
    f01 = [swap(chunk, "core") for chunk in f00]
    f11 = [swap(chunk, "core") for chunk in f10[:-1] + [after(f10[-1], *cots)]]
    half = near_product(f00 + f01, "forward")
    own, *parts = rest_product(half, f10 + f11, "forward")
    others = from_row(parts)
    (hidden,) = call(sum_kernel, "hidden", [shape(tile, width)], [own] + others)

    bias_row = bias_vector.reshape(1, width)
    (output,) = call(
        output_kernel, "output", [shape(tile, width)], [weight, bias_row, hidden]
    )
    other, hidden = far_partner(hidden, steps[0]), after(hidden, output)
    hiddens = far_chunks(pack(hidden, other), steps)

    def chunk_cots(k):
        bits = len(steps)
        places = [int(f"{2 * k + b:0{bits}b}"[::-1], 2) for b in range(2)]
        return [cots[p // 2] for p in places], [p % 2 for p in places]

    chunk_flops = 2 * tile * 6 * width * width
    g00, weight_sums, bias_sums = [], [], []
    sums = [shape(width, width, dtype=F32), shape(8, width, dtype=F32)]
    for k, chunk in enumerate(hiddens[:-1]):
        chunk_cot, halves = chunk_cots(k)
        gh, weight_sum, bias_sum = call(
            functools.partial(chunk_kernel, halves),
            "chunk",
            [shape(2 * tile, width)] + sums,
            [weight, bias_row, chunk] + chunk_cot,
            flops=chunk_flops,
        )
        g00.append(gh)
        weight_sums.append(weight_sum)
        bias_sums.append(bias_sum)
    half_rows = width // 2 + PAD
    g01 = [swap(chunk, "core") for chunk in g00]
    g10 = [swap(chunk, "mid") for chunk in g00]
    chunk_cot, halves = chunk_cots(len(g00))
    gh, both, keep = call(
        functools.partial(last_chunk_kernel, halves, len(g00)),
        "last_chunk",
        [shape(2 * tile, width), shape(2 * tile + half_rows, width), shape(half_rows, width)],
        [weight, bias_row, hiddens[-1]] + chunk_cot + weight_sums + bias_sums,
        scratch=[pltpu.VMEM((width, width), F32)],
        flops=chunk_flops,
    )
    g00.append(gh)
    g01.append(swap(after(both, *g10), "core"))
    g10.append(swap(gh, "mid"))

    (message,) = call(message_kernel, "sum_core", [shape(half_rows, width)], [keep, g01[-1]])
    bit = 1
    while bit < n_row:
        (message,) = call(
            message_kernel,
            "sum_row",
            [shape(half_rows, width)],
            [message, partner(message, "row", bit, n_row)],
        )
        bit *= 2
    g11 = [swap(chunk, "core") for chunk in g10]
    half = near_product([after(g00[0], message)] + g00[1:] + g01, "backward")
    own, *parts = rest_product(half, g10 + g11, "backward")
    others = from_row(parts)
    (message,) = call(
        halves_kernel,
        "halves",
        [shape(width + PAD, width)],
        [message, swap(message, "core")],
    )
    message = after(message, own)
    messages = [message, swap(message, "mid")]
    weight_grad, bias_grad, grad_features = call(
        functools.partial(last_kernel, 1.0 / nodes**0.5),
        "last",
        [shape(width, width, dtype=F32), shape(1, width, dtype=F32), shape(tile, width)],
        messages + [own] + others,
    )
    return output, grad_features, weight_grad, bias_grad.reshape(width)


def solution(mesh):
    n_loop, n_row = mesh.shape["loop"], mesh.shape["row"]
    every = ("far", "mid", "core", "row")
    fine = Mesh(mesh.devices.reshape(n_loop // 4, 2, 2, n_row), every)
    in_specs = (
        P(every, None),
        P(),
        P(),
        P(every, None),
        P(every, None, None),
        P(every),
        P(every),
    )
    out_specs = (P(every, None), P(every, None), P(), P())
    return jax.shard_map(
        functools.partial(shards, n_loop, n_row),
        mesh=fine,
        in_specs=in_specs,
        out_specs=out_specs,
        check_vma=False,
    )
```

```python
import functools
import math

import jax
import jax.numpy as jnp
from jax import lax
from jax.experimental import pallas as pl
from jax.experimental.pallas import tpu as pltpu
from jax.sharding import Mesh
from jax.sharding import PartitionSpec as P

BF16 = jnp.bfloat16
F32 = jnp.float32
VMEM = pl.BlockSpec(memory_space=pltpu.VMEM)
SMEM = pl.BlockSpec(memory_space=pltpu.SMEM)
MIB = 1024 * 1024
PAD = 16


def partner(x, axis, mask, n):
    return lax.ppermute(x, axis, [(i, i ^ mask) for i in range(n)])


def swap(x, axis):
    return partner(x, axis, 1, 2)


def after(x, *others):
    return lax.optimization_barrier((x,) + others)[0]


def shape(*dims, dtype=BF16):
    return jax.ShapeDtypeStruct(dims, dtype)


def dot(a, b, contract=((1,), (0,))):
    return lax.dot_general(a, b, (contract, ((), ())), preferred_element_type=F32)


def sigmoid(x):
    return 0.5 * jnp.tanh(0.5 * x) + 0.5


def tree_sum(parts):
    while len(parts) > 1:
        parts = [parts[i] + parts[i + 1] for i in range(0, len(parts), 2)]
    return parts[0]


def far_masks(n_far):
    return [1 << k for k in reversed(range(n_far.bit_length() - 1))]


def far_place(mask, n_far):
    place = 0
    for k, step in enumerate(far_masks(n_far)):
        place = place + jnp.where(jnp.bitwise_and(mask, step) > 0, 1 << k, 0)
    return place


def expand_kernel(
    n_loop, n_row, tile, rows_hbm, counts_hbm, tiles_hbm, f_hbm, c_hbm, out_ref, f_out, c_out,
    rows_ref, counts_ref, tiles_ref, sems,
):
    copies = [
        pltpu.make_async_copy(source, target, sems.at[k])
        for k, (source, target) in enumerate(
            (
                (rows_hbm, rows_ref),
                (counts_hbm, counts_ref),
                (tiles_hbm, tiles_ref),
                (f_hbm, f_out),
                (c_hbm, c_out),
            )
        )
    ]
    for copy in copies:
        copy.start()
    n_far = n_loop // 4
    my_row, my_far = lax.axis_index("row"), lax.axis_index("far")
    my_near = 2 * lax.axis_index("mid") + lax.axis_index("core")
    for copy in copies:
        copy.wait()

    def body(j, carry):
        near = jnp.bitwise_xor(lax.rem(j, 4), my_near)
        column = near * n_far + far_place(jnp.bitwise_xor(lax.div(j, 4), my_far), n_far)
        for s in range(n_row):
            slot = j * n_row + s
            place = jnp.bitwise_xor(rows_ref[slot], my_row)
            value = tiles_ref[slot]
            value = jnp.where(s < counts_ref[j], value, jnp.zeros_like(value))
            out_ref[
                pl.ds(pl.multiple_of(place * tile, tile), tile),
                pl.ds(pl.multiple_of(column * tile, tile), tile),
            ] = value
        return carry

    lax.fori_loop(0, n_loop, body, 0)


def product_rows(a_ref, first, block_refs, rows):
    step = a_ref.shape[1] // (2 * len(block_refs))
    x = jnp.concatenate([ref[:step, :] for ref in block_refs], axis=0)
    return dot(a_ref[rows, first : first + x.shape[0]], x)


def pack_kernel(*refs):
    at = 0
    for ref in refs[:-1]:
        refs[-1][at : at + ref.shape[0], :] = ref[...]
        at += ref.shape[0]


def near_kernel(tile, n_row, a_ref, *refs):
    block_refs, out_ref = refs[:-1], refs[-1]
    step = min(2, n_row) * tile
    for at in range(0, n_row * tile, step):
        rows = slice(at, at + step)
        out_ref[rows, :] = product_rows(a_ref, 0, block_refs, rows)


def output_kernel(w_ref, b_ref, h_ref, out_ref):
    preact = dot(h_ref[...], w_ref[...]) + b_ref[...]
    out_ref[...] = (preact * sigmoid(preact)).astype(BF16)


def rest_kernel(tile, n_row, n_blocks, a_ref, half_ref, *refs):
    block_refs, own_ref, send_refs = refs[:n_blocks], refs[n_blocks], refs[n_blocks + 1 :]
    first = a_ref.shape[1] // 2
    step = min(2, n_row)
    for q in range(0, n_row, step):
        rows = slice(q * tile, (q + step) * tile)
        total = half_ref[rows, :] + product_rows(a_ref, first, block_refs, rows)
        for k in range(step):
            part = total[k * tile : (k + 1) * tile, :]
            if q + k == 0:
                own_ref[...] = part
            else:
                send_refs[q + k - 1][...] = part.astype(BF16)


def sum_kernel(own_ref, *refs):
    part_refs, out_ref = refs[:-1], refs[-1]
    total = own_ref[...]
    for ref in part_refs:
        total = total + ref[...].astype(F32)
    out_ref[...] = total.astype(BF16)


def chunk_grads(w_ref, b_ref, h_ref, c_refs, gh_ref):
    tile, width = h_ref.shape[0] // 2, h_ref.shape[1]
    weight_sums, bias_sums = [], []
    for k, (c_ref, half) in enumerate(c_refs):
        rows = slice(k * tile, (k + 1) * tile)
        hidden = h_ref[rows, :]
        preact = dot(hidden, w_ref[...]) + b_ref[...]
        sig = sigmoid(preact)
        cot = c_ref[half * tile : (half + 1) * tile, :].astype(F32)
        grad_z = cot * sig * (1.0 + preact * (1.0 - sig))
        half = grad_z.astype(BF16)
        gh_ref[rows, :] = dot(half, w_ref[...], ((1,), (1,))).astype(BF16)
        bias_sums.append(jnp.sum(grad_z.reshape(tile // 8, 8, width), axis=0))
        weight_sums.append(dot(hidden, half, ((0,), (0,))))
    return tree_sum(weight_sums), tree_sum(bias_sums)


def chunk_kernel(halves, w_ref, b_ref, h_ref, c0_ref, c1_ref, gh_ref, gw_ref, gb_ref):
    c_refs = list(zip((c0_ref, c1_ref), halves))
    gw_ref[...], gb_ref[...] = chunk_grads(w_ref, b_ref, h_ref, c_refs, gh_ref)


def write_message(ref, grad_w, bias):
    rows, width = grad_w.shape
    ref[:rows, :] = grad_w.astype(BF16)
    high = bias.astype(BF16).astype(F32)
    row = lax.broadcasted_iota(jnp.int32, (PAD, width), 0)
    low = jnp.broadcast_to(bias - high, (PAD, width))
    high = jnp.broadcast_to(high, (PAD, width))
    ref[rows:, :] = jnp.where(row == 0, high, jnp.where(row == 1, low, 0.0)).astype(BF16)


def read_message(ref):
    rows = ref.shape[0] - PAD
    tail = ref[rows:, :].astype(F32)
    return ref[:rows, :].astype(F32), tail[0:1, :] + tail[1:2, :]


def last_chunk_kernel(halves, n, w_ref, b_ref, h_ref, c0_ref, c1_ref, *refs):
    gw_refs, gb_refs = refs[:n], refs[n : 2 * n]
    gh_ref, both_ref, keep_ref, sum_ref = refs[2 * n :]
    half = keep_ref.shape[0] - PAD
    c_refs = list(zip((c0_ref, c1_ref), halves))
    grad_w, grad_b = chunk_grads(w_ref, b_ref, h_ref, c_refs, gh_ref)
    sum_ref[...] = tree_sum([ref[...] for ref in gw_refs] + [grad_w])
    grad_b = tree_sum([ref[...] for ref in gb_refs] + [grad_b])
    bias = jnp.sum(grad_b, axis=0, keepdims=True)
    core = lax.axis_index("core")
    kept = sum_ref[pl.ds(pl.multiple_of(core * half, half), half), :]
    sent = sum_ref[pl.ds(pl.multiple_of((1 - core) * half, half), half), :]
    write_message(keep_ref, kept, bias)
    at = gh_ref.shape[0]
    both_ref[:at, :] = gh_ref[...]
    write_message(both_ref.at[at:, :], sent, bias)


def message_kernel(own_ref, other_ref, out_ref):
    own_w, own_b = read_message(own_ref)
    other_w, other_b = read_message(other_ref.at[other_ref.shape[0] - own_ref.shape[0] :, :])
    write_message(out_ref, own_w + other_w, own_b + other_b)


def halves_kernel(own_ref, other_ref, out_ref):
    half = own_ref.shape[0] - PAD
    core = lax.axis_index("core")
    out_ref[pl.ds(pl.multiple_of(core * half, half), half), :] = own_ref[:half, :]
    out_ref[pl.ds(pl.multiple_of((1 - core) * half, half), half), :] = other_ref[:half, :]
    out_ref[2 * half :, :] = own_ref[half:, :]


def last_kernel(factor, near_ref, far_ref, *refs):
    weight_ref, bias_ref, features_ref = refs[-3:]
    sum_kernel(*refs[:-3], features_ref)
    near_w, near_b = read_message(near_ref)
    far_w, far_b = read_message(far_ref)
    weight_ref[...] = (near_w + far_w) * factor
    bias_ref[...] = (near_b + far_b) * factor


def call(kernel, name, outs, operands, scratch=(), specs=None, flops=0):
    size = sum(o.size * o.dtype.itemsize for o in list(operands) + list(outs))
    held = size + sum(
        math.prod(s.shape) * s.dtype.itemsize for s in scratch if hasattr(s.dtype, "itemsize")
    )
    return pl.pallas_call(
        kernel,
        name=name,
        out_shape=outs,
        in_specs=specs or [VMEM] * len(operands),
        out_specs=[VMEM] * len(outs),
        scratch_shapes=scratch,
        cost_estimate=pl.CostEstimate(flops=flops, bytes_accessed=size, transcendentals=0),
        compiler_params=pltpu.CompilerParams(vmem_limit_bytes=2 * held + 4 * MIB),
    )(*operands)


def shards(n_loop, n_row, features, weight, bias_vector, cotangent, tile_values, tile_rows, counts):
    tile, width = features.shape
    n_far = n_loop // 4
    nodes = tile * n_loop * n_row
    rows = n_row * tile
    flops = rows * n_loop * tile * width

    steps = far_masks(n_far)

    def pack(*blocks):
        return call(pack_kernel, "pack", [shape(2 * tile, width)], blocks)[0]

    def far_partner(block, step):
        return partner(block, "far", step, n_far)

    def far_chunks(pair, steps):
        chunks = [pair]
        for step in steps[1:]:
            chunks = chunks + [partner(chunk, "far", step, n_far) for chunk in chunks]
        return chunks

    def near_product(near, name):
        return call(
            functools.partial(near_kernel, tile, n_row),
            name + "_near",
            [shape(rows, width, dtype=F32)],
            [adjacency] + near,
            flops=flops,
        )[0]

    def rest_product(half, rest, name):
        return call(
            functools.partial(rest_kernel, tile, n_row, len(rest)),
            name + "_rest",
            [shape(tile, width, dtype=F32)] + [shape(tile, width)] * (n_row - 1),
            [adjacency, half] + rest,
            flops=flops,
        )

    def from_row(parts):
        return [partner(part, "row", q + 1, n_row) for q, part in enumerate(parts)]

    cot_steps = steps[::-1]
    other, other_cot = far_partner(features, steps[0]), far_partner(cotangent, cot_steps[0])
    adjacency, features, cotangent = call(
        functools.partial(expand_kernel, n_loop, n_row, tile),
        "expand",
        [shape(rows, n_loop * tile), shape(tile, width), shape(tile, width)],
        [
            pltpu.with_memory_space_constraint(x, pltpu.HBM)
            for x in (tile_rows, counts, tile_values, features, cotangent)
        ],
        scratch=[
            pltpu.SMEM(tile_rows.shape, jnp.int32),
            pltpu.SMEM(counts.shape, jnp.int32),
            pltpu.VMEM(tile_values.shape, BF16),
            pltpu.SemaphoreType.DMA((5,)),
        ],
        specs=[pl.BlockSpec(memory_space=pltpu.HBM)] * 5,
    )
    f00 = far_chunks(after(pack(features, other), other_cot), steps)
    f10 = [swap(chunk, "mid") for chunk in f00]
    cots = far_chunks(pack(cotangent, after(other_cot, f00[-1])), cot_steps)
    f01 = [swap(chunk, "core") for chunk in f00]
    f11 = [swap(chunk, "core") for chunk in f10]
    half = near_product(f00 + f01, "forward")
    own, *parts = rest_product(half, f10 + f11, "forward")
    others = from_row(parts)
    (hidden,) = call(sum_kernel, "hidden", [shape(tile, width)], [own] + others)

    bias_row = bias_vector.reshape(1, width)
    (output,) = call(
        output_kernel, "output", [shape(tile, width)], [weight, bias_row, after(hidden, *cots)]
    )
    other, hidden = far_partner(hidden, steps[0]), after(hidden, output)
    hiddens = far_chunks(pack(hidden, other), steps)

    def chunk_cots(k):
        bits = len(steps)
        places = [int(f"{2 * k + b:0{bits}b}"[::-1], 2) for b in range(2)]
        return [cots[p // 2] for p in places], [p % 2 for p in places]

    chunk_flops = 2 * tile * 6 * width * width
    g00, weight_sums, bias_sums = [], [], []
    sums = [shape(width, width, dtype=F32), shape(8, width, dtype=F32)]
    for k, chunk in enumerate(hiddens[:-1]):
        chunk_cot, halves = chunk_cots(k)
        gh, weight_sum, bias_sum = call(
            functools.partial(chunk_kernel, halves),
            "chunk",
            [shape(2 * tile, width)] + sums,
            [weight, bias_row, chunk] + chunk_cot,
            flops=chunk_flops,
        )
        g00.append(gh)
        weight_sums.append(weight_sum)
        bias_sums.append(bias_sum)
    half_rows = width // 2 + PAD
    g01 = [swap(chunk, "core") for chunk in g00]
    g10 = [swap(chunk, "mid") for chunk in g00]
    chunk_cot, halves = chunk_cots(len(g00))
    gh, both, keep = call(
        functools.partial(last_chunk_kernel, halves, len(g00)),
        "last_chunk",
        [shape(2 * tile, width), shape(2 * tile + half_rows, width), shape(half_rows, width)],
        [weight, bias_row, hiddens[-1]] + chunk_cot + weight_sums + bias_sums,
        scratch=[pltpu.VMEM((width, width), F32)],
        flops=chunk_flops,
    )
    g00.append(gh)
    g01.append(swap(after(both, *g10), "core"))
    g10.append(swap(gh, "mid"))

    (message,) = call(message_kernel, "sum_core", [shape(half_rows, width)], [keep, g01[-1]])
    bit = 1
    while bit < n_row:
        (message,) = call(
            message_kernel,
            "sum_row",
            [shape(half_rows, width)],
            [message, partner(message, "row", bit, n_row)],
        )
        bit *= 2
    g11 = [swap(chunk, "core") for chunk in g10]
    half = near_product([after(g00[0], message)] + g00[1:] + g01, "backward")
    own, *parts = rest_product(half, g10 + g11, "backward")
    others = from_row(parts)
    (message,) = call(
        halves_kernel,
        "halves",
        [shape(width + PAD, width)],
        [message, swap(message, "core")],
    )
    message = after(message, own)
    messages = [message, swap(message, "mid")]
    weight_grad, bias_grad, grad_features = call(
        functools.partial(last_kernel, 1.0 / nodes**0.5),
        "last",
        [shape(width, width, dtype=F32), shape(1, width, dtype=F32), shape(tile, width)],
        messages + [own] + others,
    )
    return output, grad_features, weight_grad, bias_grad.reshape(width)


def solution(mesh):
    n_loop, n_row = mesh.shape["loop"], mesh.shape["row"]
    every = ("far", "mid", "core", "row")
    fine = Mesh(mesh.devices.reshape(n_loop // 4, 2, 2, n_row), every)
    in_specs = (
        P(every, None),
        P(),
        P(),
        P(every, None),
        P(every, None, None),
        P(every),
        P(every),
    )
    out_specs = (P(every, None), P(every, None), P(), P())
    return jax.shard_map(
        functools.partial(shards, n_loop, n_row),
        mesh=fine,
        in_specs=in_specs,
        out_specs=out_specs,
        check_vma=False,
    )
```

```python
import functools
import math

import jax
import jax.numpy as jnp
from jax import lax
from jax.experimental import pallas as pl
from jax.experimental.pallas import tpu as pltpu
from jax.sharding import Mesh
from jax.sharding import PartitionSpec as P

BF16 = jnp.bfloat16
F32 = jnp.float32
VMEM = pl.BlockSpec(memory_space=pltpu.VMEM)
SMEM = pl.BlockSpec(memory_space=pltpu.SMEM)
MIB = 1024 * 1024
PAD = 16


def partner(x, axis, mask, n):
    return lax.ppermute(x, axis, [(i, i ^ mask) for i in range(n)])


def swap(x, axis):
    return partner(x, axis, 1, 2)


def after(x, *others):
    return lax.optimization_barrier((x,) + others)[0]


def shape(*dims, dtype=BF16):
    return jax.ShapeDtypeStruct(dims, dtype)


def dot(a, b, contract=((1,), (0,))):
    return lax.dot_general(a, b, (contract, ((), ())), preferred_element_type=F32)


def sigmoid(x):
    return 0.5 * jnp.tanh(0.5 * x) + 0.5


def tree_sum(parts):
    while len(parts) > 1:
        parts = [parts[i] + parts[i + 1] for i in range(0, len(parts), 2)]
    return parts[0]


def far_masks(n_far):
    return [1 << k for k in reversed(range(n_far.bit_length() - 1))]


def far_place(mask, n_far):
    place = 0
    for k, step in enumerate(far_masks(n_far)):
        place = place + jnp.where(jnp.bitwise_and(mask, step) > 0, 1 << k, 0)
    return place


def expand_kernel(
    n_loop, n_row, tile, rows_hbm, counts_hbm, tiles_hbm, f_hbm, c_hbm, out_ref, f_out, c_out,
    rows_ref, counts_ref, tiles_ref, sems,
):
    copies = [
        pltpu.make_async_copy(source, target, sems.at[k])
        for k, (source, target) in enumerate(
            (
                (rows_hbm, rows_ref),
                (counts_hbm, counts_ref),
                (tiles_hbm, tiles_ref),
                (f_hbm, f_out),
                (c_hbm, c_out),
            )
        )
    ]
    for copy in copies:
        copy.start()
    n_far = n_loop // 4
    my_row, my_far = lax.axis_index("row"), lax.axis_index("far")
    my_near = 2 * lax.axis_index("mid") + lax.axis_index("core")
    for copy in copies:
        copy.wait()

    def body(j, carry):
        near = jnp.bitwise_xor(lax.rem(j, 4), my_near)
        column = near * n_far + far_place(jnp.bitwise_xor(lax.div(j, 4), my_far), n_far)
        for s in range(n_row):
            slot = j * n_row + s
            place = jnp.bitwise_xor(rows_ref[slot], my_row)
            value = tiles_ref[slot]
            value = jnp.where(s < counts_ref[j], value, jnp.zeros_like(value))
            out_ref[
                pl.ds(pl.multiple_of(place * tile, tile), tile),
                pl.ds(pl.multiple_of(column * tile, tile), tile),
            ] = value
        return carry

    lax.fori_loop(0, n_loop, body, 0)


def product_rows(a_ref, first, block_refs, rows):
    step = a_ref.shape[1] // (2 * len(block_refs))
    x = jnp.concatenate([ref[:step, :] for ref in block_refs], axis=0)
    return dot(a_ref[rows, first : first + x.shape[0]], x)


def pack_kernel(*refs):
    at = 0
    for ref in refs[:-1]:
        refs[-1][at : at + ref.shape[0], :] = ref[...]
        at += ref.shape[0]


def near_kernel(tile, n_row, a_ref, *refs):
    block_refs, out_ref = refs[:-1], refs[-1]
    step = min(2, n_row) * tile
    for at in range(0, n_row * tile, step):
        rows = slice(at, at + step)
        out_ref[rows, :] = product_rows(a_ref, 0, block_refs, rows)


def output_kernel(w_ref, b_ref, h_ref, out_ref):
    preact = dot(h_ref[...], w_ref[...]) + b_ref[...]
    out_ref[...] = (preact * sigmoid(preact)).astype(BF16)


def rest_kernel(tile, n_row, n_blocks, a_ref, half_ref, *refs):
    block_refs, own_ref, send_refs = refs[:n_blocks], refs[n_blocks], refs[n_blocks + 1 :]
    first = a_ref.shape[1] // 2
    step = min(2, n_row)
    for q in range(0, n_row, step):
        rows = slice(q * tile, (q + step) * tile)
        total = half_ref[rows, :] + product_rows(a_ref, first, block_refs, rows)
        for k in range(step):
            part = total[k * tile : (k + 1) * tile, :]
            if q + k == 0:
                own_ref[...] = part
            else:
                send_refs[q + k - 1][...] = part.astype(BF16)


def sum_kernel(own_ref, *refs):
    part_refs, out_ref = refs[:-1], refs[-1]
    total = own_ref[...]
    for ref in part_refs:
        total = total + ref[...].astype(F32)
    out_ref[...] = total.astype(BF16)


def chunk_grads(w_ref, b_ref, h_ref, c_refs, gh_ref):
    tile, width = h_ref.shape[0] // 2, h_ref.shape[1]
    weight_sums, bias_sums = [], []
    for k, (c_ref, half) in enumerate(c_refs):
        rows = slice(k * tile, (k + 1) * tile)
        hidden = h_ref[rows, :]
        preact = dot(hidden, w_ref[...]) + b_ref[...]
        sig = sigmoid(preact)
        cot = c_ref[half * tile : (half + 1) * tile, :].astype(F32)
        grad_z = cot * sig * (1.0 + preact * (1.0 - sig))
        half = grad_z.astype(BF16)
        gh_ref[rows, :] = dot(half, w_ref[...], ((1,), (1,))).astype(BF16)
        bias_sums.append(jnp.sum(grad_z.reshape(tile // 8, 8, width), axis=0))
        weight_sums.append(dot(hidden, half, ((0,), (0,))))
    return tree_sum(weight_sums), tree_sum(bias_sums)


def chunk_kernel(halves, w_ref, b_ref, h_ref, c0_ref, c1_ref, gh_ref, gw_ref, gb_ref):
    c_refs = list(zip((c0_ref, c1_ref), halves))
    gw_ref[...], gb_ref[...] = chunk_grads(w_ref, b_ref, h_ref, c_refs, gh_ref)


def write_message(ref, grad_w, bias):
    rows, width = grad_w.shape
    ref[:rows, :] = grad_w.astype(BF16)
    high = bias.astype(BF16).astype(F32)
    row = lax.broadcasted_iota(jnp.int32, (PAD, width), 0)
    low = jnp.broadcast_to(bias - high, (PAD, width))
    high = jnp.broadcast_to(high, (PAD, width))
    ref[rows:, :] = jnp.where(row == 0, high, jnp.where(row == 1, low, 0.0)).astype(BF16)


def read_message(ref):
    rows = ref.shape[0] - PAD
    tail = ref[rows:, :].astype(F32)
    return ref[:rows, :].astype(F32), tail[0:1, :] + tail[1:2, :]


def last_chunk_kernel(halves, n, w_ref, b_ref, h_ref, c0_ref, c1_ref, *refs):
    gw_refs, gb_refs = refs[:n], refs[n : 2 * n]
    gh_ref, both_ref, keep_ref, sum_ref = refs[2 * n :]
    half = keep_ref.shape[0] - PAD
    c_refs = list(zip((c0_ref, c1_ref), halves))
    grad_w, grad_b = chunk_grads(w_ref, b_ref, h_ref, c_refs, gh_ref)
    sum_ref[...] = tree_sum([ref[...] for ref in gw_refs] + [grad_w])
    grad_b = tree_sum([ref[...] for ref in gb_refs] + [grad_b])
    bias = jnp.sum(grad_b, axis=0, keepdims=True)
    core = lax.axis_index("core")
    kept = sum_ref[pl.ds(pl.multiple_of(core * half, half), half), :]
    sent = sum_ref[pl.ds(pl.multiple_of((1 - core) * half, half), half), :]
    write_message(keep_ref, kept, bias)
    at = gh_ref.shape[0]
    both_ref[:at, :] = gh_ref[...]
    write_message(both_ref.at[at:, :], sent, bias)


def message_kernel(own_ref, other_ref, out_ref):
    own_w, own_b = read_message(own_ref)
    other_w, other_b = read_message(other_ref.at[other_ref.shape[0] - own_ref.shape[0] :, :])
    write_message(out_ref, own_w + other_w, own_b + other_b)


def halves_kernel(own_ref, other_ref, out_ref):
    half = own_ref.shape[0] - PAD
    core = lax.axis_index("core")
    out_ref[pl.ds(pl.multiple_of(core * half, half), half), :] = own_ref[:half, :]
    out_ref[pl.ds(pl.multiple_of((1 - core) * half, half), half), :] = other_ref[:half, :]
    out_ref[2 * half :, :] = own_ref[half:, :]


def last_kernel(factor, near_ref, far_ref, *refs):
    weight_ref, bias_ref, features_ref = refs[-3:]
    sum_kernel(*refs[:-3], features_ref)
    near_w, near_b = read_message(near_ref)
    far_w, far_b = read_message(far_ref)
    weight_ref[...] = (near_w + far_w) * factor
    bias_ref[...] = (near_b + far_b) * factor


def call(kernel, name, outs, operands, scratch=(), specs=None, flops=0):
    size = sum(o.size * o.dtype.itemsize for o in list(operands) + list(outs))
    held = size + sum(
        math.prod(s.shape) * s.dtype.itemsize for s in scratch if hasattr(s.dtype, "itemsize")
    )
    return pl.pallas_call(
        kernel,
        name=name,
        out_shape=outs,
        in_specs=specs or [VMEM] * len(operands),
        out_specs=[VMEM] * len(outs),
        scratch_shapes=scratch,
        cost_estimate=pl.CostEstimate(flops=flops, bytes_accessed=size, transcendentals=0),
        compiler_params=pltpu.CompilerParams(vmem_limit_bytes=2 * held + 4 * MIB),
    )(*operands)


def shards(n_loop, n_row, features, weight, bias_vector, cotangent, tile_values, tile_rows, counts):
    tile, width = features.shape
    n_far = n_loop // 4
    nodes = tile * n_loop * n_row
    rows = n_row * tile
    flops = rows * n_loop * tile * width

    steps = far_masks(n_far)

    def pack(*blocks):
        return call(pack_kernel, "pack", [shape(2 * tile, width)], blocks)[0]

    def far_partner(block, step):
        return partner(block, "far", step, n_far)

    def far_chunks(pair, steps):
        chunks = [pair]
        for step in steps[1:]:
            chunks = chunks + [partner(chunk, "far", step, n_far) for chunk in chunks]
        return chunks

    def near_product(near, name):
        return call(
            functools.partial(near_kernel, tile, n_row),
            name + "_near",
            [shape(rows, width, dtype=F32)],
            [adjacency] + near,
            flops=flops,
        )[0]

    def rest_product(half, rest, name):
        return call(
            functools.partial(rest_kernel, tile, n_row, len(rest)),
            name + "_rest",
            [shape(tile, width, dtype=F32)] + [shape(tile, width)] * (n_row - 1),
            [adjacency, half] + rest,
            flops=flops,
        )

    def from_row(parts):
        return [partner(part, "row", q + 1, n_row) for q, part in enumerate(parts)]

    cot_steps = steps[::-1]
    other, other_cot = far_partner(features, steps[0]), far_partner(cotangent, cot_steps[0])
    adjacency, features, cotangent = call(
        functools.partial(expand_kernel, n_loop, n_row, tile),
        "expand",
        [shape(rows, n_loop * tile), shape(tile, width), shape(tile, width)],
        [
            pltpu.with_memory_space_constraint(x, pltpu.HBM)
            for x in (tile_rows, counts, tile_values, features, cotangent)
        ],
        scratch=[
            pltpu.SMEM(tile_rows.shape, jnp.int32),
            pltpu.SMEM(counts.shape, jnp.int32),
            pltpu.VMEM(tile_values.shape, BF16),
            pltpu.SemaphoreType.DMA((5,)),
        ],
        specs=[pl.BlockSpec(memory_space=pltpu.HBM)] * 5,
    )
    f00 = far_chunks(pack(features, other), steps)
    f10 = [swap(chunk, "mid") for chunk in f00]
    cots = far_chunks(pack(cotangent, after(other_cot, f00[-1])), cot_steps)
    f01 = [swap(chunk, "core") for chunk in [after(f00[0], other_cot)] + f00[1:]]
    f11 = [swap(chunk, "core") for chunk in f10]
    half = near_product(f00 + f01, "forward")
    own, *parts = rest_product(half, f10 + f11, "forward")
    others = from_row(parts)
    (hidden,) = call(sum_kernel, "hidden", [shape(tile, width)], [own] + others)

    bias_row = bias_vector.reshape(1, width)
    (output,) = call(
        output_kernel, "output", [shape(tile, width)], [weight, bias_row, after(hidden, *cots)]
    )
    other, hidden = far_partner(hidden, steps[0]), after(hidden, output)
    hiddens = far_chunks(pack(hidden, other), steps)

    def chunk_cots(k):
        bits = len(steps)
        places = [int(f"{2 * k + b:0{bits}b}"[::-1], 2) for b in range(2)]
        return [cots[p // 2] for p in places], [p % 2 for p in places]

    chunk_flops = 2 * tile * 6 * width * width
    g00, weight_sums, bias_sums = [], [], []
    sums = [shape(width, width, dtype=F32), shape(8, width, dtype=F32)]
    for k, chunk in enumerate(hiddens[:-1]):
        chunk_cot, halves = chunk_cots(k)
        gh, weight_sum, bias_sum = call(
            functools.partial(chunk_kernel, halves),
            "chunk",
            [shape(2 * tile, width)] + sums,
            [weight, bias_row, chunk] + chunk_cot,
            flops=chunk_flops,
        )
        g00.append(gh)
        weight_sums.append(weight_sum)
        bias_sums.append(bias_sum)
    half_rows = width // 2 + PAD
    g01 = [swap(chunk, "core") for chunk in g00]
    g10 = [swap(chunk, "mid") for chunk in g00]
    chunk_cot, halves = chunk_cots(len(g00))
    gh, both, keep = call(
        functools.partial(last_chunk_kernel, halves, len(g00)),
        "last_chunk",
        [shape(2 * tile, width), shape(2 * tile + half_rows, width), shape(half_rows, width)],
        [weight, bias_row, hiddens[-1]] + chunk_cot + weight_sums + bias_sums,
        scratch=[pltpu.VMEM((width, width), F32)],
        flops=chunk_flops,
    )
    g00.append(gh)
    g01.append(swap(after(both, *g10), "core"))
    g10.append(swap(gh, "mid"))

    (message,) = call(message_kernel, "sum_core", [shape(half_rows, width)], [keep, g01[-1]])
    bit = 1
    while bit < n_row:
        (message,) = call(
            message_kernel,
            "sum_row",
            [shape(half_rows, width)],
            [message, partner(message, "row", bit, n_row)],
        )
        bit *= 2
    g11 = [swap(chunk, "core") for chunk in g10]
    half = near_product([after(g00[0], message)] + g00[1:] + g01, "backward")
    own, *parts = rest_product(half, g10 + g11, "backward")
    others = from_row(parts)
    (message,) = call(
        halves_kernel,
        "halves",
        [shape(width + PAD, width)],
        [message, swap(message, "core")],
    )
    message = after(message, own)
    messages = [message, swap(message, "mid")]
    weight_grad, bias_grad, grad_features = call(
        functools.partial(last_kernel, 1.0 / nodes**0.5),
        "last",
        [shape(width, width, dtype=F32), shape(1, width, dtype=F32), shape(tile, width)],
        messages + [own] + others,
    )
    return output, grad_features, weight_grad, bias_grad.reshape(width)


def solution(mesh):
    n_loop, n_row = mesh.shape["loop"], mesh.shape["row"]
    every = ("far", "mid", "core", "row")
    fine = Mesh(mesh.devices.reshape(n_loop // 4, 2, 2, n_row), every)
    in_specs = (
        P(every, None),
        P(),
        P(),
        P(every, None),
        P(every, None, None),
        P(every),
        P(every),
    )
    out_specs = (P(every, None), P(every, None), P(), P())
    return jax.shard_map(
        functools.partial(shards, n_loop, n_row),
        mesh=fine,
        in_specs=in_specs,
        out_specs=out_specs,
        check_vma=False,
    )
```

```python
import functools
import math

import jax
import jax.numpy as jnp
from jax import lax
from jax.experimental import pallas as pl
from jax.experimental.pallas import tpu as pltpu
from jax.sharding import Mesh
from jax.sharding import PartitionSpec as P

BF16 = jnp.bfloat16
F32 = jnp.float32
VMEM = pl.BlockSpec(memory_space=pltpu.VMEM)
SMEM = pl.BlockSpec(memory_space=pltpu.SMEM)
MIB = 1024 * 1024
PAD = 16


def partner(x, axis, mask, n):
    return lax.ppermute(x, axis, [(i, i ^ mask) for i in range(n)])


def swap(x, axis):
    return partner(x, axis, 1, 2)


def after(x, *others):
    return lax.optimization_barrier((x,) + others)[0]


def shape(*dims, dtype=BF16):
    return jax.ShapeDtypeStruct(dims, dtype)


def dot(a, b, contract=((1,), (0,))):
    return lax.dot_general(a, b, (contract, ((), ())), preferred_element_type=F32)


def sigmoid(x):
    return 0.5 * jnp.tanh(0.5 * x) + 0.5


def tree_sum(parts):
    while len(parts) > 1:
        parts = [parts[i] + parts[i + 1] for i in range(0, len(parts), 2)]
    return parts[0]


def far_masks(n_far):
    return [1 << k for k in reversed(range(n_far.bit_length() - 1))]


def far_place(mask, n_far):
    place = 0
    for k, step in enumerate(far_masks(n_far)):
        place = place + jnp.where(jnp.bitwise_and(mask, step) > 0, 1 << k, 0)
    return place


def expand_kernel(
    n_loop, n_row, tile, rows_hbm, counts_hbm, tiles_hbm, f_hbm, c_hbm, out_ref, f_out, c_out,
    rows_ref, counts_ref, tiles_ref, sems,
):
    copies = [
        pltpu.make_async_copy(source, target, sems.at[k])
        for k, (source, target) in enumerate(
            (
                (rows_hbm, rows_ref),
                (counts_hbm, counts_ref),
                (tiles_hbm, tiles_ref),
                (f_hbm, f_out),
                (c_hbm, c_out),
            )
        )
    ]
    for copy in copies:
        copy.start()
    n_far = n_loop // 4
    my_row, my_far = lax.axis_index("row"), lax.axis_index("far")
    my_near = 2 * lax.axis_index("mid") + lax.axis_index("core")
    for copy in copies:
        copy.wait()

    def body(j, carry):
        near = jnp.bitwise_xor(lax.rem(j, 4), my_near)
        column = near * n_far + far_place(jnp.bitwise_xor(lax.div(j, 4), my_far), n_far)
        for s in range(n_row):
            slot = j * n_row + s
            place = jnp.bitwise_xor(rows_ref[slot], my_row)
            value = tiles_ref[slot]
            value = jnp.where(s < counts_ref[j], value, jnp.zeros_like(value))
            out_ref[
                pl.ds(pl.multiple_of(place * tile, tile), tile),
                pl.ds(pl.multiple_of(column * tile, tile), tile),
            ] = value
        return carry

    lax.fori_loop(0, n_loop, body, 0)


def product_rows(a_ref, first, block_refs, rows):
    step = a_ref.shape[1] // (2 * len(block_refs))
    x = jnp.concatenate([ref[:step, :] for ref in block_refs], axis=0)
    return dot(a_ref[rows, first : first + x.shape[0]], x)


def pack_kernel(*refs):
    at = 0
    for ref in refs[:-1]:
        refs[-1][at : at + ref.shape[0], :] = ref[...]
        at += ref.shape[0]


def near_kernel(tile, n_row, a_ref, *refs):
    block_refs, out_ref = refs[:-1], refs[-1]
    step = min(2, n_row) * tile
    for at in range(0, n_row * tile, step):
        rows = slice(at, at + step)
        out_ref[rows, :] = product_rows(a_ref, 0, block_refs, rows)


def output_kernel(w_ref, b_ref, h_ref, out_ref):
    preact = dot(h_ref[...], w_ref[...]) + b_ref[...]
    out_ref[...] = (preact * sigmoid(preact)).astype(BF16)


def rest_kernel(tile, n_row, n_blocks, a_ref, half_ref, *refs):
    block_refs, own_ref, send_refs = refs[:n_blocks], refs[n_blocks], refs[n_blocks + 1 :]
    first = a_ref.shape[1] // 2
    step = min(2, n_row)
    for q in range(0, n_row, step):
        rows = slice(q * tile, (q + step) * tile)
        total = half_ref[rows, :] + product_rows(a_ref, first, block_refs, rows)
        for k in range(step):
            part = total[k * tile : (k + 1) * tile, :]
            if q + k == 0:
                own_ref[...] = part
            else:
                send_refs[q + k - 1][...] = part.astype(BF16)


def sum_kernel(own_ref, *refs):
    part_refs, out_ref = refs[:-1], refs[-1]
    total = own_ref[...]
    for ref in part_refs:
        total = total + ref[...].astype(F32)
    out_ref[...] = total.astype(BF16)


def chunk_grads(w_ref, b_ref, h_ref, c_refs, gh_ref):
    tile, width = h_ref.shape[0] // 2, h_ref.shape[1]
    weight_sums, bias_sums = [], []
    for k, (c_ref, half) in enumerate(c_refs):
        rows = slice(k * tile, (k + 1) * tile)
        hidden = h_ref[rows, :]
        preact = dot(hidden, w_ref[...]) + b_ref[...]
        sig = sigmoid(preact)
        cot = c_ref[half * tile : (half + 1) * tile, :].astype(F32)
        grad_z = cot * sig * (1.0 + preact * (1.0 - sig))
        half = grad_z.astype(BF16)
        gh_ref[rows, :] = dot(half, w_ref[...], ((1,), (1,))).astype(BF16)
        bias_sums.append(jnp.sum(grad_z.reshape(tile // 8, 8, width), axis=0))
        weight_sums.append(dot(hidden, half, ((0,), (0,))))
    return tree_sum(weight_sums), tree_sum(bias_sums)


def chunk_kernel(halves, w_ref, b_ref, h_ref, c0_ref, c1_ref, gh_ref, gw_ref, gb_ref):
    c_refs = list(zip((c0_ref, c1_ref), halves))
    gw_ref[...], gb_ref[...] = chunk_grads(w_ref, b_ref, h_ref, c_refs, gh_ref)


def write_message(ref, grad_w, bias):
    rows, width = grad_w.shape
    ref[:rows, :] = grad_w.astype(BF16)
    high = bias.astype(BF16).astype(F32)
    row = lax.broadcasted_iota(jnp.int32, (PAD, width), 0)
    low = jnp.broadcast_to(bias - high, (PAD, width))
    high = jnp.broadcast_to(high, (PAD, width))
    ref[rows:, :] = jnp.where(row == 0, high, jnp.where(row == 1, low, 0.0)).astype(BF16)


def read_message(ref):
    rows = ref.shape[0] - PAD
    tail = ref[rows:, :].astype(F32)
    return ref[:rows, :].astype(F32), tail[0:1, :] + tail[1:2, :]


def last_chunk_kernel(halves, n, w_ref, b_ref, h_ref, c0_ref, c1_ref, *refs):
    gw_refs, gb_refs = refs[:n], refs[n : 2 * n]
    gh_ref, both_ref, keep_ref, sum_ref = refs[2 * n :]
    half = keep_ref.shape[0] - PAD
    c_refs = list(zip((c0_ref, c1_ref), halves))
    grad_w, grad_b = chunk_grads(w_ref, b_ref, h_ref, c_refs, gh_ref)
    sum_ref[...] = tree_sum([ref[...] for ref in gw_refs] + [grad_w])
    grad_b = tree_sum([ref[...] for ref in gb_refs] + [grad_b])
    bias = jnp.sum(grad_b, axis=0, keepdims=True)
    core = lax.axis_index("core")
    kept = sum_ref[pl.ds(pl.multiple_of(core * half, half), half), :]
    sent = sum_ref[pl.ds(pl.multiple_of((1 - core) * half, half), half), :]
    write_message(keep_ref, kept, bias)
    at = gh_ref.shape[0]
    both_ref[:at, :] = gh_ref[...]
    write_message(both_ref.at[at:, :], sent, bias)


def message_kernel(own_ref, other_ref, out_ref):
    own_w, own_b = read_message(own_ref)
    other_w, other_b = read_message(other_ref.at[other_ref.shape[0] - own_ref.shape[0] :, :])
    write_message(out_ref, own_w + other_w, own_b + other_b)


def halves_kernel(own_ref, other_ref, out_ref):
    half = own_ref.shape[0] - PAD
    core = lax.axis_index("core")
    out_ref[pl.ds(pl.multiple_of(core * half, half), half), :] = own_ref[:half, :]
    out_ref[pl.ds(pl.multiple_of((1 - core) * half, half), half), :] = other_ref[:half, :]
    out_ref[2 * half :, :] = own_ref[half:, :]


def last_kernel(factor, near_ref, far_ref, *refs):
    weight_ref, bias_ref, features_ref = refs[-3:]
    sum_kernel(*refs[:-3], features_ref)
    near_w, near_b = read_message(near_ref)
    far_w, far_b = read_message(far_ref)
    weight_ref[...] = (near_w + far_w) * factor
    bias_ref[...] = (near_b + far_b) * factor


def call(kernel, name, outs, operands, scratch=(), specs=None, flops=0):
    size = sum(o.size * o.dtype.itemsize for o in list(operands) + list(outs))
    held = size + sum(
        math.prod(s.shape) * s.dtype.itemsize for s in scratch if hasattr(s.dtype, "itemsize")
    )
    return pl.pallas_call(
        kernel,
        name=name,
        out_shape=outs,
        in_specs=specs or [VMEM] * len(operands),
        out_specs=[VMEM] * len(outs),
        scratch_shapes=scratch,
        cost_estimate=pl.CostEstimate(flops=flops, bytes_accessed=size, transcendentals=0),
        compiler_params=pltpu.CompilerParams(vmem_limit_bytes=2 * held + 4 * MIB),
    )(*operands)


def shards(n_loop, n_row, features, weight, bias_vector, cotangent, tile_values, tile_rows, counts):
    tile, width = features.shape
    n_far = n_loop // 4
    nodes = tile * n_loop * n_row
    rows = n_row * tile
    flops = rows * n_loop * tile * width

    steps = far_masks(n_far)

    def pack(*blocks):
        return call(pack_kernel, "pack", [shape(2 * tile, width)], blocks)[0]

    def far_partner(block, step):
        return partner(block, "far", step, n_far)

    def far_chunks(pair, steps):
        chunks = [pair]
        for step in steps[1:]:
            chunks = chunks + [partner(chunk, "far", step, n_far) for chunk in chunks]
        return chunks

    def near_product(near, name):
        return call(
            functools.partial(near_kernel, tile, n_row),
            name + "_near",
            [shape(rows, width, dtype=F32)],
            [adjacency] + near,
            flops=flops,
        )[0]

    def rest_product(half, rest, name):
        return call(
            functools.partial(rest_kernel, tile, n_row, len(rest)),
            name + "_rest",
            [shape(tile, width, dtype=F32)] + [shape(tile, width)] * (n_row - 1),
            [adjacency, half] + rest,
            flops=flops,
        )

    def from_row(parts):
        return [partner(part, "row", q + 1, n_row) for q, part in enumerate(parts)]

    cot_steps = steps[::-1]
    other, other_cot = far_partner(features, steps[0]), far_partner(cotangent, cot_steps[0])
    adjacency, features, cotangent = call(
        functools.partial(expand_kernel, n_loop, n_row, tile),
        "expand",
        [shape(rows, n_loop * tile), shape(tile, width), shape(tile, width)],
        [
            pltpu.with_memory_space_constraint(x, pltpu.HBM)
            for x in (tile_rows, counts, tile_values, features, cotangent)
        ],
        scratch=[
            pltpu.SMEM(tile_rows.shape, jnp.int32),
            pltpu.SMEM(counts.shape, jnp.int32),
            pltpu.VMEM(tile_values.shape, BF16),
            pltpu.SemaphoreType.DMA((5,)),
        ],
        specs=[pl.BlockSpec(memory_space=pltpu.HBM)] * 5,
    )
    f00 = far_chunks(after(pack(features, other), other_cot), steps)
    f10 = [swap(chunk, "mid") for chunk in f00]
    cots = far_chunks(pack(cotangent, other_cot), cot_steps)
    f01 = [swap(chunk, "core") for chunk in f00]
    f11 = [swap(chunk, "core") for chunk in f10[:-1] + [after(f10[-1], *cots)]]
    half = near_product(f00 + f01, "forward")
    own, *parts = rest_product(half, f10 + f11, "forward")
    others = from_row(parts)
    (hidden,) = call(sum_kernel, "hidden", [shape(tile, width)], [own] + others)

    bias_row = bias_vector.reshape(1, width)
    (output,) = call(
        output_kernel, "output", [shape(tile, width)], [weight, bias_row, hidden]
    )
    other, hidden = far_partner(hidden, steps[0]), after(hidden, output)
    hiddens = far_chunks(pack(hidden, other), steps)

    def chunk_cots(k):
        bits = len(steps)
        places = [int(f"{2 * k + b:0{bits}b}"[::-1], 2) for b in range(2)]
        return [cots[p // 2] for p in places], [p % 2 for p in places]

    chunk_flops = 2 * tile * 6 * width * width
    g00, weight_sums, bias_sums = [], [], []
    sums = [shape(width, width, dtype=F32), shape(8, width, dtype=F32)]
    for k, chunk in enumerate(hiddens[:-1]):
        chunk_cot, halves = chunk_cots(k)
        gh, weight_sum, bias_sum = call(
            functools.partial(chunk_kernel, halves),
            "chunk",
            [shape(2 * tile, width)] + sums,
            [weight, bias_row, chunk] + chunk_cot,
            flops=chunk_flops,
        )
        g00.append(gh)
        weight_sums.append(weight_sum)
        bias_sums.append(bias_sum)
    half_rows = width // 2 + PAD
    g01 = [swap(chunk, "core") for chunk in g00]
    g10 = [swap(chunk, "mid") for chunk in g00]
    chunk_cot, halves = chunk_cots(len(g00))
    gh, both, keep = call(
        functools.partial(last_chunk_kernel, halves, len(g00)),
        "last_chunk",
        [shape(2 * tile, width), shape(2 * tile + half_rows, width), shape(half_rows, width)],
        [weight, bias_row, hiddens[-1]] + chunk_cot + weight_sums + bias_sums,
        scratch=[pltpu.VMEM((width, width), F32)],
        flops=chunk_flops,
    )
    g00.append(gh)
    g01.append(swap(after(both, *g10), "core"))
    g10.append(swap(gh, "mid"))

    (message,) = call(message_kernel, "sum_core", [shape(half_rows, width)], [keep, g01[-1]])
    bit = 1
    while bit < n_row:
        (message,) = call(
            message_kernel,
            "sum_row",
            [shape(half_rows, width)],
            [message, partner(message, "row", bit, n_row)],
        )
        bit *= 2
    g11 = [swap(chunk, "core") for chunk in g10]
    half = near_product([after(g00[0], message)] + g00[1:] + g01, "backward")
    own, *parts = rest_product(half, g10 + g11, "backward")
    others = from_row(parts)
    (message,) = call(
        halves_kernel,
        "halves",
        [shape(width + PAD, width)],
        [message, swap(message, "core")],
    )
    message = after(message, half)
    messages = [message, swap(message, "mid")]
    weight_grad, bias_grad, grad_features = call(
        functools.partial(last_kernel, 1.0 / nodes**0.5),
        "last",
        [shape(width, width, dtype=F32), shape(1, width, dtype=F32), shape(tile, width)],
        messages + [own] + others,
    )
    return output, grad_features, weight_grad, bias_grad.reshape(width)


def solution(mesh):
    n_loop, n_row = mesh.shape["loop"], mesh.shape["row"]
    every = ("far", "mid", "core", "row")
    fine = Mesh(mesh.devices.reshape(n_loop // 4, 2, 2, n_row), every)
    in_specs = (
        P(every, None),
        P(),
        P(),
        P(every, None),
        P(every, None, None),
        P(every),
        P(every),
    )
    out_specs = (P(every, None), P(every, None), P(), P())
    return jax.shard_map(
        functools.partial(shards, n_loop, n_row),
        mesh=fine,
        in_specs=in_specs,
        out_specs=out_specs,
        check_vma=False,
    )
```
